32 devices in a mesh: seq: 8 (over z, x), shard: 4 (over y, core).
Axes of the slice: x: 2, y: 2, z: 4, core: 2. Of those that a mesh axis runs over, the one named last changes fastest.
Arguments:
- tokens: bfloat16 [2, 4096, 2048], P(None, 'seq'), may hold values from -6 to 6
- pre_gain: float32 [2048], P('seq'), may hold values from 0.1 to 1.9
- query_weight: bfloat16 [2048, 2048], P('seq', 'shard'), may hold values from -0.125 to 0.125
- key_weight: bfloat16 [2048, 2048], P('seq', 'shard'), may hold values from -0.0078125 to 0.0078125
- value_weight: bfloat16 [2048, 4096], P('seq', 'shard'), may hold values from -0.125 to 0.125
- swish_weight: bfloat16 [2048, 4096], P('seq', 'shard'), may hold values from -0.125 to 0.125
- output_weight: bfloat16 [4096, 2048], P('shard', 'seq'), may hold values from -0.125 to 0.125
- mid_gain: float32 [2048], P('seq'), may hold values from 0.1 to 1.9
- gate_weight: bfloat16 [2048, 4096], P('seq', 'shard'), may hold values from -0.125 to 0.125
- up_weight: bfloat16 [2048, 4096], P('seq', 'shard'), may hold values from -0.125 to 0.125
- down_weight: bfloat16 [4096, 2048], P('shard', 'seq'), may hold values from -0.125 to 0.125
- cotangent: bfloat16 [2, 4096, 2048], P(None, 'seq'), may hold values from -6 to 6
Outputs:
- layer_out: bfloat16 [2, 4096, 2048], P(None, 'seq')
- tokens_grad: float32 [2, 4096, 2048], P(None, 'seq')
- pre_grad: float32 [2048], P('seq')
- query_grad: float32 [2048, 2048], P('seq', 'shard')
- key_grad: float32 [2048, 2048], P('seq', 'shard')
- value_grad: float32 [2048, 4096], P('seq', 'shard')
- swish_grad: float32 [2048, 4096], P('seq', 'shard')
- output_grad: float32 [4096, 2048], P('shard', 'seq')
- mid_grad: float32 [2048], P('seq')
- gate_grad: float32 [2048, 4096], P('seq', 'shard')
- up_grad: float32 [2048, 4096], P('seq', 'shard')
- down_grad: float32 [4096, 2048], P('shard', 'seq')
The draws below stay inside these ranges and needn't reach their ends.
All inputs are finite; a program needn't handle non-finite values.
Results may differ from the reference program's by a relative error of at most 0.02.
The reference program's roundings to bfloat16 on the way count: a program that leaves them out, or rounds other values in their place, can miss the bound.
Values may be sent and summed in bfloat16 or wider, within the bound.
No kernel may reach another device: no remote copies, remote signals or barrier semaphores. Data moves between devices by JAX's collectives and lax.ppermute only.
A program may use at most 256 MiB of HBM per device.

```python
import jax
import jax.numpy as jnp
from jax import lax

D = 2048
HEADS = 8
QK = 256
VD = 512
FF = 4096
SEG = 512
SEQS = 2
LENGTH = 4096


def levels(rng, shape, cuts, smallest, largest):
    def one(axis_at, shards_of):
        steps = jax.random.uniform(jax.random.fold_in(jax.random.fold_in(rng, 6), axis_at), (shards_of,), jnp.float32, smallest / len(cuts), largest / len(cuts))
        return jnp.repeat(jnp.exp(steps), shape[axis_at] // shards_of).reshape((-1,) + (1,) * (len(shape) - axis_at - 1))

    loudness = one(*cuts[0])
    for cut in cuts[1:]:
        loudness = loudness * one(*cut)
    return loudness


def noise(stream_key, shape, scale, reach, shards=(), kind=jnp.bfloat16):
    level = levels(stream_key, shape, shards, -0.22, 0.18) if shards else 1.0
    drawn = jax.random.normal(stream_key, shape, jnp.float32) * scale * level
    return jnp.minimum(jnp.maximum(drawn, -reach), reach).astype(kind)


def setup_inputs(seed: int = 0) -> dict:
    streams_of = jax.random.split(jax.random.key(seed), 13)
    tokens = noise(streams_of[0], (SEQS, LENGTH, D), 1.0, 6.0, ((1, 8),))
    pre_gain = jnp.clip(1.0 + 0.18 * jax.random.normal(streams_of[1], (D,), jnp.float32), 0.1, 1.9)
    query_weight = noise(streams_of[2], (D, HEADS * QK), D ** -0.5, 0.125, ((0, 8), (1, 4)))
    key_weight = noise(streams_of[3], (D, HEADS * QK), (D * QK) ** -0.5, 0.0078125, ((0, 8), (1, 4)))
    value_weight = noise(streams_of[4], (D, HEADS * VD), D ** -0.5, 0.125, ((0, 8), (1, 4)))
    swish_weight = noise(streams_of[5], (D, HEADS * VD), D ** -0.5, 0.125, ((0, 8), (1, 4)))
    output_weight = noise(streams_of[6], (HEADS * VD, D), (HEADS * VD // 2) ** -0.5, 0.125, ((0, 4), (1, 8)))
    mid_gain = jnp.clip(1.0 + 0.18 * jax.random.normal(streams_of[7], (D,), jnp.float32), 0.1, 1.9)
    gate_weight = noise(streams_of[8], (D, FF), D ** -0.5, 0.125, ((0, 8), (1, 4)))
    up_weight = noise(streams_of[9], (D, FF), D ** -0.5, 0.125, ((0, 8), (1, 4)))
    down_weight = noise(streams_of[10], (FF, D), (FF // 2) ** -0.5, 0.125, ((0, 4), (1, 8)))
    cotangent = noise(streams_of[11], (SEQS, LENGTH, D), 1.0, 6.0, ((1, 8),))
    return dict(tokens=tokens, pre_gain=pre_gain, query_weight=query_weight, key_weight=key_weight, value_weight=value_weight, swish_weight=swish_weight, output_weight=output_weight, mid_gain=mid_gain, gate_weight=gate_weight, up_weight=up_weight, down_weight=down_weight, cotangent=cotangent)


@jax.custom_vjp
def low(v):
    return lax.optimization_barrier(v.astype(jnp.bfloat16)).astype(jnp.float32)

@jax.custom_vjp
def low_back(v):
    return v

def low_keep(v):
    return (low(v), None)

def low_pass(kept, grad):
    return (grad,)

def back_keep(v):
    return (v, None)

def back_low(kept, grad):
    return (low(grad),)
low.defvjp(low_keep, low_pass)
low_back.defvjp(back_keep, back_low)
precise_mode = lax.Precision.HIGHEST

def normed(values, gain):
    centred = values - lax.optimization_barrier(jnp.mean(values, axis=-1, keepdims=True))
    spread = lax.optimization_barrier(jnp.mean(centred * centred, axis=-1, keepdims=True))
    return centred * lax.rsqrt(spread + 1e-05) * gain

def group_normed(values):
    centred = values - lax.optimization_barrier(jnp.mean(values, axis=-1, keepdims=True))
    spread = lax.optimization_barrier(jnp.mean(centred * centred, axis=-1, keepdims=True))
    return centred * lax.rsqrt(spread + 1e-05)

def swish_gate(swish_pre, mixed):
    return jax.nn.silu(swish_pre) * group_normed(mixed)

def gelu_product(gate_pre, up_pre):
    return jax.nn.gelu(gate_pre) * up_pre

def decay_logs(head_index):
    return jnp.log1p(-jnp.exp2(-5.0 - head_index))

def decay_tables(logs, block_rows):
    positions = jnp.arange(block_rows, dtype=jnp.float32)
    offsets = positions[:, None] - positions[None, :]
    within = jnp.where(offsets[None] >= 0.0, jnp.exp(jnp.maximum(offsets, 0.0)[None] * logs[:, None, None]), 0.0)
    query_decay_scale = jnp.exp((positions[None] + 1.0) * logs[:, None])
    value_decay_scale = jnp.exp((block_rows - 1.0 - positions[None]) * logs[:, None])
    carry_scale = jnp.exp(block_rows * logs)
    return (within, query_decay_scale, value_decay_scale, carry_scale)

def forward(tokens_row, pre_gain, query_weight, key_weight, value_weight, swish_weight, output_weight, mid_gain, gate_weight, up_weight, down_weight):
    length_rows = tokens_row.shape[0]
    block_count = length_rows // SEG
    mixer_in = low(normed(tokens_row, low(pre_gain)))

    def project(weight, col_width):
        result = low_back(low(jnp.dot(mixer_in, weight, precision=precise_mode)))
        return result.reshape(block_count, SEG, HEADS, col_width).transpose(0, 2, 1, 3)
    queries = project(query_weight, QK)
    keys_all = project(key_weight, QK)
    values_all = project(value_weight, VD)
    within, query_decay_scale, value_decay_scale, carry_scale = decay_tables(decay_logs(jnp.arange(HEADS, dtype=jnp.float32)), SEG)

    @jax.checkpoint
    def block_step(running_state, pieces):
        block_queries, block_keys, block_values = pieces
        scores = low_back(jnp.einsum('hik,hjk->hij', block_queries, block_keys, precision=precise_mode))
        weights = low(scores * within)
        inner = jnp.einsum('hij,hjv->hiv', weights, block_values, precision=precise_mode)
        cross_term = jnp.einsum('puf,pfo->puo', block_queries * query_decay_scale[:, :, None], running_state, precision=precise_mode)
        state_update = jnp.einsum('dcf,dcg->dfg', block_keys, block_values * value_decay_scale[:, :, None], precision=precise_mode)
        return (carry_scale[:, None, None] * running_state + state_update, inner + cross_term)
    start = jnp.zeros((HEADS, QK, VD), jnp.float32)
    final_state, mixed = lax.scan(block_step, start, (queries, keys_all, values_all))
    mixed = low_back(mixed.transpose(0, 2, 1, 3).reshape(length_rows, HEADS, VD))
    swish_pre = low_back(jnp.dot(mixer_in, swish_weight, precision=precise_mode).reshape(length_rows, HEADS, VD))
    gated = low(swish_gate(swish_pre, mixed).reshape(length_rows, HEADS * VD))
    hidden_state = tokens_row + low_back(jnp.dot(gated, output_weight, precision=precise_mode))
    dense_in = low(normed(hidden_state, low(mid_gain)))
    gate_pre = low_back(jnp.dot(dense_in, gate_weight, precision=precise_mode))
    up_pre = low_back(jnp.dot(dense_in, up_weight, precision=precise_mode))
    inner_act = low_back(low(gelu_product(gate_pre, up_pre)))
    return hidden_state + low_back(jnp.dot(inner_act, down_weight, precision=precise_mode))

def reference(tokens, pre_gain, query_weight, key_weight, value_weight, swish_weight, output_weight, mid_gain, gate_weight, up_weight, down_weight, cotangent):
    params = tuple((weight.astype(jnp.float32) for weight in (pre_gain, query_weight, key_weight, value_weight, swish_weight, output_weight, mid_gain, gate_weight, up_weight, down_weight)))

    def one_sequence(totals, sequence_pair):
        row_in, row_cot = sequence_pair
        result, pullback = jax.vjp(forward, row_in.astype(jnp.float32), *params)
        grads = pullback(row_cot.astype(jnp.float32))
        summed = tuple((total + grad for total, grad in zip(totals, grads[1:])))
        return (summed, (result.astype(jnp.bfloat16), grads[0]))
    zero_grads = tuple((jnp.zeros_like(weight) for weight in params))
    totals, (layer_out, tokens_grad) = lax.scan(one_sequence, zero_grads, (tokens, cotangent))
    return (layer_out, tokens_grad) + totals
```

```python
import functools

import jax
import jax.numpy as jnp
from jax import lax
from jax.experimental import pallas as pl
from jax.experimental.pallas import tpu as pltpu
from jax.sharding import PartitionSpec as P

QK = 256
VD = 512
CHIPS_Z = 4
CORES = 2
F32 = jnp.float32
BF16 = jnp.bfloat16


class Line:
    def __init__(self, axis, total, size, stride):
        self.axis, self.size, self.stride = axis, size, stride
        self.starts = [i for i in range(total) if (i // stride) % size == 0]

    def here(self):
        return lax.rem(lax.div(lax.axis_index(self.axis), self.stride), self.size)

    def send(self, value, moves):
        pairs = [(o + i * self.stride, o + j * self.stride) for i, j in moves for o in self.starts]
        return lax.ppermute(value, self.axis, pairs)

    def ring(self, value, distance):
        return self.send(value, [(i, (i + distance) % self.size) for i in range(self.size)])

    def gather(self, own):
        return [own] + [self.ring(own, -k) for k in range(1, self.size)]

    def scatter(self, slots, kind):
        own = slots[0].astype(F32)
        for k in range(1, self.size):
            own = own + self.ring(slots[k].astype(kind), k).astype(F32)
        return own

    def place(self, slots):
        here = self.here()
        if self.size == 2:
            first = jnp.concatenate(slots, axis=0)
            second = jnp.concatenate(slots[::-1], axis=0)
            return jnp.where(here == 0, first, second)
        rows = slots[0].shape[0]
        twice = jnp.concatenate(slots + slots, axis=0)
        start = lax.rem(self.size - here, self.size) * rows
        return lax.dynamic_slice_in_dim(twice, start, self.size * rows, axis=0)


class Plan:
    def __init__(self, mesh):
        seq, shard = mesh.shape["seq"], mesh.shape["shard"]
        self.seq, self.shard = seq, shard
        self.along_x = Line("seq", seq, seq // CHIPS_Z, 1)
        self.along_z = Line("seq", seq, CHIPS_Z, seq // CHIPS_Z)
        self.along_core = Line("shard", shard, CORES, 1)
        self.along_y = Line("shard", shard, shard // CORES, CORES)

    def slot_owner(self):
        x, z = self.along_x, self.along_z
        return jnp.stack(
            [
                lax.rem(z.here() + k, z.size) * x.size + lax.rem(x.here() + j, x.size)
                for j in range(x.size)
                for k in range(z.size)
            ]
        ).astype(jnp.int32)

    def owner_slot(self):
        x, z = self.along_x, self.along_z
        return jnp.stack(
            [
                lax.rem(x.size + j - x.here(), x.size) * z.size
                + lax.rem(z.size + k - z.here(), z.size)
                for k in range(z.size)
                for j in range(x.size)
            ]
        ).astype(jnp.int32)

    def sum_rows(self, part, kind):
        core, y = self.along_core, self.along_y
        half = part.shape[0] // core.size
        halves = [
            lax.dynamic_slice_in_dim(part, lax.rem(core.here() + j, core.size) * half, half, 0)
            for j in range(core.size)
        ]
        mine = core.scatter(halves, kind)
        step = half // y.size
        steps = [
            lax.dynamic_slice_in_dim(mine, lax.rem(y.here() + k, y.size) * step, step, 0)
            for k in range(y.size)
        ]
        return y.scatter(steps, kind)

    def share_rows(self, own):
        core, y = self.along_core, self.along_y
        return core.place(core.gather(y.place(y.gather(own))))

    def own_rows(self, whole):
        core, y = self.along_core, self.along_y
        half = whole.shape[0] // core.size
        step = half // y.size
        return lax.dynamic_slice_in_dim(whole, core.here() * half + y.here() * step, step, 0)

    def scan_states(self, own, decay, later):
        x, z = self.along_x, self.along_z
        seqs, heads, rows, width = own.shape
        step = rows // x.size
        decay = decay[None, :, None, None]
        sign = -1 if later else 1
        place = x.size - 1 - x.here() if later else x.here()

        def part_for(value, distance):
            index = lax.rem(x.here() + distance, x.size) * step
            return lax.dynamic_slice_in_dim(value, index, step, 2)

        mine = part_for(own, 0)
        pieces = [mine] + [
            x.ring(part_for(own, d).astype(BF16), d).astype(F32) for d in range(1, x.size)
        ]

        def at(position):
            out = pieces[0]
            for d in range(1, x.size):
                source = lax.rem(x.here() - d + x.size, x.size)
                source = x.size - 1 - source if later else source
                out = jnp.where(source == position, pieces[d], out)
            return jnp.where(place == position, pieces[0], out)

        ordered = [at(i) for i in range(x.size)]
        row_sum = ordered[0]
        for piece in ordered[1:]:
            row_sum = row_sum * decay + piece
        row_decay = decay**x.size
        if later:
            one = [(i + 1, i) for i in range(z.size - 1)]
            two = [(i + 2, i) for i in range(z.size - 2)]
        else:
            one = [(i, i + 1) for i in range(z.size - 1)]
            two = [(i, i + 2) for i in range(z.size - 2)]
        near = z.send(row_sum.astype(BF16), one).astype(F32)
        pair = row_sum + row_decay * near
        far = z.send(pair.astype(BF16), two).astype(F32)
        running = near + row_decay * far
        entering = [running]
        for piece in ordered[:-1]:
            entering.append(entering[-1] * decay + piece)
        def for_device(distance):
            target = lax.rem(x.here() + distance, x.size)
            target = x.size - 1 - target if later else target
            out = entering[0]
            for i in range(1, x.size):
                out = jnp.where(target == i, entering[i], out)
            return out

        back = [for_device(0)] + [
            x.ring(for_device(d).astype(BF16), d).astype(F32) for d in range(1, x.size)
        ]
        step_of = [lax.rem(x.here() - d + x.size, x.size) for d in range(x.size)]
        out = jnp.zeros_like(own)
        for d in range(x.size):
            out = lax.dynamic_update_slice_in_dim(out, back[d], step_of[d] * step, 2)
        return out

    def sum_vector(self, part):
        vector = part.reshape(1, -1)
        for line in (self.along_core, self.along_y):
            total = vector
            arrived = [line.ring(vector, d) for d in range(1, line.size)]
            if line.size == 2:
                total = vector + arrived[0]
            else:
                every = [vector] + arrived
                total = sum(
                    line_pick(line, every, position) for position in range(line.size)
                )
            vector = total
        blocks = vector.reshape(self.along_x.size, self.along_z.size, -1)
        mine = self.along_x.scatter([blocks[j] for j in range(self.along_x.size)], F32)
        return self.along_z.scatter([mine[k : k + 1] for k in range(self.along_z.size)], F32)[0]


class Live:
    def __init__(self, plan):
        self._x, self._z = plan.along_x, plan.along_z

    def fence(self):
        names = [name for name in vars(self) if not name.startswith("_")]
        values = lax.optimization_barrier([getattr(self, name) for name in names])
        for name, value in zip(names, values):
            setattr(self, name, value)

    def gather_z(self, own):
        return [own] + [self._z.ring(own, -k) for k in range(1, self._z.size)]

    def gather_x(self, row):
        return [row] + [self._x.ring(row, -j) for j in range(1, self._x.size)]

    def scatter_x(self, others):
        return [self._x.ring(part, j) for j, part in enumerate(others, 1)]

    def scatter_z(self, own, arrived, axis):
        for part in arrived:
            own = own + part.astype(F32)
        step = own.shape[axis] // self._z.size
        slots = [lax.slice_in_dim(own, k * step, (k + 1) * step, axis=axis) for k in range(self._z.size)]
        return [slots[0]] + [
            self._z.ring(slots[k].astype(BF16), k) for k in range(1, self._z.size)
        ]


def total(parts):
    out = parts[0]
    for part in parts[1:]:
        out = out + part.astype(F32)
    return out


def line_pick(line, every, position):
    out = every[0]
    for d in range(1, line.size):
        source = lax.rem(line.here() - d + line.size, line.size)
        out = jnp.where(source == position, every[d], out)
    return out


def turn_kernel(table, in_ref, out_ref):
    width = in_ref.shape[1] // table.shape[0]
    for i in range(table.shape[0]):
        start = pl.multiple_of(table[i] * width, width)
        out_ref[:, i * width : (i + 1) * width] = in_ref[:, pl.ds(start, width)]


def turn(value, table):
    rows, width = value.shape
    tile = min(rows, 256)
    return pl.pallas_call(
        turn_kernel,
        grid_spec=pltpu.PrefetchScalarGridSpec(
            num_scalar_prefetch=1,
            grid=(rows // tile,),
            in_specs=[pl.BlockSpec((tile, width), lambda i, t: (i, 0))],
            out_specs=pl.BlockSpec((tile, width), lambda i, t: (i, 0)),
        ),
        out_shape=jax.ShapeDtypeStruct(value.shape, value.dtype),
        cost_estimate=pl.CostEstimate(
            flops=0, bytes_accessed=2 * value.size * value.dtype.itemsize, transcendentals=0
        ),
    )(table, value)


def norm_turn_kernel(table, in_ref, gain_ref, out_ref):
    width = in_ref.shape[1] // table.shape[0]
    values = in_ref[...].astype(F32)
    mean = jnp.mean(values, axis=-1, keepdims=True)
    centred = values - mean
    scale = lax.rsqrt(jnp.mean(centred * centred, axis=-1, keepdims=True) + 1e-05)
    for i in range(table.shape[0]):
        start = pl.multiple_of(table[i] * width, width)
        block = in_ref[:, pl.ds(start, width)].astype(F32)
        gain = gain_ref[:, i * width : (i + 1) * width]
        out_ref[:, i * width : (i + 1) * width] = ((block - mean) * scale * gain).astype(BF16)


def norm_turn(value, gain, table):
    rows, width = value.shape
    tile = min(rows, 256)
    return pl.pallas_call(
        norm_turn_kernel,
        grid_spec=pltpu.PrefetchScalarGridSpec(
            num_scalar_prefetch=1,
            grid=(rows // tile,),
            in_specs=[
                pl.BlockSpec((tile, width), lambda i, t: (i, 0)),
                pl.BlockSpec((1, width), lambda i, t: (0, 0)),
            ],
            out_specs=pl.BlockSpec((tile, width), lambda i, t: (i, 0)),
        ),
        out_shape=jax.ShapeDtypeStruct(value.shape, BF16),
        cost_estimate=pl.CostEstimate(
            flops=10 * value.size, bytes_accessed=4 * value.size, transcendentals=0
        ),
    )(table, value, gain.reshape(1, -1))


def silu_parts(values):
    sigmoid = 1.0 / (1.0 + jnp.exp(-values))
    return sigmoid, values * sigmoid


def norm_parts(values):
    centred = values - jnp.mean(values, axis=-1, keepdims=True)
    scale = lax.rsqrt(jnp.mean(centred * centred, axis=-1, keepdims=True) + 1e-05)
    return centred * scale, scale


def halves(values):
    high = values.astype(BF16)
    return high, (values - high.astype(F32)).astype(BF16)


def row_decay(log, rows, first, step):
    position = lax.broadcasted_iota(jnp.int32, (rows, 1), 0)
    return jnp.exp((first + step * position).astype(F32) * log)


def pair_decay(log, rows):
    row = lax.broadcasted_iota(jnp.int32, (rows, rows), 0)
    column = lax.broadcasted_iota(jnp.int32, (rows, rows), 1)
    offset = row - column
    return jnp.where(offset >= 0, jnp.exp(jnp.maximum(offset, 0).astype(F32) * log), 0.0)


def state_kernel(logs, key_ref, value_ref, state_ref):
    rows = key_ref.shape[0]
    scaled = key_ref[...].astype(F32) * row_decay(logs[pl.program_id(1)], rows, rows - 1, -1)
    high, low = halves(scaled)
    value = value_ref[...]
    state_ref[0, 0] = t_matmul(high, value) + t_matmul(low, value)


def mix_kernel(logs, query_ref, key_ref, value_ref, state_ref, swish_ref, gated_ref, mixed_ref):
    rows = key_ref.shape[0]
    log = logs[pl.program_id(1)]
    query = query_ref[...]
    weights = (matmul_t(query, key_ref[...]) * pair_decay(log, rows)).astype(BF16)
    high, low = halves(state_ref[0, 0])
    cross = matmul(query, high) + matmul(query, low)
    mixed = matmul(weights, value_ref[...]) + cross * row_decay(log, rows, 1, 1)
    mixed_ref[...] = mixed
    gated_ref[...] = (silu_parts(swish_ref[...])[1] * norm_parts(mixed)[0]).astype(BF16)


def gate_kernel(logs, grad_ref, swish_ref, mixed_ref, query_ref, swish_low_ref, mixed_low_ref, state_ref):
    rows = query_ref.shape[0]
    grad, swish_pre = grad_ref[...], swish_ref[...]
    normalized, scale = norm_parts(mixed_ref[...])
    sigmoid, silu = silu_parts(swish_pre)
    slope = sigmoid * (1.0 + swish_pre * (1.0 - sigmoid))
    swish_low_ref[...] = (grad * normalized * slope).astype(BF16)
    e = grad * silu
    mean = jnp.mean(e, axis=-1, keepdims=True)
    along = jnp.mean(e * normalized, axis=-1, keepdims=True)
    mixed_low = (scale * (e - mean - normalized * along)).astype(BF16)
    mixed_low_ref[...] = mixed_low
    scaled = query_ref[...].astype(F32) * row_decay(logs[pl.program_id(1)], rows, 1, 1)
    high, low = halves(scaled)
    state_ref[0, 0] = t_matmul(high, mixed_low) + t_matmul(low, mixed_low)


def mix_back_kernel(
    logs,
    query_ref,
    key_ref,
    value_ref,
    mixed_low_ref,
    state_ref,
    state_grad_ref,
    query_low_ref,
    key_low_ref,
    value_low_ref,
):
    rows = key_ref.shape[0]
    log = logs[pl.program_id(1)]
    query, key, value, mixed_low = (
        query_ref[...],
        key_ref[...],
        value_ref[...],
        mixed_low_ref[...],
    )
    decay = pair_decay(log, rows)
    weights = (matmul_t(query, key) * decay).astype(BF16)
    score = (matmul_t(mixed_low, value) * decay).astype(BF16)
    high, low = halves(state_ref[0, 0])
    cross = matmul_t(mixed_low, high) + matmul_t(mixed_low, low)
    query_low_ref[...] = (matmul(score, key) + cross * row_decay(log, rows, 1, 1)).astype(BF16)
    high, low = halves(state_grad_ref[0, 0])
    to_end = row_decay(log, rows, rows - 1, -1)
    cross = matmul_t(value, high) + matmul_t(value, low)
    key_low_ref[...] = (t_matmul(score, query) + cross * to_end).astype(BF16)
    cross = matmul(key, high) + matmul(key, low)
    value_low_ref[...] = (t_matmul(weights, mixed_low) + cross * to_end).astype(BF16)


class Heads:
    def __init__(self, logs, seqs, rows):
        self.logs, self.seqs, self.rows = logs, seqs, rows
        self.heads = logs.shape[0]

    def call(self, kernel, arrays, outs, flops):
        def flat(width, first):
            return pl.BlockSpec((self.rows, width), lambda b, h, _: (b, first + h))

        state = pl.BlockSpec((1, 1, QK, VD), lambda b, h, _: (b, h, 0, 0))
        specs, shapes, moved = [], [], 0
        for array, width, first in arrays:
            specs.append(state if width is None else flat(width, first))
            moved += array.size * array.dtype.itemsize
        for width, kind in outs:
            if width is None:
                shape = (self.seqs, self.heads, QK, VD)
            else:
                shape = (self.seqs * self.rows, self.heads * width)
            shapes.append(jax.ShapeDtypeStruct(shape, kind))
        return pl.pallas_call(
            kernel,
            grid_spec=pltpu.PrefetchScalarGridSpec(
                num_scalar_prefetch=1,
                grid=(self.seqs, self.heads),
                in_specs=specs,
                out_specs=[state if width is None else flat(width, 0) for width, _ in outs],
            ),
            out_shape=shapes,
            compiler_params=pltpu.CompilerParams(vmem_limit_bytes=40 * 1024 * 1024),
            cost_estimate=pl.CostEstimate(
                flops=flops * self.seqs * self.heads * self.rows,
                bytes_accessed=moved,
                transcendentals=self.seqs * self.heads * self.rows * self.rows,
            ),
        )(self.logs, *[array for array, _, _ in arrays])


def group_normed(values):
    centred = values - jnp.mean(values, axis=-1, keepdims=True)
    spread = jnp.mean(centred * centred, axis=-1, keepdims=True)
    return centred * lax.rsqrt(spread + 1e-05)


def normed(values, gain):
    return group_normed(values) * gain


def gelu_product(gate_pre, up_pre):
    return jax.nn.gelu(gate_pre) * up_pre


def matmul(left, right):
    return jnp.dot(left, right, preferred_element_type=F32)


def matmul_t(left, right):
    return lax.dot_general(left, right, (((1,), (1,)), ((), ())), preferred_element_type=F32)


def t_matmul(left, right):
    return lax.dot_general(left, right, (((0,), (0,)), ((), ())), preferred_element_type=F32)


def on_device(
    plan,
    tokens,
    pre_gain,
    query_weight,
    key_weight,
    value_weight,
    swish_weight,
    output_weight,
    mid_gain,
    gate_weight,
    up_weight,
    down_weight,
    cotangent,
):
    seq_count, seg_rows, model_width = tokens.shape
    row_count = seq_count * seg_rows
    blocks_x = plan.along_x.size
    block_width = model_width // blocks_x
    to_slots, to_owners = plan.slot_owner(), plan.owner_slot()

    e = Live(plan)
    e.tokens = tokens.reshape(row_count, model_width)
    e.cotangent = cotangent.reshape(row_count, model_width)
    gains = jnp.stack([pre_gain, mid_gain]).astype(BF16)
    gains = jnp.pad(gains, ((0, 14), (0, value_weight.shape[1] - gains.shape[1])))
    slice_width = pre_gain.shape[0]
    key_width = query_weight.shape[1]
    local_heads = key_width // QK
    hidden_units = gate_weight.shape[1]
    e.query_key = jnp.concatenate([query_weight, key_weight], axis=1)
    e.swish, e.output, e.gate, e.up, e.down = (
        swish_weight,
        output_weight,
        gate_weight,
        up_weight,
        down_weight,
    )

    def rows(parts):
        return jnp.concatenate(parts, axis=0)

    def columns(parts):
        return jnp.concatenate(parts, axis=1)

    head_index = (lax.axis_index("shard") * local_heads + jnp.arange(local_heads)).astype(F32)
    logs = jnp.log1p(-jnp.exp2(-5.0 - head_index))
    carry_scale = jnp.exp(seg_rows * logs)
    each = Heads(logs, seq_count, seg_rows)

    e.value = e.gather_z(jnp.concatenate([value_weight, gains], axis=0))
    e.grad_out = turn(e.cotangent, to_slots)
    del e.cotangent
    e.own_tokens = turn(plan.own_rows(e.tokens), to_slots)
    e.fence()
    e.value = e.gather_x(rows(e.value))
    e.query_key = e.gather_z(e.query_key)
    e.own_grad_out = plan.own_rows(e.grad_out).astype(F32)
    e.fence()
    e.query_key = e.gather_x(rows(e.query_key))
    e.swish = e.gather_z(e.swish)
    slots = [
        part[k * (slice_width + 16) : (k + 1) * (slice_width + 16)]
        for part in e.value
        for k in range(plan.along_z.size)
    ]
    e.full_value = rows([slot[:slice_width] for slot in slots])
    gains = columns([slot[slice_width : slice_width + 2, :slice_width] for slot in slots])
    gains = gains.astype(F32)
    e.full_pre, e.full_mid = gains[0], gains[1]
    del e.value
    e.mixer_in = norm_turn(e.tokens, e.full_pre, to_slots)
    del e.tokens
    e.values = matmul(e.mixer_in, e.full_value).astype(BF16)
    e.fence()
    e.swish = e.gather_x(rows(e.swish))
    e.output = e.gather_z(e.output)
    e.full_query_key = rows(e.query_key)
    del e.query_key
    query_key = matmul(e.mixer_in, e.full_query_key).astype(BF16)
    e.queries_keys = query_key
    (e.state,) = each.call(
        state_kernel,
        [(e.queries_keys, QK, local_heads), (e.values, VD, 0)],
        [(None, F32)],
        4 * QK * VD,
    )
    e.fence()
    e.output = e.gather_x(columns(e.output))
    e.gate = e.gather_z(e.gate)
    e.state = plan.scan_states(e.state, carry_scale, False)
    e.full_swish = rows(e.swish)
    del e.swish
    e.swish_pre = matmul(e.mixer_in, e.full_swish)
    e.fence()
    e.gate = e.gather_x(rows(e.gate))
    e.up = e.gather_z(e.up)
    e.full_output = columns(e.output)
    del e.output
    e.gated, e.mixed = each.call(
        mix_kernel,
        [
            (e.queries_keys, QK, 0),
            (e.queries_keys, QK, local_heads),
            (e.values, VD, 0),
            (e.state, None, 0),
            (e.swish_pre, VD, 0),
        ],
        [(VD, BF16), (VD, F32)],
        2 * seg_rows * (QK + VD) + 4 * QK * VD,
    )
    branch = plan.sum_rows(matmul(e.gated, e.full_output), BF16)
    e.hidden_state = e.own_tokens.astype(F32) + branch
    e.dense_own = normed(e.hidden_state, e.full_mid).astype(BF16)
    e.fence()
    e.up = e.gather_x(rows(e.up))
    e.down = e.gather_z(e.down)
    e.full_gate = rows(e.gate)
    del e.gate
    e.dense_in = plan.share_rows(e.dense_own)
    del e.dense_own
    e.fence()

    def part_rows(left, right):
        return [
            t_matmul(left[:, j * block_width : (j + 1) * block_width], right)
            for j in range(blocks_x)
        ]

    def part_columns(left, right):
        return [
            t_matmul(left, right[:, j * block_width : (j + 1) * block_width])
            for j in range(blocks_x)
        ]

    def low(parts):
        return [part.astype(BF16) for part in parts]

    e.down = e.gather_x(columns(e.down))
    e.full_up = rows(e.up)
    del e.up
    e.gate_pre = matmul(e.dense_in, e.full_gate)
    e.up_pre = matmul(e.dense_in, e.full_up)
    e.inner_act = gelu_product(e.gate_pre, e.up_pre).astype(BF16)
    e.down_own, *others = part_columns(e.inner_act, e.grad_out)
    e.down_others = low(others)
    e.fence()
    e.down_others = e.scatter_x(e.down_others)
    e.full_down = columns(e.down)
    del e.down
    inner_grad = matmul_t(e.grad_out, e.full_down).astype(BF16)
    gate_pre_grad, up_pre_grad = jax.vjp(gelu_product, e.gate_pre, e.up_pre)[1](
        inner_grad.astype(F32)
    )
    del e.gate_pre, e.up_pre
    gate_low, e.up_low = gate_pre_grad.astype(BF16), up_pre_grad.astype(BF16)
    e.dense_in_part = matmul_t(gate_low, e.full_gate) + matmul_t(e.up_low, e.full_up)
    e.gate_own, *others = part_rows(e.dense_in, gate_low)
    e.gate_others = low(others)
    e.fence()
    e.down_slots = e.scatter_z(e.down_own, e.down_others, 1)
    del e.down_own, e.down_others
    e.gate_others = e.scatter_x(e.gate_others)
    dense_in_grad = plan.sum_rows(e.dense_in_part, BF16)
    del e.dense_in_part
    hidden_from_norm, e.mid_part = jax.vjp(normed, e.hidden_state, e.full_mid)[1](dense_in_grad)
    e.hidden_grad = e.own_grad_out + hidden_from_norm
    e.branch_own = e.hidden_grad.astype(BF16)
    e.up_own, *others = part_rows(e.dense_in, e.up_low)
    e.up_others = low(others)
    e.fence()
    e.gate_slots = e.scatter_z(e.gate_own, e.gate_others, 0)
    del e.gate_own, e.gate_others
    e.up_others = e.scatter_x(e.up_others)
    branch_low = plan.share_rows(e.branch_own)
    del e.branch_own
    e.output_own, *others = part_columns(e.gated, branch_low)
    e.output_others = low(others)
    gated_grad = matmul_t(branch_low, e.full_output)
    e.swish_low, e.mixed_low, e.state_grad = each.call(
        gate_kernel,
        [
            (gated_grad, VD, 0),
            (e.swish_pre, VD, 0),
            (e.mixed, VD, 0),
            (e.queries_keys, QK, 0),
        ],
        [(VD, BF16), (VD, BF16), (None, F32)],
        4 * QK * VD,
    )
    del e.swish_pre, e.mixed
    e.fence()
    e.up_slots = e.scatter_z(e.up_own, e.up_others, 0)
    del e.up_own, e.up_others
    e.output_others = e.scatter_x(e.output_others)
    e.state_grad = plan.scan_states(e.state_grad, carry_scale, True)
    e.swish_own, *others = part_rows(e.mixer_in, e.swish_low)
    e.swish_others = low(others)
    e.fence()
    e.output_slots = e.scatter_z(e.output_own, e.output_others, 1)
    del e.output_own, e.output_others
    e.swish_others = e.scatter_x(e.swish_others)
    e.query_low, e.key_low, e.value_low = each.call(
        mix_back_kernel,
        [
            (e.queries_keys, QK, 0),
            (e.queries_keys, QK, local_heads),
            (e.values, VD, 0),
            (e.mixed_low, VD, 0),
            (e.state, None, 0),
            (e.state_grad, None, 0),
        ],
        [(QK, BF16), (QK, BF16), (VD, BF16)],
        seg_rows * (6 * QK + 4 * VD) + 12 * QK * VD,
    )
    del e.state, e.state_grad, e.mixed_low, e.queries_keys, e.values
    e.value_own, *others = part_rows(e.mixer_in, e.value_low)
    e.value_others = low(others)
    e.fence()
    e.swish_slots = e.scatter_z(e.swish_own, e.swish_others, 0)
    del e.swish_own, e.swish_others
    e.value_others = e.scatter_x(e.value_others)
    query_key_low = columns([e.query_low, e.key_low])
    e.query_key_own, *others = part_rows(e.mixer_in, query_key_low)
    e.query_key_others = low(others)
    mixer_in_part = matmul_t(query_key_low, e.full_query_key)
    mixer_in_part = mixer_in_part + matmul_t(e.value_low, e.full_value)
    e.mixer_in_part = mixer_in_part + matmul_t(e.swish_low, e.full_swish)
    del e.query_low, e.key_low, e.value_low, e.swish_low
    e.fence()
    e.value_slots = e.scatter_z(e.value_own, e.value_others, 0)
    del e.value_own, e.value_others
    e.query_key_others = e.scatter_x(e.query_key_others)
    mixer_in_grad = plan.sum_rows(e.mixer_in_part, BF16)
    del e.mixer_in_part
    tokens_from_norm, e.pre_part = jax.vjp(normed, e.own_tokens.astype(F32), e.full_pre)[1](
        mixer_in_grad
    )
    e.tokens_grad = turn((e.hidden_grad + tokens_from_norm).astype(BF16), to_owners)
    e.dense_out_part = matmul(e.inner_act, e.full_down)
    e.fence()
    e.query_key_slots = e.scatter_z(e.query_key_own, e.query_key_others, 0)
    tokens_grad = plan.share_rows(e.tokens_grad).astype(F32)
    dense_out = plan.sum_rows(e.dense_out_part, BF16)
    layer_out = plan.share_rows(turn((e.hidden_state + dense_out).astype(BF16), to_owners))
    mid_grad = plan.sum_vector(e.mid_part)
    pre_grad = plan.sum_vector(e.pre_part)
    query_key_grad = total(e.query_key_slots)
    return (
        layer_out.reshape(tokens.shape),
        tokens_grad.reshape(tokens.shape),
        pre_grad,
        query_key_grad[:, :key_width],
        query_key_grad[:, key_width:],
        total(e.value_slots),
        total(e.swish_slots),
        total(e.output_slots),
        mid_grad,
        total(e.gate_slots),
        total(e.up_slots),
        total(e.down_slots),
    )


def solution(mesh):
    rows, weight, turned, vector = (
        P(None, "seq", None),
        P("seq", "shard"),
        P("shard", "seq"),
        P("seq"),
    )
    return jax.shard_map(
        functools.partial(on_device, Plan(mesh)),
        mesh=mesh,
        in_specs=(
            rows,
            vector,
            weight,
            weight,
            weight,
            weight,
            turned,
            vector,
            weight,
            weight,
            turned,
            rows,
        ),
        out_specs=(
            rows,
            rows,
            vector,
            weight,
            weight,
            weight,
            weight,
            turned,
            vector,
            weight,
            weight,
            turned,
        ),
        check_vma=False,
    )
```

```python
import functools

import jax
import jax.numpy as jnp
from jax import lax
from jax.experimental import pallas as pl
from jax.experimental.pallas import tpu as pltpu
from jax.sharding import PartitionSpec as P

QK = 256
VD = 512
CHIPS_Z = 4
CORES = 2
F32 = jnp.float32
BF16 = jnp.bfloat16
VMEM_LIMIT = 52 * 1024 * 1024


class Line:
    def __init__(self, axis, total, size, stride):
        self.axis, self.size, self.stride = axis, size, stride
        self.starts = [i for i in range(total) if (i // stride) % size == 0]

    def here(self):
        return lax.rem(lax.div(lax.axis_index(self.axis), self.stride), self.size)

    def send(self, value, moves):
        pairs = [(o + i * self.stride, o + j * self.stride) for i, j in moves for o in self.starts]
        return lax.ppermute(value, self.axis, pairs)

    def ring(self, value, distance):
        return self.send(value, [(i, (i + distance) % self.size) for i in range(self.size)])

    def exchange(self, blocks):
        groups = [[o + i * self.stride for i in range(self.size)] for o in self.starts]
        return lax.all_to_all(
            blocks, self.axis, split_axis=0, concat_axis=0, axis_index_groups=groups, tiled=True
        )

    def total(self, value):
        every = [value] + [self.ring(value, d) for d in range(1, self.size)]
        if self.size == 2:
            return every[0] + every[1]
        out = 0.0
        for position in range(self.size):
            out = out + self.pick(every, position)
        return out

    def pick(self, every, position):
        out = every[0]
        for d in range(1, self.size):
            source = lax.rem(self.here() - d + self.size, self.size)
            out = jnp.where(source == position, every[d], out)
        return out


class Plan:
    def __init__(self, mesh):
        seq, shard = mesh.shape["seq"], mesh.shape["shard"]
        self.seq, self.shard = seq, shard
        self.along_x = Line("seq", seq, seq // CHIPS_Z, 1)
        self.along_z = Line("seq", seq, CHIPS_Z, seq // CHIPS_Z)
        self.along_core = Line("shard", shard, CORES, 1)
        self.along_y = Line("shard", shard, shard // CORES, CORES)

    def slot_owner(self):
        x, z = self.along_x, self.along_z
        return jnp.stack(
            [
                k * x.size + lax.rem(x.here() + j, x.size)
                for j in range(x.size)
                for k in range(z.size)
            ]
        ).astype(jnp.int32)

    def owner_slot(self):
        x, z = self.along_x, self.along_z
        return jnp.stack(
            [
                lax.rem(x.size + j - x.here(), x.size) * z.size + k
                for k in range(z.size)
                for j in range(x.size)
            ]
        ).astype(jnp.int32)

    def row_tiles(self):
        core, y = self.along_core, self.along_y
        return jnp.stack(
            [
                lax.rem(core.here() + j, core.size) * y.size + lax.rem(y.here() + k, y.size)
                for j in (*range(1, core.size), 0)
                for k in range(y.size)
            ]
        ).astype(jnp.int32)

    def own_rows(self, whole):
        core, y = self.along_core, self.along_y
        step = whole.shape[0] // self.shard
        return lax.dynamic_slice_in_dim(whole, (core.here() * y.size + y.here()) * step, step, 0)

    def copies(self, own):
        def kernel(_, in_ref, out_ref):
            out_ref[0] = in_ref[...]

        return call(
            kernel,
            jnp.zeros((1,), jnp.int32),
            (self.along_z.size,),
            [own],
            [resident(own)],
            [((self.along_z.size, *own.shape), own.dtype)],
            [pl.BlockSpec((1, *own.shape), lambda i, _: (i, 0, 0))],
        )[0]

    def gather_x(self, row):
        return [row] + [self.along_x.ring(row, -j) for j in range(1, self.along_x.size)]

    def scatter_x(self, others):
        return [self.along_x.ring(part, j) for j, part in enumerate(others, 1)]

    def scatter_z(self, own, arrived, extra=None):
        return self.along_z.exchange(add_blocks(own, arrived, extra))

    def sum_cores(self, others, own):
        core, y = self.along_core, self.along_y
        arrived = [core.ring(piece, d) for d in range(1, core.size) for piece in others]
        return fold_tiles(own, arrived, y.size)

    def sum_y(self, pieces):
        y = self.along_y
        return [y.ring(piece, k) for k, group in enumerate(pieces, 1) for piece in group]

    def share_y(self, pieces):
        y = self.along_y
        return [pieces] + [[y.ring(piece, -k) for piece in pieces] for k in range(1, y.size)]

    def share_cores(self, tiles, kind, columns=None):
        core, y = self.along_core, self.along_y
        others = [[core.ring(piece, 1) for piece in pieces] for pieces in tiles]
        here = jnp.stack([core.here(), y.here()]).astype(jnp.int32)
        if columns is None:
            columns = jnp.zeros((1,), jnp.int32)
        return place_tiles(jnp.concatenate([here, columns]), tiles, others, kind)

    def scan_begin(self, own):
        x = self.along_x
        step = own.shape[2] // x.size

        def part_for(distance):
            index = lax.rem(x.here() + distance, x.size) * step
            return lax.dynamic_slice_in_dim(own, index, step, 2)

        return [part_for(0)] + [
            x.ring(part_for(d).astype(BF16), d).astype(F32) for d in range(1, x.size)
        ]

    def scan_middle(self, pieces, decay, later):
        x, z = self.along_x, self.along_z
        seqs = range(pieces[0].shape[0])
        decay = decay[None, :, None, None]

        def order(device):
            return x.size - 1 - device if later else device

        def split(value):
            return [value[b : b + 1] for b in seqs]

        pieces = [split(piece) for piece in pieces]
        ordered = [
            [x.pick([piece[b] for piece in pieces], order(i)) for i in range(x.size)] for b in seqs
        ]
        row_sum = []
        for b in seqs:
            out = ordered[b][0]
            for piece in ordered[b][1:]:
                out = out * decay + piece
            row_sum.append(out)
        row_decay = decay**x.size
        pairs = [[(i, i + d) for i in range(z.size - d)] for d in (1, 2)]
        if later:
            pairs = [[(j, i) for i, j in moves] for moves in pairs]
        near = [z.send(value.astype(BF16), pairs[0]).astype(F32) for value in row_sum]
        pair = [row_sum[b] + row_decay * near[b] for b in seqs]
        far = [z.send(value.astype(BF16), pairs[1]).astype(F32) for value in pair]
        out = []
        for b in seqs:
            entering = [near[b] + row_decay * far[b]]
            for piece in ordered[b][:-1]:
                entering.append(entering[-1] * decay + piece)

            def for_device(distance):
                target = order(lax.rem(x.here() + distance, x.size))
                value = entering[0]
                for i in range(1, x.size):
                    value = jnp.where(target == i, entering[i], value)
                return value

            out.append(
                [for_device(0)] + [for_device(d).astype(BF16) for d in range(1, x.size)]
            )
        return out

    def scan_end(self, shares):
        x = self.along_x
        out = []
        for own, *others in shares:
            back = [own] + [x.ring(part, d).astype(F32) for d, part in enumerate(others, 1)]
            out.append(jnp.concatenate([x.pick(back, i) for i in range(x.size)], axis=2))
        return jnp.concatenate(out, axis=0)

    def gains_x(self, gains):
        x, z = self.along_x, self.along_z
        slots = jnp.zeros((2, z.size, x.size, gains.shape[1]), gains.dtype)
        slots = lax.dynamic_update_slice(slots, gains[:, None, None], (0, z.here(), x.here(), 0))
        return x.total(slots.reshape(2, z.size, -1))

    def gains_z(self, slots):
        x, z = self.along_x, self.along_z
        slots = z.total(slots).reshape(2, z.size, x.size, -1)
        turned = [
            lax.dynamic_slice_in_dim(slots, lax.rem(x.here() + j, x.size), 1, 2)[:, :, 0]
            for j in range(x.size)
        ]
        return jnp.concatenate(turned, axis=1).reshape(2, -1)

    def sum_vectors(self, vectors):
        mine = vectors[:, 0]
        for part in self.scatter_x([vectors[:, j] for j in range(1, self.along_x.size)]):
            mine = mine + part
        return mine.reshape(mine.shape[0], self.along_z.size, -1).transpose(1, 0, 2)


CHEAP = pl.CostEstimate(flops=0, bytes_accessed=0, transcendentals=0)


def resident(array):
    return pl.BlockSpec(
        array.shape, lambda *_: (0,) * array.ndim, pipeline_mode=pl.Buffered(1)
    )


def call(kernel, table, grid, arrays, specs, outs, out_specs):
    return pl.pallas_call(
        kernel,
        grid_spec=pltpu.PrefetchScalarGridSpec(
            num_scalar_prefetch=1, grid=grid, in_specs=specs, out_specs=out_specs
        ),
        out_shape=[jax.ShapeDtypeStruct(*out) for out in outs],
        compiler_params=pltpu.CompilerParams(vmem_limit_bytes=VMEM_LIMIT),
        cost_estimate=CHEAP,
    )(table, *arrays)


def turn_kernel(table, in_ref, out_ref):
    width = in_ref.shape[1] // table.shape[0]
    for i in range(table.shape[0]):
        start = pl.multiple_of(table[i] * width, width)
        out_ref[:, i * width : (i + 1) * width] = in_ref[:, pl.ds(start, width)]


def turn(value, table):
    rows, width = value.shape
    tile = min(rows, 256)
    return pl.pallas_call(
        turn_kernel,
        grid_spec=pltpu.PrefetchScalarGridSpec(
            num_scalar_prefetch=1,
            grid=(rows // tile,),
            in_specs=[pl.BlockSpec((tile, width), lambda i, t: (i, 0))],
            out_specs=pl.BlockSpec((tile, width), lambda i, t: (i, 0)),
        ),
        out_shape=jax.ShapeDtypeStruct(value.shape, value.dtype),
        cost_estimate=CHEAP,
    )(table, value)


def norm_turn_kernel(table, in_ref, gain_ref, out_ref):
    width = in_ref.shape[1] // table.shape[0]
    values = in_ref[...].astype(F32)
    mean = jnp.mean(values, axis=-1, keepdims=True)
    centred = values - mean
    scale = lax.rsqrt(jnp.mean(centred * centred, axis=-1, keepdims=True) + 1e-05)
    for i in range(table.shape[0]):
        start = pl.multiple_of(table[i] * width, width)
        block = in_ref[:, pl.ds(start, width)].astype(F32)
        gain = gain_ref[:, i * width : (i + 1) * width]
        out_ref[:, i * width : (i + 1) * width] = ((block - mean) * scale * gain).astype(BF16)


def norm_turn(value, gain, table):
    rows, width = value.shape
    tile = min(rows, 256)
    return pl.pallas_call(
        norm_turn_kernel,
        grid_spec=pltpu.PrefetchScalarGridSpec(
            num_scalar_prefetch=1,
            grid=(rows // tile,),
            in_specs=[
                pl.BlockSpec((tile, width), lambda i, t: (i, 0)),
                pl.BlockSpec((1, width), lambda i, t: (0, 0)),
            ],
            out_specs=pl.BlockSpec((tile, width), lambda i, t: (i, 0)),
        ),
        out_shape=jax.ShapeDtypeStruct(value.shape, BF16),
        cost_estimate=CHEAP,
    )(table, value, gain.reshape(1, -1))


def silu_parts(values):
    sigmoid = 1.0 / (1.0 + jnp.exp(-values))
    return sigmoid, values * sigmoid


def norm_parts(values):
    centred = values - jnp.mean(values, axis=-1, keepdims=True)
    scale = lax.rsqrt(jnp.mean(centred * centred, axis=-1, keepdims=True) + 1e-05)
    return centred * scale, scale


def halves(values):
    high = values.astype(BF16)
    return high, (values - high.astype(F32)).astype(BF16)


def row_decay(log, rows, first, step):
    position = lax.broadcasted_iota(jnp.int32, (rows, 1), 0)
    return jnp.exp((first + step * position).astype(F32) * log)


def pair_decay(log, rows):
    row = lax.broadcasted_iota(jnp.int32, (rows, rows), 0)
    column = lax.broadcasted_iota(jnp.int32, (rows, rows), 1)
    offset = row - column
    return jnp.where(offset >= 0, jnp.exp(jnp.maximum(offset, 0).astype(F32) * log), 0.0)


def state_kernel(logs, key_ref, value_ref, state_ref):
    rows = key_ref.shape[0]
    scaled = key_ref[...].astype(F32) * row_decay(logs[pl.program_id(1)], rows, rows - 1, -1)
    high, low = halves(scaled)
    value = value_ref[...]
    state_ref[0, 0] = t_matmul(high, value) + t_matmul(low, value)


def mix_kernel(logs, query_ref, key_ref, value_ref, state_ref, swish_ref, gated_ref, mixed_ref):
    rows = key_ref.shape[0]
    log = logs[pl.program_id(1)]
    query = query_ref[...]
    weights = (matmul_t(query, key_ref[...]) * pair_decay(log, rows)).astype(BF16)
    high, low = halves(state_ref[0, 0])
    cross = matmul(query, high) + matmul(query, low)
    mixed = matmul(weights, value_ref[...]) + cross * row_decay(log, rows, 1, 1)
    mixed_ref[...] = mixed
    gated_ref[...] = (silu_parts(swish_ref[...])[1] * norm_parts(mixed)[0]).astype(BF16)


def gate_kernel(logs, *refs):
    (branch_ref, *output_refs), (swish_ref, mixed_ref, query_ref) = refs[:-6], refs[-6:-3]
    swish_low_ref, mixed_low_ref, state_ref = refs[-3:]
    rows = query_ref.shape[0]
    swish_pre = swish_ref[...]
    grad = from_columns(branch_ref[...], output_refs)
    normalized, scale = norm_parts(mixed_ref[...])
    sigmoid, silu = silu_parts(swish_pre)
    slope = sigmoid * (1.0 + swish_pre * (1.0 - sigmoid))
    swish_low_ref[...] = (grad * normalized * slope).astype(BF16)
    e = grad * silu
    mean = jnp.mean(e, axis=-1, keepdims=True)
    along = jnp.mean(e * normalized, axis=-1, keepdims=True)
    mixed_low = (scale * (e - mean - normalized * along)).astype(BF16)
    mixed_low_ref[...] = mixed_low
    scaled = query_ref[...].astype(F32) * row_decay(logs[pl.program_id(1)], rows, 1, 1)
    high, low = halves(scaled)
    state_ref[0, 0] = t_matmul(high, mixed_low) + t_matmul(low, mixed_low)


def mix_back_kernel(
    logs,
    query_ref,
    key_ref,
    value_ref,
    mixed_low_ref,
    state_ref,
    state_grad_ref,
    query_low_ref,
    key_low_ref,
    value_low_ref,
):
    rows = key_ref.shape[0]
    log = logs[pl.program_id(1)]
    query, key, value, mixed_low = (
        query_ref[...],
        key_ref[...],
        value_ref[...],
        mixed_low_ref[...],
    )
    decay = pair_decay(log, rows)
    weights = (matmul_t(query, key) * decay).astype(BF16)
    score = (matmul_t(mixed_low, value) * decay).astype(BF16)
    high, low = halves(state_ref[0, 0])
    cross = matmul_t(mixed_low, high) + matmul_t(mixed_low, low)
    query_low_ref[...] = (matmul(score, key) + cross * row_decay(log, rows, 1, 1)).astype(BF16)
    high, low = halves(state_grad_ref[0, 0])
    to_end = row_decay(log, rows, rows - 1, -1)
    cross = matmul_t(value, high) + matmul_t(value, low)
    key_low_ref[...] = (t_matmul(score, query) + cross * to_end).astype(BF16)
    cross = matmul(key, high) + matmul(key, low)
    value_low_ref[...] = (t_matmul(weights, mixed_low) + cross * to_end).astype(BF16)


def at_once(kernel, arrays, outs, table=None):
    if table is None:
        table = jnp.zeros((1,), jnp.int32)
    return call(
        kernel,
        table,
        (1,),
        arrays,
        [resident(array) for array in arrays],
        outs,
        [pl.BlockSpec(shape, lambda i, _, n=len(shape): (0,) * n) for shape, _ in outs],
    )


def add_blocks(own, arrived, extra=None):
    count, rows, columns = own.shape
    more = () if extra is None else (extra,)
    below = 0 if extra is None else 16

    def kernel(_, *refs):
        out = refs[0][...].astype(F32)
        for ref in refs[1 : 1 + len(arrived)]:
            out = out + ref[...].astype(F32)
        refs[-1][:, :rows, :] = out.astype(BF16)
        if more:
            refs[-1][:, rows:, :] = refs[-2][...]

    block = pl.BlockSpec((1, rows, columns), lambda i, _: (i, 0, 0))
    if more:
        extra = jnp.pad(
            extra.astype(BF16),
            ((0, 0), (0, below - extra.shape[1]), (0, columns - extra.shape[2])),
        )
        more = (extra,)
    return call(
        kernel,
        jnp.zeros((1,), jnp.int32),
        (count,),
        [own, *arrived, *more],
        [block] * (1 + len(arrived))
        + [pl.BlockSpec((1, below, columns), lambda i, _: (i, 0, 0)) for _ in more],
        [((count, rows + below, columns), BF16)],
        [pl.BlockSpec((1, rows + below, columns), lambda i, _: (i, 0, 0))],
    )[0]


def fold_tiles(own, arrived, tiles):
    rows, width = own.shape
    tile = rows // tiles
    piece = tile // 2

    def kernel(_, own_ref, *refs):
        outs = refs[len(arrived) :]
        for i in range(2 * tiles):
            value = own_ref[i * piece : (i + 1) * piece, :]
            for ref in refs[i : len(arrived) : 2 * tiles]:
                value = value + ref[...].astype(F32)
            if i < 2:
                outs[0][i * piece : (i + 1) * piece, :] = value
            else:
                outs[i - 1][...] = value.astype(BF16)

    mine, *pieces = at_once(
        kernel,
        [own, *arrived],
        [((tile, width), F32)] + [((piece, width), BF16)] * (2 * tiles - 2),
    )
    return mine, [pieces[2 * k : 2 * k + 2] for k in range(tiles - 1)]


def summed(mine_ref, refs, piece):
    rows = mine_ref.shape[0] // 2
    value = mine_ref[piece * rows : (piece + 1) * rows, :]
    for ref in refs[piece::2]:
        value = value + ref[...].astype(F32)
    return value


def enter_dense(mine, arrived, tokens, gain):
    rows, width = mine.shape
    half = rows // 2

    def kernel(_, mine_ref, tokens_ref, gain_ref, *refs):
        hidden_ref, *outs = refs[len(arrived) :]
        for i in range(2):
            part = slice(i * half, (i + 1) * half)
            hidden = tokens_ref[part, :].astype(F32) + summed(mine_ref, refs[: len(arrived)], i)
            hidden_ref[part, :] = hidden
            outs[i][...] = (norm_parts(hidden)[0] * gain_ref[...]).astype(BF16)

    hidden, *pieces = at_once(
        kernel,
        [mine, tokens, gain.reshape(1, -1), *arrived],
        [((rows, width), F32)] + [((half, width), BF16)] * 2,
    )
    return hidden, pieces


def leave_dense(mine, arrived, hidden):
    rows, width = mine.shape
    half = rows // 2

    def kernel(_, mine_ref, hidden_ref, *refs):
        for i in range(2):
            value = hidden_ref[i * half : (i + 1) * half, :] + summed(
                mine_ref, refs[: len(arrived)], i
            )
            refs[len(arrived) + i][...] = value.astype(BF16)

    return at_once(kernel, [mine, hidden, *arrived], [((half, width), BF16)] * 2)


def norm_backward(mine, arrived, values, gain, residual, keep):
    rows, width = mine.shape
    half = rows // 2

    def kernel(_, mine_ref, values_ref, gain_ref, residual_ref, *refs):
        gain_out, first, second, *whole = refs[len(arrived) :]
        gain_sum = 0.0
        for i in range(2):
            part = slice(i * half, (i + 1) * half)
            grad = summed(mine_ref, refs[: len(arrived)], i)
            normalized, scale = norm_parts(values_ref[part, :].astype(F32))
            gain_sum = gain_sum + jnp.sum(grad * normalized, axis=0, keepdims=True)
            e = grad * gain_ref[...]
            mean = jnp.mean(e, axis=-1, keepdims=True)
            along = jnp.mean(e * normalized, axis=-1, keepdims=True)
            out = residual_ref[part, :].astype(F32) + scale * (e - mean - normalized * along)
            (first, second)[i][...] = out.astype(BF16)
            for ref in whole:
                ref[part, :] = out
        gain_out[...] = gain_sum

    gain_part, first, second, *whole = at_once(
        kernel,
        [mine, values, gain.reshape(1, -1), residual, *arrived],
        [((1, width), F32)]
        + [((half, width), BF16)] * 2
        + [((rows, width), F32)] * (1 if keep else 0),
    )
    return gain_part, [first, second], *whole


def place_tiles(table, near, far, kind):
    tiles = len(near)
    pieces = [piece for tile in near + far for piece in tile]
    piece, width = pieces[0].shape
    columns = table.shape[0] - 2
    block = width // columns

    def kernel(table, *refs):
        out_ref = refs[-1]
        step = pl.program_id(0)
        for i in range(2 * tiles):
            core = lax.rem(table[0] + i // tiles, CORES)
            row = lax.rem(table[1] + i % tiles, tiles)

            @pl.when(step == core * tiles + row)
            def _(i=i):
                for part in range(2):
                    ref = refs[2 * i + part]
                    for j in range(columns):
                        start = pl.multiple_of(table[2 + j] * block, block)
                        out_ref[
                            part * piece : (part + 1) * piece, j * block : (j + 1) * block
                        ] = ref[:, pl.ds(start, block)].astype(kind)

    return call(
        kernel,
        table,
        (CORES * tiles,),
        pieces,
        [resident(ref) for ref in pieces],
        [((2 * CORES * tiles * piece, width), kind)],
        [pl.BlockSpec((2 * piece, width), lambda i, _: (i, 0))],
    )[0]


def by_rows(ref):
    return ref[...].reshape(-1, ref.shape[2])


def from_columns(values, refs):
    width = refs[0].shape[0] * refs[0].shape[2]
    out = 0.0
    for j, ref in enumerate(refs):
        weight = jnp.concatenate([ref[k] for k in range(ref.shape[0])], axis=1)
        out = out + matmul_t(values[:, j * width : (j + 1) * width], weight)
    return out


def project(values, weight, kind):
    rows, width = values.shape
    tile = min(rows, 256)
    columns = weight[0].shape[2]

    def kernel(_, in_ref, *refs):
        depth = width // len(weight)
        out = matmul(in_ref[:, :depth], by_rows(refs[0]))
        for j in range(1, len(weight)):
            out = out + matmul(in_ref[:, j * depth : (j + 1) * depth], by_rows(refs[j]))
        refs[-1][...] = out.astype(kind)

    return call(
        kernel,
        jnp.zeros((1,), jnp.int32),
        (rows // tile,),
        [values, *weight],
        [pl.BlockSpec((tile, width), lambda i, _: (i, 0))] + [resident(w) for w in weight],
        [((rows, columns), kind)],
        [pl.BlockSpec((tile, columns), lambda i, _: (i, 0))],
    )[0]


def parts_by_rows(compute, table, model_width, arrays, specs, outs, out_specs):
    count = table.shape[0]
    rows = arrays[0].shape[0]
    tile = rows // count
    away = count - count // CORES
    half = tile // 2

    def kernel(table, *refs):
        step = pl.program_id(0)
        pieces, own_ref = refs[-2 * away - 1 : -1], refs[-1]
        value = compute(*refs[: -2 * away - 1])
        for i in range(away):

            @pl.when(step == i)
            def _(i=i):
                pieces[2 * i][...] = value[:half].astype(BF16)
                pieces[2 * i + 1][...] = value[half:].astype(BF16)

        @pl.when(step >= away)
        def _():
            own_ref[...] = value

    *results, own = call(
        kernel,
        table,
        (count,),
        arrays,
        specs,
        outs + [((half, model_width), BF16)] * (2 * away) + [(((count - away) * tile, model_width), F32)],
        out_specs
        + [pl.BlockSpec((half, model_width), lambda i, t: (0, 0))] * (2 * away)
        + [pl.BlockSpec((tile, model_width), lambda i, t: (jnp.maximum(i - away, 0), 0))],
    )
    return *results[: len(outs)], results[len(outs) :], own


def tile_of(array, table):
    return pl.BlockSpec(
        (array.shape[0] // table.shape[0], array.shape[1]), lambda i, t: (t[i], 0)
    )


def to_columns(values, weight, table):
    count, _, width = weight[0].shape

    def compute(in_ref, *refs):
        value = in_ref[...]
        return jnp.concatenate(
            [matmul(value, ref[k]) for ref in refs for k in range(count)], axis=1
        )

    return parts_by_rows(
        compute,
        table,
        len(weight) * count * width,
        [values, *weight],
        [tile_of(values, table)] + [resident(w) for w in weight],
        [],
        [],
    )


def dense_forward(dense_in, gate, up):
    rows, width = dense_in.shape
    tile = min(rows, 256)
    units = gate[0].shape[2]

    def kernel(_, in_ref, *refs):
        gate_refs, up_refs = refs[: len(gate)], refs[len(gate) : -3]
        depth = width // len(gate)
        pre = []
        for weights in (gate_refs, up_refs):
            out = 0.0
            for j, ref in enumerate(weights):
                out = out + matmul(in_ref[:, j * depth : (j + 1) * depth], by_rows(ref))
            pre.append(out)
        refs[-3][...], refs[-2][...] = pre
        refs[-1][...] = (gelu_parts(pre[0])[0] * pre[1]).astype(BF16)

    block = pl.BlockSpec((tile, units), lambda i, _: (i, 0))
    return call(
        kernel,
        jnp.zeros((1,), jnp.int32),
        (rows // tile,),
        [dense_in, *gate, *up],
        [pl.BlockSpec((tile, width), lambda i, _: (i, 0))] + [resident(w) for w in (*gate, *up)],
        [((rows, units), F32), ((rows, units), F32), ((rows, units), BF16)],
        [block] * 3,
    )


def dense_backward(grad_out, gate_pre, up_pre, down, gate, up, table):
    units = gate_pre.shape[1]

    def compute(grad_ref, gate_pre_ref, up_pre_ref, *refs):
        count = len(down)
        down_refs, gate_refs, up_refs = (refs[i * count : (i + 1) * count] for i in range(3))
        gate_low_ref, up_low_ref = refs[3 * count :]
        grad = from_columns(grad_ref[...], down_refs).astype(BF16).astype(F32)
        act, slope = gelu_parts(gate_pre_ref[...])
        gate_low = (grad * up_pre_ref[...] * slope).astype(BF16)
        up_low = (grad * act).astype(BF16)
        gate_low_ref[...] = gate_low
        up_low_ref[...] = up_low
        return jnp.concatenate(
            [
                matmul_t(gate_low, by_rows(g)) + matmul_t(up_low, by_rows(u))
                for g, u in zip(gate_refs, up_refs)
            ],
            axis=1,
        )

    weights = [*down, *gate, *up]
    tiles = [grad_out, gate_pre, up_pre]
    return parts_by_rows(
        compute,
        table,
        grad_out.shape[1],
        tiles + weights,
        [tile_of(a, table) for a in tiles] + [resident(w) for w in weights],
        [((gate_pre.shape[0], units), BF16)] * 2,
        [tile_of(gate_pre, table)] * 2,
    )


def to_rows(values, weights, table):
    counts = [len(group) for group in values]
    blocks = len(weights[0])

    def compute(*refs):
        refs = list(refs)
        inputs = []
        for count in counts:
            group = [refs.pop(0)[...] for _ in range(count)]
            inputs.append(group[0] if count == 1 else jnp.concatenate(group, axis=1))
        outs = [0.0] * blocks
        for value in inputs:
            for j in range(blocks):
                outs[j] = outs[j] + matmul_t(value, by_rows(refs.pop(0)))
        return jnp.concatenate(outs, axis=1)

    flat = [value for group in values for value in group]
    every = [w for weight in weights for w in weight]
    model_width = sum(w.shape[0] * w.shape[1] for w in weights[0])
    return parts_by_rows(
        compute,
        table,
        model_width,
        flat + every,
        [tile_of(value, table) for value in flat] + [resident(w) for w in every],
        [],
        [],
    )


def grad_by_rows(left, rights, plan):
    rows, width = left.shape
    x, z = plan.along_x.size, plan.along_z.size
    block = width // (x * z)
    columns = [right.shape[1] for right in rights]
    away = (x - 1) * z

    def kernel(_, left_ref, *refs):
        step = pl.program_id(0)
        own_ref, other_ref = refs[-2:]
        start = 0
        value = []
        for right_ref in refs[:-2]:
            value.append(t_matmul(left_ref[...], right_ref[...]))
        value = value[0] if len(value) == 1 else jnp.concatenate(value, axis=1)

        @pl.when(step < away)
        def _():
            other_ref[0] = value.astype(BF16)

        @pl.when(step >= away)
        def _():
            own_ref[0] = value.astype(BF16)

    own, others = call(
        kernel,
        jnp.zeros((1,), jnp.int32),
        (x * z,),
        [left, *rights],
        [pl.BlockSpec((rows, block), lambda i, _: (0, lax.rem(i + z, x * z)))]
        + [resident(right) for right in rights],
        [((z, block, sum(columns)), BF16), ((away, block, sum(columns)), BF16)],
        [
            pl.BlockSpec((1, block, sum(columns)), lambda i, _: (jnp.maximum(i - away, 0), 0, 0)),
            pl.BlockSpec((1, block, sum(columns)), lambda i, _: (jnp.minimum(i, away - 1), 0, 0)),
        ],
    )
    return own, [others[j * z : (j + 1) * z] for j in range(x - 1)]


def grad_by_columns(left, right, plan):
    rows, units = left.shape
    x, z = plan.along_x.size, plan.along_z.size
    block = right.shape[1] // (x * z)
    tile = min(units, 256)

    def kernel(_, left_ref, right_ref, own_ref, other_ref):
        value = t_matmul(left_ref[...], right_ref[...])
        for i in range(x * z):
            part = value[:, i * block : (i + 1) * block]
            if i < z:
                own_ref[i] = part.astype(BF16)
            else:
                other_ref[i - z] = part.astype(BF16)

    own, others = call(
        kernel,
        jnp.zeros((1,), jnp.int32),
        (units // tile,),
        [left, right],
        [pl.BlockSpec((rows, tile), lambda i, _: (0, i)), resident(right)],
        [((z, units, block), BF16), (((x - 1) * z, units, block), BF16)],
        [
            pl.BlockSpec((z, tile, block), lambda i, _: (0, i, 0)),
            pl.BlockSpec(((x - 1) * z, tile, block), lambda i, _: (0, i, 0)),
        ],
    )
    return own, [others[j * z : (j + 1) * z] for j in range(x - 1)]


def gelu_parts(values):
    root = 0.7978845608028654
    inner = jnp.tanh(root * (values + 0.044715 * (values * values * values)))
    half = 0.5 * (1.0 + inner)
    slope = half + 0.5 * values * (1.0 - inner * inner) * root * (
        1.0 + 3 * 0.044715 * (values * values)
    )
    return values * half, slope


class Heads:
    def __init__(self, logs, seqs, rows):
        self.logs, self.seqs, self.rows = logs, seqs, rows
        self.heads = logs.shape[0]

    def flat(self, array, width, first):
        return array, pl.BlockSpec((self.rows, width), lambda b, h, _: (b, first + h))

    def whole(self, array):
        return array, pl.BlockSpec((self.rows, array.shape[1]), lambda b, h, _: (b, 0))

    def rows_of(self, weight):
        count, _, width = weight.shape
        return weight, pl.BlockSpec((count, VD, width), lambda b, h, _: (0, h, 0))

    def state(self, array):
        return array, pl.BlockSpec((1, 1, QK, VD), lambda b, h, _: (b, h, 0, 0))

    def call(self, kernel, inputs, outs):
        shapes, specs = [], []
        for width, kind in outs:
            if width is None:
                shapes.append(((self.seqs, self.heads, QK, VD), kind))
                specs.append(self.state(None)[1])
            else:
                shapes.append(((self.seqs * self.rows, self.heads * width), kind))
                specs.append(self.flat(None, width, 0)[1])
        return call(
            kernel,
            self.logs,
            (self.seqs, self.heads),
            [array for array, _ in inputs],
            [spec for _, spec in inputs],
            shapes,
            specs,
        )


def matmul(left, right):
    return jnp.dot(left, right, preferred_element_type=F32)


def matmul_t(left, right):
    return lax.dot_general(left, right, (((1,), (1,)), ((), ())), preferred_element_type=F32)


def t_matmul(left, right):
    return lax.dot_general(left, right, (((0,), (0,)), ((), ())), preferred_element_type=F32)


class Live:
    def fence(self):
        names = list(vars(self))
        values = lax.optimization_barrier([getattr(self, name) for name in names])
        for name, value in zip(names, values):
            setattr(self, name, value)


def added(blocks):
    return jnp.sum(blocks.astype(F32), axis=0)


def on_device(
    plan,
    tokens,
    pre_gain,
    query_weight,
    key_weight,
    value_weight,
    swish_weight,
    output_weight,
    mid_gain,
    gate_weight,
    up_weight,
    down_weight,
    cotangent,
):
    seq_count, seg_rows, model_width = tokens.shape
    row_count = seq_count * seg_rows
    to_slots, to_owners, table = plan.slot_owner(), plan.owner_slot(), plan.row_tiles()
    e = Live()
    e.tokens = tokens.reshape(row_count, model_width)
    e.cotangent = cotangent.reshape(row_count, model_width)
    key_width = query_weight.shape[1]
    local_heads = key_width // QK
    copies, blocks_x = plan.copies, plan.along_x.size
    along_z, along_core, along_y = plan.along_z, plan.along_core, plan.along_y
    head_index = (lax.axis_index("shard") * local_heads + jnp.arange(local_heads)).astype(F32)
    logs = jnp.log1p(-jnp.exp2(-5.0 - head_index))
    carry_scale = jnp.exp(seg_rows * logs)
    each = Heads(logs, seq_count, seg_rows)

    e.value = along_z.exchange(copies(value_weight))
    e.gains = plan.gains_x(jnp.stack([pre_gain, mid_gain]).astype(BF16))
    e.query_key = copies(jnp.concatenate([query_weight, key_weight], axis=1))
    e.grad_out = turn(e.cotangent, to_slots)
    del e.cotangent
    e.own_tokens = turn(plan.own_rows(e.tokens), to_slots)
    e.fence()
    e.value = plan.gather_x(e.value)
    e.query_key = along_z.exchange(e.query_key)
    e.own_grad_out = plan.own_rows(e.grad_out)
    gains = plan.gains_z(e.gains).astype(F32)
    e.full_pre, e.full_mid = gains[0], gains[1]
    del e.gains
    e.swish = copies(swish_weight)
    e.fence()
    e.query_key = plan.gather_x(e.query_key)
    e.swish = along_z.exchange(e.swish)
    e.output = copies(output_weight)
    e.mixer_in = norm_turn(e.tokens, e.full_pre, to_slots)
    del e.tokens
    e.values = project(e.mixer_in, e.value, BF16)
    e.fence()
    e.swish = plan.gather_x(e.swish)
    e.output = along_z.exchange(e.output)
    e.queries_keys = project(e.mixer_in, e.query_key, BF16)
    (state,) = each.call(
        state_kernel,
        [each.flat(e.queries_keys, QK, local_heads), each.flat(e.values, VD, 0)],
        [(None, F32)],
    )
    e.state = plan.scan_begin(state)
    e.fence()
    e.output = plan.gather_x(e.output)
    e.state = plan.scan_middle(e.state, carry_scale, False)
    e.swish_pre = project(e.mixer_in, e.swish, F32)
    e.gate = copies(gate_weight)
    e.fence()
    e.gate = along_z.exchange(e.gate)
    e.state = plan.scan_end(e.state)
    e.gated, e.mixed = each.call(
        mix_kernel,
        [
            each.flat(e.queries_keys, QK, 0),
            each.flat(e.queries_keys, QK, local_heads),
            each.flat(e.values, VD, 0),
            each.state(e.state),
            each.flat(e.swish_pre, VD, 0),
        ],
        [(VD, BF16), (VD, F32)],
    )
    e.part = plan.sum_cores(*to_columns(e.gated, e.output, table))
    e.up = copies(up_weight)
    e.fence()
    e.gate = plan.gather_x(e.gate)
    e.up = along_z.exchange(e.up)
    mine, pieces = e.part
    e.hidden_state, e.dense_own = enter_dense(
        mine, plan.sum_y(pieces), e.own_tokens, e.full_mid
    )
    del e.part
    e.down = copies(down_weight)
    e.fence()
    e.up = plan.gather_x(e.up)
    e.down = along_z.exchange(e.down)
    e.dense_in = plan.share_cores(plan.share_y(e.dense_own), BF16)
    del e.dense_own
    e.fence()
    e.down = plan.gather_x(e.down)
    e.gate_pre, e.up_pre, e.inner_act = dense_forward(e.dense_in, e.gate, e.up)
    e.down_own, e.down_others = grad_by_columns(e.inner_act, e.grad_out, plan)
    e.fence()
    e.down_others = plan.scatter_x(e.down_others)
    gate_low, e.up_low, e.part_others, e.part_own = dense_backward(
        e.grad_out, e.gate_pre, e.up_pre, e.down, e.gate, e.up, table
    )
    del e.gate_pre, e.up_pre, e.gate, e.up, e.grad_out
    e.gate_own, e.gate_others = grad_by_rows(e.dense_in, [gate_low], plan)
    e.out_others, e.out_own = to_columns(e.inner_act, e.down, table)
    del e.inner_act, e.down
    e.fence()
    e.down_sum = plan.scatter_z(e.down_own, e.down_others)
    del e.down_own, e.down_others
    e.gate_others = plan.scatter_x(e.gate_others)
    mine, pieces = plan.sum_cores(e.part_others, e.part_own)
    del e.part_others, e.part_own
    e.mid_part, e.branch_own, e.hidden_grad = norm_backward(
        mine, plan.sum_y(pieces), e.hidden_state, e.full_mid, e.own_grad_out, True
    )
    e.up_own, e.up_others = grad_by_rows(e.dense_in, [e.up_low], plan)
    del e.dense_in, e.up_low, e.own_grad_out
    e.fence()
    e.gate_sum = plan.scatter_z(e.gate_own, e.gate_others)
    del e.gate_own, e.gate_others
    e.up_others = plan.scatter_x(e.up_others)
    branch_low = plan.share_cores(plan.share_y(e.branch_own), BF16)
    del e.branch_own
    e.swish_low, e.mixed_low, state_grad = each.call(
        gate_kernel,
        [
            each.whole(branch_low),
            *[each.rows_of(weight) for weight in e.output],
            each.flat(e.swish_pre, VD, 0),
            each.flat(e.mixed, VD, 0),
            each.flat(e.queries_keys, QK, 0),
        ],
        [(VD, BF16), (VD, BF16), (None, F32)],
    )
    e.state_grad = plan.scan_begin(state_grad)
    e.output_own, e.output_others = grad_by_columns(e.gated, branch_low, plan)
    del e.swish_pre, e.mixed, e.output, e.gated
    e.fence()
    e.output_others = plan.scatter_x(e.output_others)
    e.state_grad = plan.scan_middle(e.state_grad, carry_scale, True)
    e.swish_own, e.swish_others = grad_by_rows(e.mixer_in, [e.swish_low], plan)
    e.down_sum = added(e.down_sum)
    e.fence()
    up_sum = plan.scatter_z(e.up_own, e.up_others)
    del e.up_own, e.up_others
    e.state_grad = plan.scan_end(e.state_grad)
    e.fence()
    e.up_sum = up_sum
    e.swish_others = plan.scatter_x(e.swish_others)
    e.query_low, e.key_low, e.value_low = each.call(
        mix_back_kernel,
        [
            each.flat(e.queries_keys, QK, 0),
            each.flat(e.queries_keys, QK, local_heads),
            each.flat(e.values, VD, 0),
            each.flat(e.mixed_low, VD, 0),
            each.state(e.state),
            each.state(e.state_grad),
        ],
        [(QK, BF16), (QK, BF16), (VD, BF16)],
    )
    del e.state, e.state_grad, e.mixed_low, e.queries_keys, e.values
    e.value_own, e.value_others = grad_by_rows(e.mixer_in, [e.value_low], plan)
    mine, pieces = plan.sum_cores(e.out_others, e.out_own)
    del e.out_others, e.out_own
    e.layer_own = leave_dense(mine, plan.sum_y(pieces), e.hidden_state)
    del e.hidden_state
    e.gate_sum = added(e.gate_sum)
    e.fence()
    output_sum = plan.scatter_z(e.output_own, e.output_others)
    del e.output_own, e.output_others
    value_others = plan.scatter_x(e.value_others)
    del e.value_others
    e.layer_tiles = plan.share_y(e.layer_own)
    del e.layer_own
    e.query_key_own, e.query_key_others = grad_by_rows(
        e.mixer_in, [e.query_low, e.key_low], plan
    )
    del e.mixer_in
    e.up_sum = added(e.up_sum)
    e.fence()
    e.layer_out = plan.share_cores(e.layer_tiles, BF16, to_owners)
    del e.layer_tiles
    e.part_others, e.part_own = to_rows(
        [[e.query_low, e.key_low], [e.value_low], [e.swish_low]],
        [e.query_key, e.value, e.swish],
        table,
    )
    del e.query_low, e.key_low, e.value_low, e.swish_low, e.query_key, e.value, e.swish
    e.output_sum, e.value_others = output_sum, value_others
    e.fence()
    e.swish_sum = plan.scatter_z(e.swish_own, e.swish_others)
    del e.swish_own, e.swish_others
    e.query_key_others = plan.scatter_x(e.query_key_others)
    mine, pieces = plan.sum_cores(e.part_others, e.part_own)
    del e.part_others, e.part_own
    e.pre_part, e.tokens_own = norm_backward(
        mine, plan.sum_y(pieces), e.own_tokens, e.full_pre, e.hidden_grad, False
    )
    del e.own_tokens, e.hidden_grad
    e.output_sum = added(e.output_sum)
    e.fence()
    e.value_sum = plan.scatter_z(e.value_own, e.value_others)
    del e.value_own, e.value_others
    e.tokens_grad = plan.share_cores(plan.share_y(e.tokens_own), F32, to_owners)
    del e.tokens_own
    vectors = jnp.stack([e.mid_part, e.pre_part]).reshape(2, blocks_x, -1)
    vectors = along_y.total(along_core.total(vectors))
    e.vectors = plan.sum_vectors(vectors)
    del e.mid_part, e.pre_part
    e.swish_sum = added(e.swish_sum)
    e.fence()
    last = added(plan.scatter_z(e.query_key_own, e.query_key_others, e.vectors))
    slice_width = pre_gain.shape[0]
    query_key_grad = last[:slice_width]
    mid_grad, pre_grad = (last[slice_width + i, :slice_width] for i in range(2))
    return (
        e.layer_out.reshape(tokens.shape),
        e.tokens_grad.reshape(tokens.shape),
        pre_grad,
        query_key_grad[:, :key_width],
        query_key_grad[:, key_width:],
        added(e.value_sum),
        e.swish_sum,
        e.output_sum,
        mid_grad,
        e.gate_sum,
        e.up_sum,
        e.down_sum,
    )


def solution(mesh):
    rows, weight, turned, vector = (
        P(None, "seq", None),
        P("seq", "shard"),
        P("shard", "seq"),
        P("seq"),
    )
    return jax.shard_map(
        functools.partial(on_device, Plan(mesh)),
        mesh=mesh,
        in_specs=(
            rows,
            vector,
            weight,
            weight,
            weight,
            weight,
            turned,
            vector,
            weight,
            weight,
            turned,
            rows,
        ),
        out_specs=(
            rows,
            rows,
            vector,
            weight,
            weight,
            weight,
            weight,
            turned,
            vector,
            weight,
            weight,
            turned,
        ),
        check_vma=False,
    )
```

```python
import functools

import jax
import jax.numpy as jnp
from jax import lax
from jax.experimental import pallas as pl
from jax.experimental.pallas import tpu as pltpu
from jax.sharding import PartitionSpec as P

QK = 256
VD = 512
CHIPS_Z = 4
CORES = 2
F32 = jnp.float32
BF16 = jnp.bfloat16
VMEM_LIMIT = 52 * 1024 * 1024


class Line:
    def __init__(self, axis, total, size, stride):
        self.axis, self.size, self.stride = axis, size, stride
        self.starts = [i for i in range(total) if (i // stride) % size == 0]

    def here(self):
        return lax.rem(lax.div(lax.axis_index(self.axis), self.stride), self.size)

    def send(self, value, moves):
        pairs = [(o + i * self.stride, o + j * self.stride) for i, j in moves for o in self.starts]
        return lax.ppermute(value, self.axis, pairs)

    def ring(self, value, distance):
        return self.send(value, [(i, (i + distance) % self.size) for i in range(self.size)])

    def exchange(self, blocks):
        groups = [[o + i * self.stride for i in range(self.size)] for o in self.starts]
        return lax.all_to_all(
            blocks, self.axis, split_axis=0, concat_axis=0, axis_index_groups=groups, tiled=True
        )

    def total(self, value):
        every = [value] + [self.ring(value, d) for d in range(1, self.size)]
        if self.size == 2:
            return every[0] + every[1]
        out = 0.0
        for position in range(self.size):
            out = out + self.pick(every, position)
        return out

    def pick(self, every, position):
        out = every[0]
        for d in range(1, self.size):
            source = lax.rem(self.here() - d + self.size, self.size)
            out = jnp.where(source == position, every[d], out)
        return out


class Plan:
    def __init__(self, mesh):
        seq, shard = mesh.shape["seq"], mesh.shape["shard"]
        self.seq, self.shard = seq, shard
        self.along_x = Line("seq", seq, seq // CHIPS_Z, 1)
        self.along_z = Line("seq", seq, CHIPS_Z, seq // CHIPS_Z)
        self.along_core = Line("shard", shard, CORES, 1)
        self.along_y = Line("shard", shard, shard // CORES, CORES)

    def slot_owner(self):
        x, z = self.along_x, self.along_z
        return jnp.stack(
            [
                k * x.size + lax.rem(x.here() + j, x.size)
                for j in range(x.size)
                for k in range(z.size)
            ]
        ).astype(jnp.int32)

    def owner_slot(self):
        x, z = self.along_x, self.along_z
        return jnp.stack(
            [
                lax.rem(x.size + j - x.here(), x.size) * z.size + k
                for k in range(z.size)
                for j in range(x.size)
            ]
        ).astype(jnp.int32)

    def row_tiles(self):
        core, y = self.along_core, self.along_y
        return jnp.stack(
            [
                lax.rem(core.here() + j, core.size) * y.size + lax.rem(y.here() + k, y.size)
                for j in (*range(1, core.size), 0)
                for k in range(y.size)
            ]
        ).astype(jnp.int32)

    def own_rows(self, whole):
        core, y = self.along_core, self.along_y
        step = whole.shape[0] // self.shard
        return lax.dynamic_slice_in_dim(whole, (core.here() * y.size + y.here()) * step, step, 0)

    def copies(self, own):
        def kernel(_, in_ref, out_ref):
            out_ref[0] = in_ref[...]

        return call(
            kernel,
            jnp.zeros((1,), jnp.int32),
            (self.along_z.size,),
            [own],
            [resident(own)],
            [((self.along_z.size, *own.shape), own.dtype)],
            [pl.BlockSpec((1, *own.shape), lambda i, _: (i, 0, 0))],
        )[0]

    def gather_x(self, row):
        return [row] + [self.along_x.ring(row, -j) for j in range(1, self.along_x.size)]

    def scatter_x(self, others):
        return [self.along_x.ring(part, j) for j, part in enumerate(others, 1)]

    def sum_cores(self, others):
        core = self.along_core
        return [core.ring(piece, d) for d in range(1, core.size) for piece in others]

    def sum_y(self, pieces):
        y = self.along_y
        return [y.ring(piece, k) for k, group in enumerate(pieces, 1) for piece in group]

    def share_y(self, pieces):
        y = self.along_y
        return [pieces] + [[y.ring(piece, -k) for piece in pieces] for k in range(1, y.size)]

    def share_cores(self, tiles, kind, columns=None):
        core, y = self.along_core, self.along_y
        others = [[core.ring(piece, 1) for piece in pieces] for pieces in tiles]
        here = jnp.stack([core.here(), y.here()]).astype(jnp.int32)
        if columns is None:
            columns = jnp.zeros((1,), jnp.int32)
        return place_tiles(jnp.concatenate([here, columns]), tiles, others, kind)

    def scan_begin(self, own):
        x = self.along_x
        step = own.shape[2] // x.size

        def part_for(distance):
            index = lax.rem(x.here() + distance, x.size) * step
            return lax.dynamic_slice_in_dim(own, index, step, 2)

        return [part_for(0)] + [
            x.ring(part_for(d).astype(BF16), d).astype(F32) for d in range(1, x.size)
        ]

    def order(self, device, later):
        return self.along_x.size - 1 - device if later else device

    def scan_sums(self, pieces, decay, later):
        x = self.along_x
        decay = decay[None, :, None, None]
        out = []
        for b in range(pieces[0].shape[0]):
            parts = [piece[b : b + 1] for piece in pieces]
            ordered = [x.pick(parts, self.order(i, later)) for i in range(x.size)]
            row_sum = ordered[0]
            for piece in ordered[1:]:
                row_sum = row_sum * decay + piece
            out.append((ordered[:-1], row_sum, row_sum.astype(BF16)))
        return out

    def scan_middle(self, sums, decay, later):
        x, z = self.along_x, self.along_z
        decay = decay[None, :, None, None]
        row_decay = decay**x.size
        pairs = [[(i, i + d) for i in range(z.size - d)] for d in (1, 2)]
        if later:
            pairs = [[(j, i) for i, j in moves] for moves in pairs]
        near = [z.send(low, pairs[0]).astype(F32) for _, _, low in sums]
        pair = [row_sum + row_decay * part for (_, row_sum, _), part in zip(sums, near)]
        far = [z.send(value.astype(BF16), pairs[1]).astype(F32) for value in pair]
        out = []
        for (ordered, _, _), near_part, far_part in zip(sums, near, far):
            entering = [near_part + row_decay * far_part]
            for piece in ordered:
                entering.append(entering[-1] * decay + piece)

            def for_device(distance):
                target = self.order(lax.rem(x.here() + distance, x.size), later)
                value = entering[0]
                for i in range(1, x.size):
                    value = jnp.where(target == i, entering[i], value)
                return value

            out.append(
                [for_device(0)] + [for_device(d).astype(BF16) for d in range(1, x.size)]
            )
        return out

    def scan_end(self, shares):
        x = self.along_x
        out = []
        for own, *others in shares:
            back = [own] + [x.ring(part, d).astype(F32) for d, part in enumerate(others, 1)]
            out.append(jnp.concatenate([x.pick(back, i) for i in range(x.size)], axis=2))
        return jnp.concatenate(out, axis=0)

    def gains_x(self, gains):
        x, z = self.along_x, self.along_z
        slots = jnp.zeros((2, z.size, x.size, gains.shape[1]), gains.dtype)
        slots = lax.dynamic_update_slice(slots, gains[:, None, None], (0, z.here(), x.here(), 0))
        return x.total(slots.reshape(2, z.size, -1))

    def gains_z(self, slots):
        x, z = self.along_x, self.along_z
        slots = z.total(slots).reshape(2, z.size, x.size, -1)
        turned = [
            lax.dynamic_slice_in_dim(slots, lax.rem(x.here() + j, x.size), 1, 2)[:, :, 0]
            for j in range(x.size)
        ]
        return jnp.concatenate(turned, axis=1).reshape(2, -1)

    def sum_vectors(self, vectors):
        mine = vectors[:, 0]
        for part in self.scatter_x([vectors[:, j] for j in range(1, self.along_x.size)]):
            mine = mine + part
        return mine.reshape(mine.shape[0], self.along_z.size, -1).transpose(1, 0, 2)


CHEAP = pl.CostEstimate(flops=0, bytes_accessed=0, transcendentals=0)


def resident(array):
    return pl.BlockSpec(
        array.shape, lambda *_: (0,) * array.ndim, pipeline_mode=pl.Buffered(1)
    )


def call(kernel, table, grid, arrays, specs, outs, out_specs):
    return pl.pallas_call(
        kernel,
        grid_spec=pltpu.PrefetchScalarGridSpec(
            num_scalar_prefetch=1, grid=grid, in_specs=specs, out_specs=out_specs
        ),
        out_shape=[jax.ShapeDtypeStruct(*out) for out in outs],
        compiler_params=pltpu.CompilerParams(vmem_limit_bytes=VMEM_LIMIT),
        cost_estimate=CHEAP,
    )(table, *arrays)


def turn_kernel(table, in_ref, out_ref):
    width = in_ref.shape[1] // table.shape[0]
    for i in range(table.shape[0]):
        start = pl.multiple_of(table[i] * width, width)
        out_ref[:, i * width : (i + 1) * width] = in_ref[:, pl.ds(start, width)]


def turn(value, table):
    rows, width = value.shape
    tile = min(rows, 256)
    return pl.pallas_call(
        turn_kernel,
        grid_spec=pltpu.PrefetchScalarGridSpec(
            num_scalar_prefetch=1,
            grid=(rows // tile,),
            in_specs=[pl.BlockSpec((tile, width), lambda i, t: (i, 0))],
            out_specs=pl.BlockSpec((tile, width), lambda i, t: (i, 0)),
        ),
        out_shape=jax.ShapeDtypeStruct(value.shape, value.dtype),
        cost_estimate=CHEAP,
    )(table, value)


def norm_turn_kernel(table, in_ref, gain_ref, out_ref):
    width = in_ref.shape[1] // table.shape[0]
    values = in_ref[...].astype(F32)
    mean = jnp.mean(values, axis=-1, keepdims=True)
    centred = values - mean
    scale = lax.rsqrt(jnp.mean(centred * centred, axis=-1, keepdims=True) + 1e-05)
    for i in range(table.shape[0]):
        start = pl.multiple_of(table[i] * width, width)
        block = in_ref[:, pl.ds(start, width)].astype(F32)
        gain = gain_ref[:, i * width : (i + 1) * width]
        out_ref[:, i * width : (i + 1) * width] = ((block - mean) * scale * gain).astype(BF16)


def norm_turn(value, gain, table):
    rows, width = value.shape
    tile = min(rows, 256)
    return pl.pallas_call(
        norm_turn_kernel,
        grid_spec=pltpu.PrefetchScalarGridSpec(
            num_scalar_prefetch=1,
            grid=(rows // tile,),
            in_specs=[
                pl.BlockSpec((tile, width), lambda i, t: (i, 0)),
                pl.BlockSpec((1, width), lambda i, t: (0, 0)),
            ],
            out_specs=pl.BlockSpec((tile, width), lambda i, t: (i, 0)),
        ),
        out_shape=jax.ShapeDtypeStruct(value.shape, BF16),
        cost_estimate=CHEAP,
    )(table, value, gain.reshape(1, -1))


def silu_parts(values):
    sigmoid = 1.0 / (1.0 + jnp.exp(-values))
    return sigmoid, values * sigmoid


def norm_parts(values):
    centred = values - jnp.mean(values, axis=-1, keepdims=True)
    scale = lax.rsqrt(jnp.mean(centred * centred, axis=-1, keepdims=True) + 1e-05)
    return centred * scale, scale


def halves(values):
    high = values.astype(BF16)
    return high, (values - high.astype(F32)).astype(BF16)


def row_decay(log, rows, first, step):
    position = lax.broadcasted_iota(jnp.int32, (rows, 1), 0)
    return jnp.exp((first + step * position).astype(F32) * log)


def pair_decay(log, rows):
    row = lax.broadcasted_iota(jnp.int32, (rows, rows), 0)
    column = lax.broadcasted_iota(jnp.int32, (rows, rows), 1)
    offset = row - column
    return jnp.where(offset >= 0, jnp.exp(jnp.maximum(offset, 0).astype(F32) * log), 0.0)


def state_kernel(logs, key_ref, value_ref, state_ref):
    rows = key_ref.shape[0]
    scaled = key_ref[...].astype(F32) * row_decay(logs[pl.program_id(1)], rows, rows - 1, -1)
    high, low = halves(scaled)
    value = value_ref[...]
    state_ref[0, 0] = t_matmul(high, value) + t_matmul(low, value)


def mix_kernel(logs, query_ref, key_ref, value_ref, state_ref, swish_ref, gated_ref, mixed_ref):
    rows = key_ref.shape[0]
    log = logs[pl.program_id(1)]
    query = query_ref[...]
    weights = (matmul_t(query, key_ref[...]) * pair_decay(log, rows)).astype(BF16)
    high, low = halves(state_ref[0, 0])
    cross = matmul(query, high) + matmul(query, low)
    mixed = matmul(weights, value_ref[...]) + cross * row_decay(log, rows, 1, 1)
    mixed_ref[...] = mixed
    gated_ref[...] = (silu_parts(swish_ref[...])[1] * norm_parts(mixed)[0]).astype(BF16)


def gate_kernel(logs, *refs):
    (branch_ref, *output_refs), (swish_ref, mixed_ref, query_ref) = refs[:-6], refs[-6:-3]
    swish_low_ref, mixed_low_ref, state_ref = refs[-3:]
    rows = query_ref.shape[0]
    swish_pre = swish_ref[...]
    grad = from_columns(branch_ref[...], output_refs)
    normalized, scale = norm_parts(mixed_ref[...])
    sigmoid, silu = silu_parts(swish_pre)
    slope = sigmoid * (1.0 + swish_pre * (1.0 - sigmoid))
    swish_low_ref[...] = (grad * normalized * slope).astype(BF16)
    e = grad * silu
    mean = jnp.mean(e, axis=-1, keepdims=True)
    along = jnp.mean(e * normalized, axis=-1, keepdims=True)
    mixed_low = (scale * (e - mean - normalized * along)).astype(BF16)
    mixed_low_ref[...] = mixed_low
    scaled = query_ref[...].astype(F32) * row_decay(logs[pl.program_id(1)], rows, 1, 1)
    high, low = halves(scaled)
    state_ref[0, 0] = t_matmul(high, mixed_low) + t_matmul(low, mixed_low)


def mix_back_kernel(
    logs,
    query_ref,
    key_ref,
    value_ref,
    mixed_low_ref,
    state_ref,
    state_grad_ref,
    query_low_ref,
    key_low_ref,
    value_low_ref,
):
    rows = key_ref.shape[0]
    log = logs[pl.program_id(1)]
    query, key, value, mixed_low = (
        query_ref[...],
        key_ref[...],
        value_ref[...],
        mixed_low_ref[...],
    )
    decay = pair_decay(log, rows)
    weights = (matmul_t(query, key) * decay).astype(BF16)
    score = (matmul_t(mixed_low, value) * decay).astype(BF16)
    high, low = halves(state_ref[0, 0])
    cross = matmul_t(mixed_low, high) + matmul_t(mixed_low, low)
    query_low_ref[...] = (matmul(score, key) + cross * row_decay(log, rows, 1, 1)).astype(BF16)
    high, low = halves(state_grad_ref[0, 0])
    to_end = row_decay(log, rows, rows - 1, -1)
    cross = matmul_t(value, high) + matmul_t(value, low)
    key_low_ref[...] = (t_matmul(score, query) + cross * to_end).astype(BF16)
    cross = matmul(key, high) + matmul(key, low)
    value_low_ref[...] = (t_matmul(weights, mixed_low) + cross * to_end).astype(BF16)


def at_once(kernel, arrays, outs, table=None):
    if table is None:
        table = jnp.zeros((1,), jnp.int32)
    return call(
        kernel,
        table,
        (1,),
        arrays,
        [resident(array) for array in arrays],
        outs,
        [pl.BlockSpec(shape, lambda i, _, n=len(shape): (0,) * n) for shape, _ in outs],
    )


def add_blocks(own, arrived, extra=None):
    count, rows, columns = own.shape
    more = () if extra is None else (extra,)
    below = 0 if extra is None else 16
    arrays, specs = [own], [pl.BlockSpec((1, rows, columns), lambda i, _: (i, 0, 0))]
    for parts in arrived:
        start = 0
        for part in parts if isinstance(parts, list) else [parts]:
            size = part.shape[0]
            arrays.append(part)
            specs.append(
                pl.BlockSpec(
                    (1, rows, columns),
                    lambda i, _, start=start, size=size: (jnp.clip(i - start, 0, size - 1), 0, 0),
                )
            )
            start += size
    sizes = [array.shape[0] for array in arrays[1:]]

    def kernel(_, *refs):
        step = pl.program_id(0)
        out = refs[0][...].astype(F32)
        start = 0
        for ref, size in zip(refs[1 : len(arrays)], sizes):
            part = ref[...].astype(F32)
            if size < count:
                part = jnp.where((step >= start) & (step < start + size), part, 0.0)
                start = (start + size) % count
            out = out + part
        refs[-1][:, :rows, :] = out.astype(BF16)
        if more:
            refs[-1][:, rows:, :] = refs[-2][...]

    if more:
        extra = jnp.pad(
            extra.astype(BF16),
            ((0, 0), (0, below - extra.shape[1]), (0, columns - extra.shape[2])),
        )
        more = (extra,)
    return call(
        kernel,
        jnp.zeros((1,), jnp.int32),
        (count,),
        [*arrays, *more],
        specs + [pl.BlockSpec((1, below, columns), lambda i, _: (i, 0, 0)) for _ in more],
        [((count, rows + below, columns), BF16)],
        [pl.BlockSpec((1, rows + below, columns), lambda i, _: (i, 0, 0))],
    )[0]


def fold_tiles(own, arrived, tiles):
    rows, width = own.shape
    tile = rows // tiles
    piece = tile // 2

    def kernel(_, own_ref, *refs):
        outs = refs[len(arrived) :]
        for i in range(2 * tiles):
            value = own_ref[i * piece : (i + 1) * piece, :]
            for ref in refs[i : len(arrived) : 2 * tiles]:
                value = value + ref[...].astype(F32)
            if i < 2:
                outs[0][i * piece : (i + 1) * piece, :] = value
            else:
                outs[i - 1][...] = value.astype(BF16)

    mine, *pieces = at_once(
        kernel,
        [own, *arrived],
        [((tile, width), F32)] + [((piece, width), BF16)] * (2 * tiles - 2),
    )
    return mine, [pieces[2 * k : 2 * k + 2] for k in range(tiles - 1)]


def summed(mine_ref, refs, piece):
    rows = mine_ref.shape[0] // 2
    value = mine_ref[piece * rows : (piece + 1) * rows, :]
    for ref in refs[piece::2]:
        value = value + ref[...].astype(F32)
    return value


def enter_dense(mine, arrived, tokens, gain):
    rows, width = mine.shape
    half = rows // 2

    def kernel(_, mine_ref, tokens_ref, gain_ref, *refs):
        hidden_ref, *outs = refs[len(arrived) :]
        for i in range(2):
            part = slice(i * half, (i + 1) * half)
            hidden = tokens_ref[part, :].astype(F32) + summed(mine_ref, refs[: len(arrived)], i)
            hidden_ref[part, :] = hidden
            outs[i][...] = (norm_parts(hidden)[0] * gain_ref[...]).astype(BF16)

    hidden, *pieces = at_once(
        kernel,
        [mine, tokens, gain.reshape(1, -1), *arrived],
        [((rows, width), F32)] + [((half, width), BF16)] * 2,
    )
    return hidden, pieces


def leave_dense(mine, arrived, hidden):
    rows, width = mine.shape
    half = rows // 2

    def kernel(_, mine_ref, hidden_ref, *refs):
        for i in range(2):
            value = hidden_ref[i * half : (i + 1) * half, :] + summed(
                mine_ref, refs[: len(arrived)], i
            )
            refs[len(arrived) + i][...] = value.astype(BF16)

    return at_once(kernel, [mine, hidden, *arrived], [((half, width), BF16)] * 2)


def norm_backward(mine, arrived, values, gain, residual, keep):
    rows, width = mine.shape
    half = rows // 2

    def kernel(_, mine_ref, values_ref, gain_ref, residual_ref, *refs):
        gain_out, first, second, *whole = refs[len(arrived) :]
        gain_sum = 0.0
        for i in range(2):
            part = slice(i * half, (i + 1) * half)
            grad = summed(mine_ref, refs[: len(arrived)], i)
            normalized, scale = norm_parts(values_ref[part, :].astype(F32))
            gain_sum = gain_sum + jnp.sum(grad * normalized, axis=0, keepdims=True)
            e = grad * gain_ref[...]
            mean = jnp.mean(e, axis=-1, keepdims=True)
            along = jnp.mean(e * normalized, axis=-1, keepdims=True)
            out = residual_ref[part, :].astype(F32) + scale * (e - mean - normalized * along)
            (first, second)[i][...] = out.astype(BF16)
            for ref in whole:
                ref[part, :] = out
        gain_out[...] = gain_sum

    gain_part, first, second, *whole = at_once(
        kernel,
        [mine, values, gain.reshape(1, -1), residual, *arrived],
        [((1, width), F32)]
        + [((half, width), BF16)] * 2
        + [((rows, width), F32)] * (1 if keep else 0),
    )
    return gain_part, [first, second], *whole


def place_tiles(table, near, far, kind):
    tiles = len(near)
    pieces = [piece for tile in near + far for piece in tile]
    piece, width = pieces[0].shape
    columns = table.shape[0] - 2
    block = width // columns

    def kernel(table, *refs):
        out_ref = refs[-1]
        step = pl.program_id(0)
        for i in range(2 * tiles):
            core = lax.rem(table[0] + i // tiles, CORES)
            row = lax.rem(table[1] + i % tiles, tiles)

            @pl.when(step == core * tiles + row)
            def _(i=i):
                for part in range(2):
                    ref = refs[2 * i + part]
                    for j in range(columns):
                        start = pl.multiple_of(table[2 + j] * block, block)
                        out_ref[
                            part * piece : (part + 1) * piece, j * block : (j + 1) * block
                        ] = ref[:, pl.ds(start, block)].astype(kind)

    return call(
        kernel,
        table,
        (CORES * tiles,),
        pieces,
        [resident(ref) for ref in pieces],
        [((2 * CORES * tiles * piece, width), kind)],
        [pl.BlockSpec((2 * piece, width), lambda i, _: (i, 0))],
    )[0]


def by_rows(ref):
    return ref[...].reshape(-1, ref.shape[2])


def from_columns(values, refs):
    width = refs[0].shape[0] * refs[0].shape[2]
    out = 0.0
    for j, ref in enumerate(refs):
        weight = jnp.concatenate([ref[k] for k in range(ref.shape[0])], axis=1)
        out = out + matmul_t(values[:, j * width : (j + 1) * width], weight)
    return out


def project(values, weight, kind):
    rows, width = values.shape
    tile = min(rows, 256)
    columns = weight[0].shape[2]

    def kernel(_, in_ref, *refs):
        depth = width // len(weight)
        out = matmul(in_ref[:, :depth], by_rows(refs[0]))
        for j in range(1, len(weight)):
            out = out + matmul(in_ref[:, j * depth : (j + 1) * depth], by_rows(refs[j]))
        refs[-1][...] = out.astype(kind)

    return call(
        kernel,
        jnp.zeros((1,), jnp.int32),
        (rows // tile,),
        [values, *weight],
        [pl.BlockSpec((tile, width), lambda i, _: (i, 0))] + [resident(w) for w in weight],
        [((rows, columns), kind)],
        [pl.BlockSpec((tile, columns), lambda i, _: (i, 0))],
    )[0]


def parts_by_rows(compute, table, model_width, arrays, specs, outs, out_specs):
    count = table.shape[0]
    rows = arrays[0].shape[0]
    tile = rows // count
    away = count - count // CORES
    half = tile // 2

    def kernel(table, *refs):
        step = pl.program_id(0)
        pieces, own_ref = refs[-2 * away - 1 : -1], refs[-1]
        value = compute(*refs[: -2 * away - 1])
        for i in range(away):

            @pl.when(step == i)
            def _(i=i):
                pieces[2 * i][...] = value[:half].astype(BF16)
                pieces[2 * i + 1][...] = value[half:].astype(BF16)

        @pl.when(step >= away)
        def _():
            own_ref[...] = value

    *results, own = call(
        kernel,
        table,
        (count,),
        arrays,
        specs,
        outs + [((half, model_width), BF16)] * (2 * away) + [(((count - away) * tile, model_width), F32)],
        out_specs
        + [pl.BlockSpec((half, model_width), lambda i, t: (0, 0))] * (2 * away)
        + [pl.BlockSpec((tile, model_width), lambda i, t: (jnp.maximum(i - away, 0), 0))],
    )
    return *results[: len(outs)], results[len(outs) :], own


def tile_of(array, table):
    return pl.BlockSpec(
        (array.shape[0] // table.shape[0], array.shape[1]), lambda i, t: (t[i], 0)
    )


def to_columns(values, weight, table):
    count, _, width = weight[0].shape

    def compute(in_ref, *refs):
        value = in_ref[...]
        return jnp.concatenate(
            [matmul(value, ref[k]) for ref in refs for k in range(count)], axis=1
        )

    return parts_by_rows(
        compute,
        table,
        len(weight) * count * width,
        [values, *weight],
        [tile_of(values, table)] + [resident(w) for w in weight],
        [],
        [],
    )


def dense_forward(dense_in, gate, up):
    rows, width = dense_in.shape
    tile = min(rows, 256)
    units = gate[0].shape[2]

    def kernel(_, in_ref, *refs):
        gate_refs, up_refs = refs[: len(gate)], refs[len(gate) : -3]
        depth = width // len(gate)
        pre = []
        for weights in (gate_refs, up_refs):
            out = 0.0
            for j, ref in enumerate(weights):
                out = out + matmul(in_ref[:, j * depth : (j + 1) * depth], by_rows(ref))
            pre.append(out)
        refs[-3][...], refs[-2][...] = pre
        refs[-1][...] = (gelu_parts(pre[0])[0] * pre[1]).astype(BF16)

    block = pl.BlockSpec((tile, units), lambda i, _: (i, 0))
    return call(
        kernel,
        jnp.zeros((1,), jnp.int32),
        (rows // tile,),
        [dense_in, *gate, *up],
        [pl.BlockSpec((tile, width), lambda i, _: (i, 0))] + [resident(w) for w in (*gate, *up)],
        [((rows, units), F32), ((rows, units), F32), ((rows, units), BF16)],
        [block] * 3,
    )


def dense_backward(grad_out, gate_pre, up_pre, down, gate, up, table):
    units = gate_pre.shape[1]

    def compute(grad_ref, gate_pre_ref, up_pre_ref, *refs):
        count = len(down)
        down_refs, gate_refs, up_refs = (refs[i * count : (i + 1) * count] for i in range(3))
        gate_low_ref, up_low_ref = refs[3 * count :]
        grad = from_columns(grad_ref[...], down_refs).astype(BF16).astype(F32)
        act, slope = gelu_parts(gate_pre_ref[...])
        gate_low = (grad * up_pre_ref[...] * slope).astype(BF16)
        up_low = (grad * act).astype(BF16)
        gate_low_ref[...] = gate_low
        up_low_ref[...] = up_low
        return jnp.concatenate(
            [
                matmul_t(gate_low, by_rows(g)) + matmul_t(up_low, by_rows(u))
                for g, u in zip(gate_refs, up_refs)
            ],
            axis=1,
        )

    weights = [*down, *gate, *up]
    tiles = [grad_out, gate_pre, up_pre]
    return parts_by_rows(
        compute,
        table,
        grad_out.shape[1],
        tiles + weights,
        [tile_of(a, table) for a in tiles] + [resident(w) for w in weights],
        [((gate_pre.shape[0], units), BF16)] * 2,
        [tile_of(gate_pre, table)] * 2,
    )


def to_rows(values, weights, table):
    counts = [len(group) for group in values]
    blocks = len(weights[0])

    def compute(*refs):
        refs = list(refs)
        inputs = []
        for count in counts:
            group = [refs.pop(0)[...] for _ in range(count)]
            inputs.append(group[0] if count == 1 else jnp.concatenate(group, axis=1))
        outs = [0.0] * blocks
        for value in inputs:
            for j in range(blocks):
                outs[j] = outs[j] + matmul_t(value, by_rows(refs.pop(0)))
        return jnp.concatenate(outs, axis=1)

    flat = [value for group in values for value in group]
    every = [w for weight in weights for w in weight]
    model_width = sum(w.shape[0] * w.shape[1] for w in weights[0])
    return parts_by_rows(
        compute,
        table,
        model_width,
        flat + every,
        [tile_of(value, table) for value in flat] + [resident(w) for w in every],
        [],
        [],
    )


def grad_by_rows(left, rights, plan):
    rows, width = left.shape
    x, z = plan.along_x.size, plan.along_z.size
    block = width // (x * z)
    columns = [right.shape[1] for right in rights]
    away = (x - 1) * z

    def kernel(_, left_ref, *refs):
        step = pl.program_id(0)
        own_ref, other_ref = refs[-2:]
        start = 0
        value = []
        for right_ref in refs[:-2]:
            value.append(t_matmul(left_ref[...], right_ref[...]))
        value = value[0] if len(value) == 1 else jnp.concatenate(value, axis=1)

        @pl.when(step < away)
        def _():
            other_ref[0] = value.astype(BF16)

        @pl.when(step >= away)
        def _():
            own_ref[0] = value.astype(BF16)

    own, others = call(
        kernel,
        jnp.zeros((1,), jnp.int32),
        (x * z,),
        [left, *rights],
        [pl.BlockSpec((rows, block), lambda i, _: (0, lax.rem(i + z, x * z)))]
        + [resident(right) for right in rights],
        [((z, block, sum(columns)), BF16), ((away, block, sum(columns)), BF16)],
        [
            pl.BlockSpec((1, block, sum(columns)), lambda i, _: (jnp.maximum(i - away, 0), 0, 0)),
            pl.BlockSpec((1, block, sum(columns)), lambda i, _: (jnp.minimum(i, away - 1), 0, 0)),
        ],
    )
    return own, [others[j * z : (j + 1) * z] for j in range(x - 1)]


def grad_by_columns(left, right, plan):
    rows, units = left.shape
    x, z = plan.along_x.size, plan.along_z.size
    block = right.shape[1] // (x * z)
    tile = min(units, 256)

    def kernel(_, left_ref, right_ref, own_ref, other_ref):
        value = t_matmul(left_ref[...], right_ref[...])
        for i in range(x * z):
            part = value[:, i * block : (i + 1) * block]
            if i < z:
                own_ref[i] = part.astype(BF16)
            else:
                other_ref[i - z] = part.astype(BF16)

    own, others = call(
        kernel,
        jnp.zeros((1,), jnp.int32),
        (units // tile,),
        [left, right],
        [pl.BlockSpec((rows, tile), lambda i, _: (0, i)), resident(right)],
        [((z, units, block), BF16), (((x - 1) * z, units, block), BF16)],
        [
            pl.BlockSpec((z, tile, block), lambda i, _: (0, i, 0)),
            pl.BlockSpec(((x - 1) * z, tile, block), lambda i, _: (0, i, 0)),
        ],
    )
    return own, [others[j * z : (j + 1) * z] for j in range(x - 1)]


def gelu_parts(values):
    root = 0.7978845608028654
    inner = jnp.tanh(root * (values + 0.044715 * (values * values * values)))
    half = 0.5 * (1.0 + inner)
    slope = half + 0.5 * values * (1.0 - inner * inner) * root * (
        1.0 + 3 * 0.044715 * (values * values)
    )
    return values * half, slope


class Heads:
    def __init__(self, logs, seqs, rows):
        self.logs, self.seqs, self.rows = logs, seqs, rows
        self.heads = logs.shape[0]

    def flat(self, array, width, first):
        return array, pl.BlockSpec((self.rows, width), lambda b, h, _: (b, first + h))

    def whole(self, array):
        return array, pl.BlockSpec((self.rows, array.shape[1]), lambda b, h, _: (b, 0))

    def rows_of(self, weight):
        count, _, width = weight.shape
        return weight, pl.BlockSpec((count, VD, width), lambda b, h, _: (0, h, 0))

    def state(self, array):
        return array, pl.BlockSpec((1, 1, QK, VD), lambda b, h, _: (b, h, 0, 0))

    def call(self, kernel, inputs, outs):
        shapes, specs = [], []
        for width, kind in outs:
            if width is None:
                shapes.append(((self.seqs, self.heads, QK, VD), kind))
                specs.append(self.state(None)[1])
            else:
                shapes.append(((self.seqs * self.rows, self.heads * width), kind))
                specs.append(self.flat(None, width, 0)[1])
        return call(
            kernel,
            self.logs,
            (self.seqs, self.heads),
            [array for array, _ in inputs],
            [spec for _, spec in inputs],
            shapes,
            specs,
        )


def matmul(left, right):
    return jnp.dot(left, right, preferred_element_type=F32)


def matmul_t(left, right):
    return lax.dot_general(left, right, (((1,), (1,)), ((), ())), preferred_element_type=F32)


def t_matmul(left, right):
    return lax.dot_general(left, right, (((0,), (0,)), ((), ())), preferred_element_type=F32)


class Live:
    def fence(self):
        names = list(vars(self))
        values = lax.optimization_barrier([getattr(self, name) for name in names])
        for name, value in zip(names, values):
            setattr(self, name, value)


def added(blocks):
    count, rows, columns = blocks.shape
    parts = 2 if rows % 32 == 0 else 1

    def kernel(_, in_ref, out_ref):
        out = in_ref[0].astype(F32)
        for k in range(1, count):
            out = out + in_ref[k].astype(F32)
        out_ref[...] = out

    return call(
        kernel,
        jnp.zeros((1,), jnp.int32),
        (parts,),
        [blocks],
        [pl.BlockSpec((count, rows // parts, columns), lambda i, _: (0, i, 0))],
        [((rows, columns), F32)],
        [pl.BlockSpec((rows // parts, columns), lambda i, _: (i, 0))],
    )[0]


def on_device(
    plan,
    tokens,
    pre_gain,
    query_weight,
    key_weight,
    value_weight,
    swish_weight,
    output_weight,
    mid_gain,
    gate_weight,
    up_weight,
    down_weight,
    cotangent,
):
    seq_count, seg_rows, model_width = tokens.shape
    row_count = seq_count * seg_rows
    to_slots, to_owners, table = plan.slot_owner(), plan.owner_slot(), plan.row_tiles()
    e = Live()
    e.tokens = tokens.reshape(row_count, model_width)
    e.cotangent = cotangent.reshape(row_count, model_width)
    key_width = query_weight.shape[1]
    local_heads = key_width // QK
    copies, blocks_x = plan.copies, plan.along_x.size
    along_z, along_core, along_y = plan.along_z, plan.along_core, plan.along_y
    head_index = (lax.axis_index("shard") * local_heads + jnp.arange(local_heads)).astype(F32)
    logs = jnp.log1p(-jnp.exp2(-5.0 - head_index))
    carry_scale = jnp.exp(seg_rows * logs)
    each = Heads(logs, seq_count, seg_rows)

    e.value = along_z.exchange(copies(value_weight))
    e.gains = plan.gains_x(jnp.stack([pre_gain, mid_gain]).astype(BF16))
    e.query_key = copies(jnp.concatenate([query_weight, key_weight], axis=1))
    e.down = plan.gather_x(down_weight)
    e.grad_out = turn(e.cotangent, to_slots)
    del e.cotangent
    e.own_tokens = turn(plan.own_rows(e.tokens), to_slots)
    e.fence()
    e.value = plan.gather_x(e.value)
    e.query_key = along_z.exchange(e.query_key)
    e.own_grad_out = plan.own_rows(e.grad_out)
    gains = plan.gains_z(e.gains).astype(F32)
    e.full_pre, e.full_mid = gains[0], gains[1]
    del e.gains
    e.swish = copies(swish_weight)
    e.fence()
    e.query_key = plan.gather_x(e.query_key)
    e.swish = along_z.exchange(e.swish)
    e.output = copies(output_weight)
    e.mixer_in = norm_turn(e.tokens, e.full_pre, to_slots)
    del e.tokens
    e.values = project(e.mixer_in, e.value, BF16)
    e.fence()
    output_z = along_z.exchange(e.output)
    del e.output
    e.queries_keys = project(e.mixer_in, e.query_key, BF16)
    (state,) = each.call(
        state_kernel,
        [each.flat(e.queries_keys, QK, local_heads), each.flat(e.values, VD, 0)],
        [(None, F32)],
    )
    e.state = plan.scan_begin(state)
    e.fence()
    swish_x = plan.gather_x(e.swish)
    del e.swish
    e.output = output_z
    e.gate = copies(gate_weight)
    e.state = plan.scan_sums(e.state, carry_scale, False)
    e.fence()
    e.state = plan.scan_middle(e.state, carry_scale, False)
    e.swish = swish_x
    e.fence()
    gate_z = along_z.exchange(e.gate)
    del e.gate
    e.state = plan.scan_end(e.state)
    e.fence()
    output_x = plan.gather_x(e.output)
    del e.output
    e.gate = gate_z
    e.swish_pre = project(e.mixer_in, e.swish, F32)
    e.gated, e.mixed = each.call(
        mix_kernel,
        [
            each.flat(e.queries_keys, QK, 0),
            each.flat(e.queries_keys, QK, local_heads),
            each.flat(e.values, VD, 0),
            each.state(e.state),
            each.flat(e.swish_pre, VD, 0),
        ],
        [(VD, BF16), (VD, F32)],
    )
    e.up = copies(up_weight)
    e.fence()
    e.up = along_z.exchange(e.up)
    e.gate = plan.gather_x(e.gate)
    branch_others, branch_own = to_columns(e.gated, output_x, table)
    e.output = output_x
    mine, pieces = fold_tiles(branch_own, plan.sum_cores(branch_others), along_y.size)
    e.mine, e.arrived = mine, plan.sum_y(pieces)
    e.down = [copies(part) for part in e.down]
    e.fence()
    down_z = along_z.exchange(e.down[0])
    e.down = e.down[1:]
    up_x = plan.gather_x(e.up)
    del e.up
    e.hidden_state, dense_own = enter_dense(e.mine, e.arrived, e.own_tokens, e.full_mid)
    del e.mine, e.arrived
    e.dense_tiles = plan.share_y(dense_own)
    e.fence()
    e.dense_in = plan.share_cores(e.dense_tiles, BF16)
    del e.dense_tiles
    e.down_first, e.up = down_z, up_x
    e.fence()
    down_z = [along_z.exchange(part) for part in e.down]
    del e.down
    e.gate_pre, e.up_pre, e.inner_act = dense_forward(e.dense_in, e.gate, e.up)
    e.down_own, e.down_others = grad_by_columns(e.inner_act, e.grad_out, plan)
    e.fence()
    down_x = plan.scatter_x(e.down_others)
    del e.down_others
    e.down = [e.down_first, *down_z]
    del e.down_first
    e.fence()
    e.gate_low, e.up_low, e.part_others, e.part_own = dense_backward(
        e.grad_out, e.gate_pre, e.up_pre, e.down, e.gate, e.up, table
    )
    del e.gate_pre, e.up_pre, e.gate, e.up, e.grad_out
    e.fence()
    e.part_others = plan.sum_cores(e.part_others)
    e.down_sum = add_blocks(e.down_own, down_x)
    del e.down_own
    e.fence()
    down_z = along_z.exchange(e.down_sum)
    del e.down_sum
    e.gate_own, e.gate_others = grad_by_rows(e.dense_in, [e.gate_low], plan)
    del e.gate_low
    mine, pieces = fold_tiles(e.part_own, e.part_others, along_y.size)
    e.mine, e.arrived = mine, plan.sum_y(pieces)
    del e.part_own, e.part_others
    gate_x = plan.scatter_x(e.gate_others)
    del e.gate_others
    e.up_own, e.up_others = grad_by_rows(e.dense_in, [e.up_low], plan)
    del e.dense_in, e.up_low
    e.fence()
    e.mid_part, branch_own, e.hidden_grad = norm_backward(
        e.mine, e.arrived, e.hidden_state, e.full_mid, e.own_grad_out, True
    )
    del e.mine, e.arrived, e.own_grad_out
    e.branch_own = branch_own
    e.out_others, e.out_own = to_columns(e.inner_act, e.down, table)
    del e.inner_act, e.down
    e.gate_sum = add_blocks(e.gate_own, gate_x)
    del e.gate_own
    e.down_sum = down_z
    e.fence()
    gate_z = along_z.exchange(e.gate_sum)
    del e.gate_sum
    up_x = plan.scatter_x(e.up_others)
    del e.up_others
    e.branch_tiles = plan.share_y(e.branch_own)
    del e.branch_own
    e.fence()
    e.branch_low = plan.share_cores(e.branch_tiles, BF16)
    del e.branch_tiles
    e.swish_low, e.mixed_low, state_grad = each.call(
        gate_kernel,
        [
            each.whole(e.branch_low),
            *[each.rows_of(weight) for weight in e.output],
            each.flat(e.swish_pre, VD, 0),
            each.flat(e.mixed, VD, 0),
            each.flat(e.queries_keys, QK, 0),
        ],
        [(VD, BF16), (VD, BF16), (None, F32)],
    )
    e.state_grad = state_grad
    del e.swish_pre, e.mixed, e.output
    e.fence()
    e.up_sum = add_blocks(e.up_own, up_x)
    del e.up_own
    e.gate_sum = gate_z
    e.fence()
    up_z = along_z.exchange(e.up_sum)
    del e.up_sum
    e.output_own, e.output_others = grad_by_columns(e.gated, e.branch_low, plan)
    del e.gated, e.branch_low
    e.swish_own, e.swish_others = grad_by_rows(e.mixer_in, [e.swish_low], plan)
    e.state_grad = plan.scan_begin(e.state_grad)
    e.out_others = plan.sum_cores(e.out_others)
    e.fence()
    output_x = plan.scatter_x(e.output_others)
    del e.output_others
    e.down_sum = added(e.down_sum)
    e.gate_sum = added(e.gate_sum)
    e.state_grad = plan.scan_sums(e.state_grad, carry_scale, True)
    e.up_sum = up_z
    e.fence()
    half = along_z.size // 2
    e.swish_first = plan.scatter_x([part[:half] for part in e.swish_others])
    e.swish_others = [part[half:] for part in e.swish_others]
    e.state_grad = plan.scan_middle(e.state_grad, carry_scale, True)
    e.output_sum = add_blocks(e.output_own, output_x)
    del e.output_own
    e.fence()
    output_z = along_z.exchange(e.output_sum)
    del e.output_sum
    e.state_grad = plan.scan_end(e.state_grad)
    e.fence()
    swish_x = plan.scatter_x(e.swish_others)
    del e.swish_others
    e.query_low, e.key_low, e.value_low = each.call(
        mix_back_kernel,
        [
            each.flat(e.queries_keys, QK, 0),
            each.flat(e.queries_keys, QK, local_heads),
            each.flat(e.values, VD, 0),
            each.flat(e.mixed_low, VD, 0),
            each.state(e.state),
            each.state(e.state_grad),
        ],
        [(QK, BF16), (QK, BF16), (VD, BF16)],
    )
    del e.state, e.state_grad, e.mixed_low, e.queries_keys, e.values
    e.value_own, e.value_others = grad_by_rows(e.mixer_in, [e.value_low], plan)
    mine, pieces = fold_tiles(e.out_own, e.out_others, along_y.size)
    del e.out_own, e.out_others
    e.mine, e.arrived = mine, plan.sum_y(pieces)
    e.fence()
    swish_x = [list(parts) for parts in zip(e.swish_first, swish_x)]
    e.swish_sum = add_blocks(e.swish_own, swish_x)
    del e.swish_own, e.swish_first
    e.output_sum = output_z
    e.fence()
    swish_z = along_z.exchange(e.swish_sum)
    del e.swish_sum
    value_x = plan.scatter_x(e.value_others)
    del e.value_others
    e.part_others, e.part_own = to_rows(
        [[e.query_low, e.key_low], [e.value_low], [e.swish_low]],
        [e.query_key, e.value, e.swish],
        table,
    )
    del e.value_low, e.swish_low, e.query_key, e.value, e.swish
    e.layer_tiles = plan.share_y(leave_dense(e.mine, e.arrived, e.hidden_state))
    del e.mine, e.arrived, e.hidden_state
    e.fence()
    e.query_key_own, e.query_key_others = grad_by_rows(
        e.mixer_in, [e.query_low, e.key_low], plan
    )
    del e.query_low, e.key_low, e.mixer_in
    query_key_x = plan.scatter_x(e.query_key_others)
    del e.query_key_others
    e.part_others = plan.sum_cores(e.part_others)
    e.up_sum = added(e.up_sum)
    e.fence()
    e.mine, e.pieces = fold_tiles(e.part_own, e.part_others, along_y.size)
    del e.part_own, e.part_others
    e.value_sum = add_blocks(e.value_own, value_x)
    del e.value_own
    e.swish_sum = swish_z
    e.fence()
    value_z = along_z.exchange(e.value_sum)
    del e.value_sum
    e.arrived = plan.sum_y(e.pieces)
    del e.pieces
    e.output_sum = added(e.output_sum)
    e.swish_sum = added(e.swish_sum)
    e.fence()
    e.pre_part, e.tokens_own = norm_backward(
        e.mine, e.arrived, e.own_tokens, e.full_pre, e.hidden_grad, False
    )
    del e.mine, e.arrived, e.own_tokens, e.hidden_grad
    vectors = jnp.stack([e.mid_part, e.pre_part]).reshape(2, blocks_x, -1)
    vectors = plan.sum_vectors(along_y.total(along_core.total(vectors)))
    del e.mid_part, e.pre_part
    e.query_key_sum = add_blocks(e.query_key_own, query_key_x, vectors)
    del e.query_key_own
    e.value_sum = value_z
    e.fence()
    e.layer_out = plan.share_cores(e.layer_tiles, BF16, to_owners)
    e.tokens_grad = plan.share_cores(plan.share_y(e.tokens_own), F32, to_owners)
    last = added(along_z.exchange(e.query_key_sum))
    slice_width = pre_gain.shape[0]
    query_key_grad = last[:slice_width]
    mid_grad, pre_grad = (last[slice_width + i, :slice_width] for i in range(2))
    return (
        e.layer_out.reshape(tokens.shape),
        e.tokens_grad.reshape(tokens.shape),
        pre_grad,
        query_key_grad[:, :key_width],
        query_key_grad[:, key_width:],
        added(e.value_sum),
        e.swish_sum,
        e.output_sum,
        mid_grad,
        e.gate_sum,
        e.up_sum,
        e.down_sum,
    )


def solution(mesh):
    rows, weight, turned, vector = (
        P(None, "seq", None),
        P("seq", "shard"),
        P("shard", "seq"),
        P("seq"),
    )
    return jax.shard_map(
        functools.partial(on_device, Plan(mesh)),
        mesh=mesh,
        in_specs=(
            rows,
            vector,
            weight,
            weight,
            weight,
            weight,
            turned,
            vector,
            weight,
            weight,
            turned,
            rows,
        ),
        out_specs=(
            rows,
            rows,
            vector,
            weight,
            weight,
            weight,
            weight,
            turned,
            vector,
            weight,
            weight,
            turned,
        ),
        check_vma=False,
    )
```

```python
import functools

import jax
import jax.numpy as jnp
from jax import lax
from jax.experimental import pallas as pl
from jax.experimental.pallas import tpu as pltpu
from jax.sharding import PartitionSpec as P

QK = 256
VD = 512
CHIPS_Z = 4
CORES = 2
F32 = jnp.float32
BF16 = jnp.bfloat16
VMEM_LIMIT = 52 * 1024 * 1024


class Line:
    def __init__(self, axis, total, size, stride):
        self.axis, self.size, self.stride = axis, size, stride
        self.starts = [i for i in range(total) if (i // stride) % size == 0]

    def here(self):
        return lax.rem(lax.div(lax.axis_index(self.axis), self.stride), self.size)

    def send(self, value, moves):
        pairs = [(o + i * self.stride, o + j * self.stride) for i, j in moves for o in self.starts]
        return lax.ppermute(value, self.axis, pairs)

    def ring(self, value, distance):
        return self.send(value, [(i, (i + distance) % self.size) for i in range(self.size)])

    def exchange(self, blocks):
        groups = [[o + i * self.stride for i in range(self.size)] for o in self.starts]
        return lax.all_to_all(
            blocks, self.axis, split_axis=0, concat_axis=0, axis_index_groups=groups, tiled=True
        )

    def total(self, value):
        every = [value] + [self.ring(value, d) for d in range(1, self.size)]
        if self.size == 2:
            return every[0] + every[1]
        out = 0.0
        for position in range(self.size):
            out = out + self.pick(every, position)
        return out

    def pick(self, every, position):
        out = every[0]
        for d in range(1, self.size):
            source = lax.rem(self.here() - d + self.size, self.size)
            out = jnp.where(source == position, every[d], out)
        return out


class Plan:
    def __init__(self, mesh):
        seq, shard = mesh.shape["seq"], mesh.shape["shard"]
        self.seq, self.shard = seq, shard
        self.along_x = Line("seq", seq, seq // CHIPS_Z, 1)
        self.along_z = Line("seq", seq, CHIPS_Z, seq // CHIPS_Z)
        self.along_core = Line("shard", shard, CORES, 1)
        self.along_y = Line("shard", shard, shard // CORES, CORES)

    def slot_owner(self):
        x, z = self.along_x, self.along_z
        return jnp.stack(
            [
                k * x.size + lax.rem(x.here() + j, x.size)
                for j in range(x.size)
                for k in range(z.size)
            ]
        ).astype(jnp.int32)

    def owner_slot(self):
        x, z = self.along_x, self.along_z
        return jnp.stack(
            [
                lax.rem(x.size + j - x.here(), x.size) * z.size + k
                for k in range(z.size)
                for j in range(x.size)
            ]
        ).astype(jnp.int32)

    def row_tiles(self):
        core, y = self.along_core, self.along_y
        return jnp.stack(
            [
                lax.rem(core.here() + j, core.size) * y.size + lax.rem(y.here() + k, y.size)
                for j in (*range(1, core.size), 0)
                for k in range(y.size)
            ]
        ).astype(jnp.int32)

    def own_rows(self, whole):
        core, y = self.along_core, self.along_y
        step = whole.shape[0] // self.shard
        return lax.dynamic_slice_in_dim(whole, (core.here() * y.size + y.here()) * step, step, 0)

    def copies(self, own):
        def kernel(_, in_ref, out_ref):
            out_ref[0] = in_ref[...]

        return call(
            kernel,
            jnp.zeros((1,), jnp.int32),
            (self.along_z.size,),
            [own],
            [resident(own)],
            [((self.along_z.size, *own.shape), own.dtype)],
            [pl.BlockSpec((1, *own.shape), lambda i, _: (i, 0, 0))],
        )[0]

    def gather_z(self, own):
        return [own] + [self.along_z.ring(own, -k) for k in range(1, self.along_z.size)]

    def gather_x(self, row):
        return [row] + [self.along_x.ring(row, -j) for j in range(1, self.along_x.size)]

    def scatter_x(self, others):
        return [self.along_x.ring(part, j) for j, part in enumerate(others, 1)]

    def sum_cores(self, others):
        core = self.along_core
        return [core.ring(piece, d) for d in range(1, core.size) for piece in others]

    def sum_y(self, pieces):
        y = self.along_y
        return [y.ring(piece, k) for k, group in enumerate(pieces, 1) for piece in group]

    def share_y(self, pieces):
        y = self.along_y
        return [pieces] + [[y.ring(piece, -k) for piece in pieces] for k in range(1, y.size)]

    def share_cores(self, tiles, kind, columns=None):
        core, y = self.along_core, self.along_y
        others = [[core.ring(piece, 1) for piece in pieces] for pieces in tiles]
        here = jnp.stack([core.here(), y.here()]).astype(jnp.int32)
        if columns is None:
            columns = jnp.zeros((1,), jnp.int32)
        return place_tiles(jnp.concatenate([here, columns]), tiles, others, kind)

    def scan_begin(self, own):
        x = self.along_x
        step = own.shape[2] // x.size

        def part_for(distance):
            index = lax.rem(x.here() + distance, x.size) * step
            return lax.dynamic_slice_in_dim(own, index, step, 2)

        return [part_for(0)] + [
            x.ring(part_for(d).astype(BF16), d).astype(F32) for d in range(1, x.size)
        ]

    def order(self, device, later):
        return self.along_x.size - 1 - device if later else device

    def scan_sums(self, pieces, decay, later):
        x = self.along_x
        decay = decay[None, :, None, None]
        out = []
        for b in range(pieces[0].shape[0]):
            parts = [piece[b : b + 1] for piece in pieces]
            ordered = [x.pick(parts, self.order(i, later)) for i in range(x.size)]
            row_sum = ordered[0]
            for piece in ordered[1:]:
                row_sum = row_sum * decay + piece
            out.append((ordered[:-1], row_sum, row_sum.astype(BF16)))
        return out

    def scan_middle(self, sums, decay, later):
        x, z = self.along_x, self.along_z
        decay = decay[None, :, None, None]
        row_decay = decay**x.size
        pairs = [[(i, i + d) for i in range(z.size - d)] for d in (1, 2)]
        if later:
            pairs = [[(j, i) for i, j in moves] for moves in pairs]
        near = [z.send(low, pairs[0]).astype(F32) for _, _, low in sums]
        pair = [row_sum + row_decay * part for (_, row_sum, _), part in zip(sums, near)]
        far = [z.send(value.astype(BF16), pairs[1]).astype(F32) for value in pair]
        out = []
        for (ordered, _, _), near_part, far_part in zip(sums, near, far):
            entering = [near_part + row_decay * far_part]
            for piece in ordered:
                entering.append(entering[-1] * decay + piece)

            def for_device(distance):
                target = self.order(lax.rem(x.here() + distance, x.size), later)
                value = entering[0]
                for i in range(1, x.size):
                    value = jnp.where(target == i, entering[i], value)
                return value

            out.append(
                [for_device(0)] + [for_device(d).astype(BF16) for d in range(1, x.size)]
            )
        return out

    def scan_end(self, shares):
        x = self.along_x
        out = []
        for own, *others in shares:
            back = [own] + [x.ring(part, d).astype(F32) for d, part in enumerate(others, 1)]
            out.append(jnp.concatenate([x.pick(back, i) for i in range(x.size)], axis=2))
        return jnp.concatenate(out, axis=0)

    def gains_x(self, gains):
        x, z = self.along_x, self.along_z
        slots = jnp.zeros((2, z.size, x.size, gains.shape[1]), gains.dtype)
        slots = lax.dynamic_update_slice(slots, gains[:, None, None], (0, z.here(), x.here(), 0))
        return x.total(slots.reshape(2, z.size, -1))

    def gains_z(self, slots):
        x, z = self.along_x, self.along_z
        slots = z.total(slots).reshape(2, z.size, x.size, -1)
        turned = [
            lax.dynamic_slice_in_dim(slots, lax.rem(x.here() + j, x.size), 1, 2)[:, :, 0]
            for j in range(x.size)
        ]
        return jnp.concatenate(turned, axis=1).reshape(2, -1)

    def sum_vectors(self, vectors):
        mine = vectors[:, 0]
        for part in self.scatter_x([vectors[:, j] for j in range(1, self.along_x.size)]):
            mine = mine + part
        return mine.reshape(mine.shape[0], self.along_z.size, -1).transpose(1, 0, 2)


CHEAP = pl.CostEstimate(flops=0, bytes_accessed=0, transcendentals=0)


def resident(array):
    if isinstance(array, Part):
        return pl.BlockSpec(
            array.shape, lambda *_: (0, array.index, 0), pipeline_mode=pl.Buffered(1)
        )
    return pl.BlockSpec(
        array.shape, lambda *_: (0,) * array.ndim, pipeline_mode=pl.Buffered(1)
    )


class Part:
    def __init__(self, array, index, count):
        self.array, self.index = array, index
        planes, rows, columns = array.shape
        self.shape, self.ndim, self.dtype = (planes, rows // count, columns), 3, array.dtype


def call(kernel, table, grid, arrays, specs, outs, out_specs, flops=0):
    return pl.pallas_call(
        kernel,
        grid_spec=pltpu.PrefetchScalarGridSpec(
            num_scalar_prefetch=1, grid=grid, in_specs=specs, out_specs=out_specs
        ),
        out_shape=[jax.ShapeDtypeStruct(*out) for out in outs],
        compiler_params=pltpu.CompilerParams(vmem_limit_bytes=VMEM_LIMIT),
        cost_estimate=pl.CostEstimate(flops=flops, bytes_accessed=0, transcendentals=0),
    )(table, *[array.array if isinstance(array, Part) else array for array in arrays])


def turn_kernel(table, in_ref, out_ref):
    width = in_ref.shape[1] // table.shape[0]
    for i in range(table.shape[0]):
        start = pl.multiple_of(table[i] * width, width)
        out_ref[:, i * width : (i + 1) * width] = in_ref[:, pl.ds(start, width)]


def turn(value, table):
    rows, width = value.shape
    tile = min(rows, 256)
    return pl.pallas_call(
        turn_kernel,
        grid_spec=pltpu.PrefetchScalarGridSpec(
            num_scalar_prefetch=1,
            grid=(rows // tile,),
            in_specs=[pl.BlockSpec((tile, width), lambda i, t: (i, 0))],
            out_specs=pl.BlockSpec((tile, width), lambda i, t: (i, 0)),
        ),
        out_shape=jax.ShapeDtypeStruct(value.shape, value.dtype),
        cost_estimate=CHEAP,
    )(table, value)


def norm_turn_kernel(table, in_ref, gain_ref, out_ref):
    width = in_ref.shape[1] // table.shape[0]
    values = in_ref[...].astype(F32)
    mean = jnp.mean(values, axis=-1, keepdims=True)
    centred = values - mean
    scale = lax.rsqrt(jnp.mean(centred * centred, axis=-1, keepdims=True) + 1e-05)
    for i in range(table.shape[0]):
        start = pl.multiple_of(table[i] * width, width)
        block = in_ref[:, pl.ds(start, width)].astype(F32)
        gain = gain_ref[:, i * width : (i + 1) * width]
        out_ref[:, i * width : (i + 1) * width] = ((block - mean) * scale * gain).astype(BF16)


def norm_turn(value, gain, table):
    rows, width = value.shape
    tile = min(rows, 256)
    return pl.pallas_call(
        norm_turn_kernel,
        grid_spec=pltpu.PrefetchScalarGridSpec(
            num_scalar_prefetch=1,
            grid=(rows // tile,),
            in_specs=[
                pl.BlockSpec((tile, width), lambda i, t: (i, 0)),
                pl.BlockSpec((1, width), lambda i, t: (0, 0)),
            ],
            out_specs=pl.BlockSpec((tile, width), lambda i, t: (i, 0)),
        ),
        out_shape=jax.ShapeDtypeStruct(value.shape, BF16),
        cost_estimate=CHEAP,
    )(table, value, gain.reshape(1, -1))


def silu_parts(values):
    sigmoid = 1.0 / (1.0 + jnp.exp(-values))
    return sigmoid, values * sigmoid


def norm_parts(values):
    centred = values - jnp.mean(values, axis=-1, keepdims=True)
    scale = lax.rsqrt(jnp.mean(centred * centred, axis=-1, keepdims=True) + 1e-05)
    return centred * scale, scale


def halves(values):
    high = values.astype(BF16)
    return high, (values - high.astype(F32)).astype(BF16)


def row_decay(log, rows, first, step):
    position = lax.broadcasted_iota(jnp.int32, (rows, 1), 0)
    return jnp.exp((first + step * position).astype(F32) * log)


def pair_decay(log, rows):
    row = lax.broadcasted_iota(jnp.int32, (rows, rows), 0)
    column = lax.broadcasted_iota(jnp.int32, (rows, rows), 1)
    offset = row - column
    return jnp.where(offset >= 0, jnp.exp(jnp.maximum(offset, 0).astype(F32) * log), 0.0)


def state_kernel(logs, key_ref, value_ref, state_ref):
    rows = key_ref.shape[0]
    scaled = key_ref[...].astype(F32) * row_decay(logs[pl.program_id(1)], rows, rows - 1, -1)
    high, low = halves(scaled)
    value = value_ref[...]
    state_ref[0, 0] = t_matmul(high, value) + t_matmul(low, value)


def mix_kernel(logs, query_ref, key_ref, value_ref, state_ref, swish_ref, gated_ref, mixed_ref):
    rows = key_ref.shape[0]
    log = logs[pl.program_id(1)]
    query = query_ref[...]
    weights = (matmul_t(query, key_ref[...]) * pair_decay(log, rows)).astype(BF16)
    high, low = halves(state_ref[0, 0])
    cross = matmul(query, high) + matmul(query, low)
    mixed = matmul(weights, value_ref[...]) + cross * row_decay(log, rows, 1, 1)
    mixed_ref[...] = mixed
    gated_ref[...] = (silu_parts(swish_ref[...])[1] * norm_parts(mixed)[0]).astype(BF16)


def gate_kernel(logs, *refs):
    (branch_ref, *output_refs), (swish_ref, mixed_ref, query_ref) = refs[:-6], refs[-6:-3]
    swish_low_ref, mixed_low_ref, state_ref = refs[-3:]
    rows = query_ref.shape[0]
    swish_pre = swish_ref[...]
    grad = from_columns(branch_ref[...], output_refs)
    normalized, scale = norm_parts(mixed_ref[...])
    sigmoid, silu = silu_parts(swish_pre)
    slope = sigmoid * (1.0 + swish_pre * (1.0 - sigmoid))
    swish_low_ref[...] = (grad * normalized * slope).astype(BF16)
    e = grad * silu
    mean = jnp.mean(e, axis=-1, keepdims=True)
    along = jnp.mean(e * normalized, axis=-1, keepdims=True)
    mixed_low = (scale * (e - mean - normalized * along)).astype(BF16)
    mixed_low_ref[...] = mixed_low
    scaled = query_ref[...].astype(F32) * row_decay(logs[pl.program_id(1)], rows, 1, 1)
    high, low = halves(scaled)
    state_ref[0, 0] = t_matmul(high, mixed_low) + t_matmul(low, mixed_low)


def mix_back_kernel(
    logs,
    query_ref,
    key_ref,
    value_ref,
    mixed_low_ref,
    state_ref,
    state_grad_ref,
    query_low_ref,
    key_low_ref,
    value_low_ref,
):
    rows = key_ref.shape[0]
    log = logs[pl.program_id(1)]
    query, key, value, mixed_low = (
        query_ref[...],
        key_ref[...],
        value_ref[...],
        mixed_low_ref[...],
    )
    decay = pair_decay(log, rows)
    weights = (matmul_t(query, key) * decay).astype(BF16)
    score = (matmul_t(mixed_low, value) * decay).astype(BF16)
    high, low = halves(state_ref[0, 0])
    cross = matmul_t(mixed_low, high) + matmul_t(mixed_low, low)
    query_low_ref[...] = (matmul(score, key) + cross * row_decay(log, rows, 1, 1)).astype(BF16)
    high, low = halves(state_grad_ref[0, 0])
    to_end = row_decay(log, rows, rows - 1, -1)
    cross = matmul_t(value, high) + matmul_t(value, low)
    key_low_ref[...] = (t_matmul(score, query) + cross * to_end).astype(BF16)
    cross = matmul(key, high) + matmul(key, low)
    value_low_ref[...] = (t_matmul(weights, mixed_low) + cross * to_end).astype(BF16)


def at_once(kernel, arrays, outs, table=None, flops=0):
    if table is None:
        table = jnp.zeros((1,), jnp.int32)
    return call(
        kernel,
        table,
        (1,),
        arrays,
        [resident(array) for array in arrays],
        outs,
        [pl.BlockSpec(shape, lambda i, _, n=len(shape): (0,) * n) for shape, _ in outs],
        flops,
    )


def add_blocks(own, arrived, extra=None, flops=0):
    count, rows, columns = own.shape
    more = () if extra is None else (extra,)
    below = 0 if extra is None else 16
    arrays, specs = [own], [pl.BlockSpec((1, rows, columns), lambda i, _: (i, 0, 0))]
    for parts in arrived:
        start = 0
        for part in parts if isinstance(parts, list) else [parts]:
            size = part.shape[0]
            arrays.append(part)
            specs.append(
                pl.BlockSpec(
                    (1, rows, columns),
                    lambda i, _, start=start, size=size: (jnp.clip(i - start, 0, size - 1), 0, 0),
                )
            )
            start += size
    sizes = [array.shape[0] for array in arrays[1:]]

    def kernel(_, *refs):
        step = pl.program_id(0)
        out = refs[0][...].astype(F32)
        start = 0
        for ref, size in zip(refs[1 : len(arrays)], sizes):
            part = ref[...].astype(F32)
            if size < count:
                part = jnp.where((step >= start) & (step < start + size), part, 0.0)
                start = (start + size) % count
            out = out + part
        refs[-1][:, :rows, :] = out.astype(BF16)
        if more:
            refs[-1][:, rows:, :] = refs[-2][...]

    if more:
        extra = jnp.pad(
            extra.astype(BF16),
            ((0, 0), (0, below - extra.shape[1]), (0, columns - extra.shape[2])),
        )
        more = (extra,)
    return call(
        kernel,
        jnp.zeros((1,), jnp.int32),
        (count,),
        [*arrays, *more],
        specs + [pl.BlockSpec((1, below, columns), lambda i, _: (i, 0, 0)) for _ in more],
        [((count, rows + below, columns), BF16)],
        [pl.BlockSpec((1, rows + below, columns), lambda i, _: (i, 0, 0))],
        flops,
    )[0]


def order_blocks(first, blocks):
    count = len(blocks)
    shape = blocks[0].shape

    def kernel(first, *refs):
        for k in range(count):

            @pl.when(pl.program_id(0) == lax.rem(first[0] + k, count))
            def _(k=k):
                refs[-1][0] = refs[k][...]

    return call(
        kernel,
        first.astype(jnp.int32).reshape(1),
        (count,),
        blocks,
        [resident(block) for block in blocks],
        [((count, *shape), blocks[0].dtype)],
        [pl.BlockSpec((1, *shape), lambda i, _: (i, 0, 0))],
    )[0]


def fold_tiles(own, arrived, tiles, flops=0):
    rows, width = own.shape
    tile = rows // tiles
    piece = tile // 2

    def kernel(_, own_ref, *refs):
        outs = refs[len(arrived) :]
        for i in range(2 * tiles):
            value = own_ref[i * piece : (i + 1) * piece, :]
            for ref in refs[i : len(arrived) : 2 * tiles]:
                value = value + ref[...].astype(F32)
            if i < 2:
                outs[0][i * piece : (i + 1) * piece, :] = value
            else:
                outs[i - 1][...] = value.astype(BF16)

    mine, *pieces = at_once(
        kernel,
        [own, *arrived],
        [((tile, width), F32)] + [((piece, width), BF16)] * (2 * tiles - 2),
        flops=flops,
    )
    return mine, [pieces[2 * k : 2 * k + 2] for k in range(tiles - 1)]


def summed(mine_ref, refs, piece):
    rows = mine_ref.shape[0] // 2
    value = mine_ref[piece * rows : (piece + 1) * rows, :]
    for ref in refs[piece::2]:
        value = value + ref[...].astype(F32)
    return value


def enter_dense(mine, arrived, tokens, gain):
    rows, width = mine.shape
    half = rows // 2

    def kernel(_, mine_ref, tokens_ref, gain_ref, *refs):
        hidden_ref, *outs = refs[len(arrived) :]
        for i in range(2):
            part = slice(i * half, (i + 1) * half)
            hidden = tokens_ref[part, :].astype(F32) + summed(mine_ref, refs[: len(arrived)], i)
            hidden_ref[part, :] = hidden
            outs[i][...] = (norm_parts(hidden)[0] * gain_ref[...]).astype(BF16)

    hidden, *pieces = at_once(
        kernel,
        [mine, tokens, gain.reshape(1, -1), *arrived],
        [((rows, width), F32)] + [((half, width), BF16)] * 2,
    )
    return hidden, pieces


def leave_dense(mine, arrived, hidden):
    rows, width = mine.shape
    half = rows // 2

    def kernel(_, mine_ref, hidden_ref, *refs):
        for i in range(2):
            value = hidden_ref[i * half : (i + 1) * half, :] + summed(
                mine_ref, refs[: len(arrived)], i
            )
            refs[len(arrived) + i][...] = value.astype(BF16)

    return at_once(kernel, [mine, hidden, *arrived], [((half, width), BF16)] * 2)


def norm_backward(mine, arrived, values, gain, residual, keep):
    rows, width = mine.shape
    half = rows // 2

    def kernel(_, mine_ref, values_ref, gain_ref, residual_ref, *refs):
        gain_out, first, second, *whole = refs[len(arrived) :]
        gain_sum = 0.0
        for i in range(2):
            part = slice(i * half, (i + 1) * half)
            grad = summed(mine_ref, refs[: len(arrived)], i)
            normalized, scale = norm_parts(values_ref[part, :].astype(F32))
            gain_sum = gain_sum + jnp.sum(grad * normalized, axis=0, keepdims=True)
            e = grad * gain_ref[...]
            mean = jnp.mean(e, axis=-1, keepdims=True)
            along = jnp.mean(e * normalized, axis=-1, keepdims=True)
            out = residual_ref[part, :].astype(F32) + scale * (e - mean - normalized * along)
            (first, second)[i][...] = out.astype(BF16)
            for ref in whole:
                ref[part, :] = out
        gain_out[...] = gain_sum

    gain_part, first, second, *whole = at_once(
        kernel,
        [mine, values, gain.reshape(1, -1), residual, *arrived],
        [((1, width), F32)]
        + [((half, width), BF16)] * 2
        + [((rows, width), F32)] * (1 if keep else 0),
    )
    return gain_part, [first, second], *whole


def place_tiles(table, near, far, kind):
    tiles = len(near)
    pieces = [piece for tile in near + far for piece in tile]
    piece, width = pieces[0].shape
    columns = table.shape[0] - 2
    block = width // columns

    def kernel(table, *refs):
        out_ref = refs[-1]
        step = pl.program_id(0)
        for i in range(2 * tiles):
            core = lax.rem(table[0] + i // tiles, CORES)
            row = lax.rem(table[1] + i % tiles, tiles)

            @pl.when(step == core * tiles + row)
            def _(i=i):
                for part in range(2):
                    ref = refs[2 * i + part]
                    for j in range(columns):
                        start = pl.multiple_of(table[2 + j] * block, block)
                        out_ref[
                            part * piece : (part + 1) * piece, j * block : (j + 1) * block
                        ] = ref[:, pl.ds(start, block)].astype(kind)

    return call(
        kernel,
        table,
        (CORES * tiles,),
        pieces,
        [resident(ref) for ref in pieces],
        [((2 * CORES * tiles * piece, width), kind)],
        [pl.BlockSpec((2 * piece, width), lambda i, _: (i, 0))],
    )[0]


def by_rows(ref):
    return ref[...].reshape(-1, ref.shape[2])


def from_columns(values, refs):
    out, start = 0.0, 0
    for ref in refs:
        weight = jnp.concatenate([ref[k] for k in range(ref.shape[0])], axis=1)
        stop = start + weight.shape[1]
        out = out + matmul_t(values[:, start:stop], weight)
        start = stop
    return out


def project(values, weight, kind):
    rows, width = values.shape
    tile = min(rows, 256)
    columns = weight[0].shape[2]

    def kernel(_, in_ref, *refs):
        depth = width // len(weight)
        out = matmul(in_ref[:, :depth], by_rows(refs[0]))
        for j in range(1, len(weight)):
            out = out + matmul(in_ref[:, j * depth : (j + 1) * depth], by_rows(refs[j]))
        refs[-1][...] = out.astype(kind)

    return call(
        kernel,
        jnp.zeros((1,), jnp.int32),
        (rows // tile,),
        [values, *weight],
        [pl.BlockSpec((tile, width), lambda i, _: (i, 0))] + [resident(w) for w in weight],
        [((rows, columns), kind)],
        [pl.BlockSpec((tile, columns), lambda i, _: (i, 0))],
    )[0]


def parts_by_rows(compute, table, model_width, arrays, specs, outs, out_specs):
    count = table.shape[0]
    rows = arrays[0].shape[0]
    tile = rows // count
    away = count - count // CORES
    half = tile // 2

    def kernel(table, *refs):
        step = pl.program_id(0)
        pieces, own_ref = refs[-2 * away - 1 : -1], refs[-1]
        value = compute(*refs[: -2 * away - 1])
        for i in range(away):

            @pl.when(step == i)
            def _(i=i):
                pieces[2 * i][...] = value[:half].astype(BF16)
                pieces[2 * i + 1][...] = value[half:].astype(BF16)

        @pl.when(step >= away)
        def _():
            own_ref[...] = value

    *results, own = call(
        kernel,
        table,
        (count,),
        arrays,
        specs,
        outs + [((half, model_width), BF16)] * (2 * away) + [(((count - away) * tile, model_width), F32)],
        out_specs
        + [pl.BlockSpec((half, model_width), lambda i, t: (0, 0))] * (2 * away)
        + [pl.BlockSpec((tile, model_width), lambda i, t: (jnp.maximum(i - away, 0), 0))],
    )
    return *results[: len(outs)], results[len(outs) :], own


def tile_of(array, table):
    return pl.BlockSpec(
        (array.shape[0] // table.shape[0], array.shape[1]), lambda i, t: (t[i], 0)
    )


def to_columns(values, weight, table):
    def compute(in_ref, *refs):
        value = in_ref[...]
        return jnp.concatenate(
            [matmul(value, ref[k]) for ref in refs for k in range(ref.shape[0])], axis=1
        )

    return parts_by_rows(
        compute,
        table,
        sum(w.shape[0] * w.shape[2] for w in weight),
        [values, *weight],
        [tile_of(values, table)] + [resident(w) for w in weight],
        [],
        [],
    )


def dense_forward(dense_in, gate, up):
    rows, width = dense_in.shape
    tile = min(rows, 256)
    units = gate[0].shape[2]

    def kernel(_, in_ref, *refs):
        gate_refs, up_refs = refs[: len(gate)], refs[len(gate) : -3]
        depth = width // len(gate)
        pre = []
        for weights in (gate_refs, up_refs):
            out = 0.0
            for j, ref in enumerate(weights):
                out = out + matmul(in_ref[:, j * depth : (j + 1) * depth], by_rows(ref))
            pre.append(out)
        refs[-3][...], refs[-2][...] = pre
        refs[-1][...] = (gelu_parts(pre[0])[0] * pre[1]).astype(BF16)

    block = pl.BlockSpec((tile, units), lambda i, _: (i, 0))
    return call(
        kernel,
        jnp.zeros((1,), jnp.int32),
        (rows // tile,),
        [dense_in, *gate, *up],
        [pl.BlockSpec((tile, width), lambda i, _: (i, 0))] + [resident(w) for w in (*gate, *up)],
        [((rows, units), F32), ((rows, units), F32), ((rows, units), BF16)],
        [block] * 3,
    )


def dense_backward(grad_out, gate_pre, up_pre, down, gate, up, table):
    units = gate_pre.shape[1]

    def compute(grad_ref, gate_pre_ref, up_pre_ref, *refs):
        count = len(down)
        down_refs, gate_refs, up_refs = (refs[i * count : (i + 1) * count] for i in range(3))
        gate_low_ref, up_low_ref = refs[3 * count :]
        grad = from_columns(grad_ref[...], down_refs).astype(BF16).astype(F32)
        act, slope = gelu_parts(gate_pre_ref[...])
        gate_low = (grad * up_pre_ref[...] * slope).astype(BF16)
        up_low = (grad * act).astype(BF16)
        gate_low_ref[...] = gate_low
        up_low_ref[...] = up_low
        return jnp.concatenate(
            [
                matmul_t(gate_low, by_rows(g)) + matmul_t(up_low, by_rows(u))
                for g, u in zip(gate_refs, up_refs)
            ],
            axis=1,
        )

    weights = [*down, *gate, *up]
    tiles = [grad_out, gate_pre, up_pre]
    return parts_by_rows(
        compute,
        table,
        grad_out.shape[1],
        tiles + weights,
        [tile_of(a, table) for a in tiles]
        + [resident(w) for w in weights],
        [((gate_pre.shape[0], units), BF16)] * 2,
        [tile_of(gate_pre, table)] * 2,
    )


def to_rows(values, weights, table):
    counts = [len(group) for group in values]
    blocks = len(weights[0])

    def compute(*refs):
        refs = list(refs)
        inputs = []
        for count in counts:
            group = [refs.pop(0)[...] for _ in range(count)]
            inputs.append(group[0] if count == 1 else jnp.concatenate(group, axis=1))
        outs = [0.0] * blocks
        for value in inputs:
            for j in range(blocks):
                outs[j] = outs[j] + matmul_t(value, by_rows(refs.pop(0)))
        return jnp.concatenate(outs, axis=1)

    flat = [value for group in values for value in group]
    every = [w for weight in weights for w in weight]
    model_width = sum(w.shape[0] * w.shape[1] for w in weights[0])
    return parts_by_rows(
        compute,
        table,
        model_width,
        flat + every,
        [tile_of(value, table) for value in flat] + [resident(w) for w in every],
        [],
        [],
    )


def grad_by_rows(left, rights, plan, own=True, others=True, pieces=1):
    rows, width = left.shape
    x, z = plan.along_x.size, plan.along_z.size
    block = width // (x * z)
    columns = sum(right.shape[1] for right in rights)
    half = z // 2
    away = 2 * (x - 1) if others else 0
    steps = away + (2 if own else 0)
    first = 0 if own and not others else 2

    def kernel(_, left_ref, *refs):
        step = pl.program_id(0)
        value = []
        for right_ref in refs[: len(rights)]:
            value.append(t_matmul(left_ref[...], right_ref[...]))
        value = value[0] if len(value) == 1 else jnp.concatenate(value, axis=1)
        value = value.astype(BF16).reshape(half, block, columns)
        outs = refs[len(rights) :]
        for i in range(away):

            @pl.when(step == i)
            def _(i=i):
                outs[i * pieces // 2][...] = value

        if own:

            @pl.when(step >= away)
            def _():
                outs[-1][...] = value

    piece = (half, block, columns)
    results = call(
        kernel,
        jnp.zeros((1,), jnp.int32),
        (steps,),
        [left, *rights],
        [pl.BlockSpec((rows, half * block), lambda i, _: (0, lax.rem(i + first, 2 * x)))]
        + [resident(right) for right in rights],
        [((z // pieces, block, columns), BF16)] * (away * pieces // 2)
        + [((z, block, columns), BF16)] * own,
        [
            pl.BlockSpec(piece, lambda i, _, j=j: (jnp.clip(i - 2 * j, 0, 1) if pieces == 1 else 0, 0, 0))
            for j in range(away * pieces // 2)
        ]
        + [pl.BlockSpec(piece, lambda i, _: (jnp.maximum(i - away, 0), 0, 0))] * own,
    )
    if not others:
        return results[0]
    parts = list(results[: away * pieces // 2])
    if pieces == 2:
        parts = [parts[2 * j : 2 * j + 2] for j in range(x - 1)]
    return (results[-1], parts) if own else parts


def grad_by_columns(left, right, plan, pieces=1):
    rows, units = left.shape
    x, z = plan.along_x.size, plan.along_z.size
    block = right.shape[1] // (x * z)
    tile = min(units, 512)
    half = z // pieces

    def kernel(_, left_ref, right_ref, own_ref, *other_refs):
        value = t_matmul(left_ref[...], right_ref[...])
        for i in range(x * z):
            part = value[:, i * block : (i + 1) * block].astype(BF16)
            if i < z:
                own_ref[i] = part
            else:
                other_refs[(i - z) // half][(i - z) % half] = part

    own, *others = call(
        kernel,
        jnp.zeros((1,), jnp.int32),
        (units // tile,),
        [left, right],
        [pl.BlockSpec((rows, tile), lambda i, _: (0, i)), resident(right)],
        [((z, units, block), BF16)] + [((half, units, block), BF16)] * (pieces * (x - 1)),
        [pl.BlockSpec((z, tile, block), lambda i, _: (0, i, 0))]
        + [pl.BlockSpec((half, tile, block), lambda i, _: (0, i, 0))] * (pieces * (x - 1)),
    )
    if pieces == 2:
        others = [others[2 * j : 2 * j + 2] for j in range(x - 1)]
    return own, others


def gelu_parts(values):
    root = 0.7978845608028654
    inner = jnp.tanh(root * (values + 0.044715 * (values * values * values)))
    half = 0.5 * (1.0 + inner)
    slope = half + 0.5 * values * (1.0 - inner * inner) * root * (
        1.0 + 3 * 0.044715 * (values * values)
    )
    return values * half, slope


class Heads:
    def __init__(self, logs, seqs, rows):
        self.logs, self.seqs, self.rows = logs, seqs, rows
        self.heads = logs.shape[0]

    def flat(self, array, width, first):
        return array, pl.BlockSpec((self.rows, width), lambda b, h, _: (b, first + h))

    def whole(self, array):
        return array, pl.BlockSpec((self.rows, array.shape[1]), lambda b, h, _: (b, 0))

    def rows_of(self, weight):
        count, _, width = weight.shape
        return weight, pl.BlockSpec((count, VD, width), lambda b, h, _: (0, h, 0))

    def state(self, array):
        return array, pl.BlockSpec((1, 1, QK, VD), lambda b, h, _: (b, h, 0, 0))

    def call(self, kernel, inputs, outs):
        shapes, specs = [], []
        for width, kind in outs:
            if width is None:
                shapes.append(((self.seqs, self.heads, QK, VD), kind))
                specs.append(self.state(None)[1])
            else:
                shapes.append(((self.seqs * self.rows, self.heads * width), kind))
                specs.append(self.flat(None, width, 0)[1])
        return call(
            kernel,
            self.logs,
            (self.seqs, self.heads),
            [array for array, _ in inputs],
            [spec for _, spec in inputs],
            shapes,
            specs,
        )


def matmul(left, right):
    return jnp.dot(left, right, preferred_element_type=F32)


def matmul_t(left, right):
    return lax.dot_general(left, right, (((1,), (1,)), ((), ())), preferred_element_type=F32)


def t_matmul(left, right):
    return lax.dot_general(left, right, (((0,), (0,)), ((), ())), preferred_element_type=F32)


class Live:
    def fence(self):
        names = list(vars(self))
        values = lax.optimization_barrier([getattr(self, name) for name in names])
        for name, value in zip(names, values):
            setattr(self, name, value)


def added(blocks):
    count, rows, columns = blocks.shape
    parts = 2 if rows % 32 == 0 else 1

    def kernel(_, in_ref, out_ref):
        out = in_ref[0].astype(F32)
        for k in range(1, count):
            out = out + in_ref[k].astype(F32)
        out_ref[...] = out

    return call(
        kernel,
        jnp.zeros((1,), jnp.int32),
        (parts,),
        [blocks],
        [pl.BlockSpec((count, rows // parts, columns), lambda i, _: (0, i, 0))],
        [((rows, columns), F32)],
        [pl.BlockSpec((rows // parts, columns), lambda i, _: (i, 0))],
    )[0]


def on_device(
    plan,
    tokens,
    pre_gain,
    query_weight,
    key_weight,
    value_weight,
    swish_weight,
    output_weight,
    mid_gain,
    gate_weight,
    up_weight,
    down_weight,
    cotangent,
):
    seq_count, seg_rows, model_width = tokens.shape
    row_count = seq_count * seg_rows
    to_slots, to_owners, table = plan.slot_owner(), plan.owner_slot(), plan.row_tiles()
    e = Live()
    e.tokens = tokens.reshape(row_count, model_width)
    e.cotangent = cotangent.reshape(row_count, model_width)
    key_width = query_weight.shape[1]
    local_heads = key_width // QK
    copies, blocks_x = plan.copies, plan.along_x.size
    along_z, along_core, along_y = plan.along_z, plan.along_core, plan.along_y
    def parts_of(array):
        return [Part(array, j, blocks_x) for j in range(blocks_x)]

    head_index = (lax.axis_index("shard") * local_heads + jnp.arange(local_heads)).astype(F32)
    logs = jnp.log1p(-jnp.exp2(-5.0 - head_index))
    carry_scale = jnp.exp(seg_rows * logs)
    each = Heads(logs, seq_count, seg_rows)

    e.value = plan.gather_z(value_weight)
    e.gains = plan.gains_x(jnp.stack([pre_gain, mid_gain]).astype(BF16))
    e.query_key = copies(jnp.concatenate([query_weight, key_weight], axis=1))
    e.down = plan.gather_x(down_weight)
    e.grad_out = turn(e.cotangent, to_slots)
    del e.cotangent
    e.own_tokens = turn(plan.own_rows(e.tokens), to_slots)
    e.fence()
    e.value = plan.gather_x(order_blocks(along_z.here(), e.value))
    e.query_key = along_z.exchange(e.query_key)
    e.own_grad_out = plan.own_rows(e.grad_out)
    gains = plan.gains_z(e.gains).astype(F32)
    e.full_pre, e.full_mid = gains[0], gains[1]
    del e.gains
    e.swish = swish_weight
    e.fence()
    e.query_key = plan.gather_x(e.query_key)
    e.swish = plan.gather_z(e.swish)
    e.output = copies(output_weight)
    e.mixer_in = norm_turn(e.tokens, e.full_pre, to_slots)
    del e.tokens
    e.values = project(e.mixer_in, e.value, BF16)
    e.fence()
    output_z = along_z.exchange(e.output)
    del e.output
    e.swish = order_blocks(along_z.here(), e.swish)
    e.queries_keys = project(e.mixer_in, e.query_key, BF16)
    (state,) = each.call(
        state_kernel,
        [each.flat(e.queries_keys, QK, local_heads), each.flat(e.values, VD, 0)],
        [(None, F32)],
    )
    e.state = plan.scan_begin(state)
    e.fence()
    swish_x = plan.gather_x(e.swish)
    del e.swish
    e.output = output_z
    e.gate = copies(gate_weight)
    e.state = plan.scan_sums(e.state, carry_scale, False)
    e.fence()
    e.output_first = plan.gather_x(e.output[:1])[1:]
    e.state = plan.scan_middle(e.state, carry_scale, False)
    e.swish = swish_x
    e.fence()
    gate_z = along_z.exchange(e.gate)
    del e.gate
    e.state = plan.scan_end(e.state)
    e.fence()
    output_x = [e.output]
    for parts in zip(e.output_first, plan.gather_x(e.output[1:])[1:]):
        output_x += parts
    del e.output, e.output_first
    e.gate = gate_z
    e.swish_pre = project(e.mixer_in, e.swish, F32)
    e.gated, e.mixed = each.call(
        mix_kernel,
        [
            each.flat(e.queries_keys, QK, 0),
            each.flat(e.queries_keys, QK, local_heads),
            each.flat(e.values, VD, 0),
            each.state(e.state),
            each.flat(e.swish_pre, VD, 0),
        ],
        [(VD, BF16), (VD, F32)],
    )
    e.up = copies(up_weight)
    e.fence()
    e.up = along_z.exchange(e.up)
    e.gate = plan.gather_x(e.gate)
    branch_others, branch_own = to_columns(e.gated, output_x, table)
    e.output = output_x
    mine, pieces = fold_tiles(
        branch_own, plan.sum_cores(branch_others), along_y.size, flops=9_000_000_000
    )
    e.mine, e.arrived = mine, plan.sum_y(pieces)
    e.down = copies(jnp.concatenate(e.down, axis=0))
    e.fence()
    down_z = along_z.exchange(e.down)
    del e.down
    up_x = plan.gather_x(e.up)
    del e.up
    e.hidden_state, dense_own = enter_dense(e.mine, e.arrived, e.own_tokens, e.full_mid)
    del e.mine, e.arrived
    e.dense_tiles = plan.share_y(dense_own)
    e.fence()
    e.dense_in = plan.share_cores(e.dense_tiles, BF16)
    del e.dense_tiles
    e.up = up_x
    e.fence()
    e.gate_pre, e.up_pre, e.inner_act = dense_forward(e.dense_in, e.gate, e.up)
    e.down_own, e.down_others = grad_by_columns(e.inner_act, e.grad_out, plan)
    e.fence()
    down_x = plan.scatter_x(e.down_others)
    del e.down_others
    e.down = down_z
    e.fence()
    e.gate_low, e.up_low, e.part_others, e.part_own = dense_backward(
        e.grad_out, e.gate_pre, e.up_pre, parts_of(e.down), e.gate, e.up, table
    )
    del e.gate_pre, e.up_pre, e.gate, e.up, e.grad_out
    e.fence()
    e.gate_others = grad_by_rows(e.dense_in, [e.gate_low], plan, own=False)
    e.fence()
    gate_x = plan.scatter_x(e.gate_others)
    del e.gate_others
    e.down_sum = add_blocks(e.down_own, down_x)
    del e.down_own
    e.fence()
    down_z = along_z.exchange(e.down_sum)
    del e.down_sum
    e.part_others = plan.sum_cores(e.part_others)
    e.gate_own = grad_by_rows(e.dense_in, [e.gate_low], plan, others=False)
    del e.gate_low
    e.fence()
    mine, pieces = fold_tiles(e.part_own, e.part_others, along_y.size)
    e.mine, e.arrived = mine, plan.sum_y(pieces)
    del e.part_own, e.part_others
    e.up_own, e.up_others = grad_by_rows(e.dense_in, [e.up_low], plan)
    del e.dense_in, e.up_low
    e.fence()
    e.mid_part, branch_own, e.hidden_grad = norm_backward(
        e.mine, e.arrived, e.hidden_state, e.full_mid, e.own_grad_out, True
    )
    del e.mine, e.arrived, e.own_grad_out
    e.branch_own = branch_own
    e.gate_sum = add_blocks(e.gate_own, gate_x, flops=12_000_000_000)
    del e.gate_own
    e.down_sum = down_z
    e.fence()
    gate_z = along_z.exchange(e.gate_sum)
    del e.gate_sum
    up_x = plan.scatter_x(e.up_others)
    del e.up_others
    e.branch_tiles = plan.share_y(e.branch_own)
    del e.branch_own
    e.out_others, e.out_own = to_columns(e.inner_act, parts_of(e.down), table)
    del e.inner_act, e.down
    e.fence()
    e.branch_low = plan.share_cores(e.branch_tiles, BF16)
    del e.branch_tiles
    e.output_own, e.output_others = grad_by_columns(e.gated, e.branch_low, plan, pieces=2)
    del e.gated
    e.up_sum = add_blocks(e.up_own, up_x, flops=12_000_000_000)
    del e.up_own
    e.gate_sum = gate_z
    e.fence()
    up_z = along_z.exchange(e.up_sum)
    del e.up_sum
    e.output_first = plan.scatter_x([part[0] for part in e.output_others])
    e.output_others = [part[1] for part in e.output_others]
    e.swish_low, e.mixed_low, e.state_grad = each.call(
        gate_kernel,
        [
            each.whole(e.branch_low),
            *[each.rows_of(weight) for weight in e.output],
            each.flat(e.swish_pre, VD, 0),
            each.flat(e.mixed, VD, 0),
            each.flat(e.queries_keys, QK, 0),
        ],
        [(VD, BF16), (VD, BF16), (None, F32)],
    )
    del e.swish_pre, e.mixed, e.output, e.branch_low
    e.fence()
    e.swish_own, e.swish_others = grad_by_rows(e.mixer_in, [e.swish_low], plan, pieces=2)
    e.state_grad = plan.scan_begin(e.state_grad)
    e.out_others = plan.sum_cores(e.out_others)
    e.fence()
    output_x = plan.scatter_x(e.output_others)
    del e.output_others
    e.mine, e.pieces = fold_tiles(e.out_own, e.out_others, along_y.size)
    del e.out_own, e.out_others
    e.state_grad = plan.scan_sums(e.state_grad, carry_scale, True)
    e.up_sum = up_z
    e.fence()
    e.swish_first = plan.scatter_x([part[0] for part in e.swish_others])
    e.swish_others = [part[1] for part in e.swish_others]
    e.state_grad = plan.scan_middle(e.state_grad, carry_scale, True)
    output_x = [list(parts) for parts in zip(e.output_first, output_x)]
    e.output_sum = add_blocks(e.output_own, output_x)
    del e.output_own, e.output_first
    e.fence()
    output_z = along_z.exchange(e.output_sum)
    del e.output_sum
    e.state_grad = plan.scan_end(e.state_grad)
    e.fence()
    swish_x = plan.scatter_x(e.swish_others)
    del e.swish_others
    e.query_low, e.key_low, e.value_low = each.call(
        mix_back_kernel,
        [
            each.flat(e.queries_keys, QK, 0),
            each.flat(e.queries_keys, QK, local_heads),
            each.flat(e.values, VD, 0),
            each.flat(e.mixed_low, VD, 0),
            each.state(e.state),
            each.state(e.state_grad),
        ],
        [(QK, BF16), (QK, BF16), (VD, BF16)],
    )
    del e.state, e.state_grad, e.mixed_low, e.queries_keys, e.values
    e.value_own, e.value_others = grad_by_rows(e.mixer_in, [e.value_low], plan)
    e.arrived = plan.sum_y(e.pieces)
    del e.pieces
    e.fence()
    swish_x = [list(parts) for parts in zip(e.swish_first, swish_x)]
    e.swish_sum = add_blocks(e.swish_own, swish_x)
    del e.swish_own, e.swish_first
    e.output_sum = output_z
    e.fence()
    swish_z = along_z.exchange(e.swish_sum)
    del e.swish_sum
    value_x = plan.scatter_x(e.value_others)
    del e.value_others
    e.part_others, e.part_own = to_rows(
        [[e.query_low, e.key_low], [e.value_low], [e.swish_low]],
        [e.query_key, e.value, e.swish],
        table,
    )
    del e.value_low, e.swish_low, e.query_key, e.value, e.swish
    e.layer_tiles = plan.share_y(leave_dense(e.mine, e.arrived, e.hidden_state))
    del e.mine, e.arrived, e.hidden_state
    e.fence()
    e.query_key_own, e.query_key_others = grad_by_rows(
        e.mixer_in, [e.query_low, e.key_low], plan
    )
    del e.query_low, e.key_low, e.mixer_in
    query_key_x = plan.scatter_x(e.query_key_others)
    del e.query_key_others
    e.part_others = plan.sum_cores(e.part_others)
    e.value_sum = add_blocks(e.value_own, value_x, flops=12_000_000_000)
    del e.value_own
    e.fence()
    e.mine, e.pieces = fold_tiles(e.part_own, e.part_others, along_y.size)
    del e.part_own, e.part_others
    e.swish_sum = swish_z
    e.fence()
    value_z = along_z.exchange(e.value_sum)
    del e.value_sum
    e.arrived = plan.sum_y(e.pieces)
    del e.pieces
    e.down_sum = added(e.down_sum)
    e.gate_sum = added(e.gate_sum)
    e.up_sum = added(e.up_sum)
    e.fence()
    e.pre_part, e.tokens_own = norm_backward(
        e.mine, e.arrived, e.own_tokens, e.full_pre, e.hidden_grad, False
    )
    del e.mine, e.arrived, e.own_tokens, e.hidden_grad
    vectors = jnp.stack([e.mid_part, e.pre_part]).reshape(2, blocks_x, -1)
    vectors = plan.sum_vectors(along_y.total(along_core.total(vectors)))
    del e.mid_part, e.pre_part
    e.query_key_sum = add_blocks(
        e.query_key_own, query_key_x, vectors, flops=12_000_000_000
    )
    del e.query_key_own
    e.value_sum = value_z
    e.fence()
    e.layer_out = plan.share_cores(e.layer_tiles, BF16, to_owners)
    e.tokens_grad = plan.share_cores(plan.share_y(e.tokens_own), F32, to_owners)
    last = added(along_z.exchange(e.query_key_sum))
    slice_width = pre_gain.shape[0]
    query_key_grad = last[:slice_width]
    mid_grad, pre_grad = (last[slice_width + i, :slice_width] for i in range(2))
    return (
        e.layer_out.reshape(tokens.shape),
        e.tokens_grad.reshape(tokens.shape),
        pre_grad,
        query_key_grad[:, :key_width],
        query_key_grad[:, key_width:],
        added(e.value_sum),
        added(e.swish_sum),
        added(e.output_sum),
        mid_grad,
        e.gate_sum,
        e.up_sum,
        e.down_sum,
    )


def solution(mesh):
    rows, weight, turned, vector = (
        P(None, "seq", None),
        P("seq", "shard"),
        P("shard", "seq"),
        P("seq"),
    )
    return jax.shard_map(
        functools.partial(on_device, Plan(mesh)),
        mesh=mesh,
        in_specs=(
            rows,
            vector,
            weight,
            weight,
            weight,
            weight,
            turned,
            vector,
            weight,
            weight,
            turned,
            rows,
        ),
        out_specs=(
            rows,
            rows,
            vector,
            weight,
            weight,
            weight,
            weight,
            turned,
            vector,
            weight,
            weight,
            turned,
        ),
        check_vma=False,
    )
```

```python
import functools

import jax
import jax.numpy as jnp
from jax import lax
from jax.experimental import pallas as pl
from jax.experimental.pallas import tpu as pltpu
from jax.sharding import PartitionSpec as P

QK = 256
VD = 512
CHIPS_Z = 4
CORES = 2
F32 = jnp.float32
BF16 = jnp.bfloat16
VMEM_LIMIT = 52 * 1024 * 1024


class Line:
    def __init__(self, axis, total, size, stride):
        self.axis, self.size, self.stride = axis, size, stride
        self.starts = [i for i in range(total) if (i // stride) % size == 0]

    def here(self):
        return lax.rem(lax.div(lax.axis_index(self.axis), self.stride), self.size)

    def send(self, value, moves):
        pairs = [(o + i * self.stride, o + j * self.stride) for i, j in moves for o in self.starts]
        return lax.ppermute(value, self.axis, pairs)

    def ring(self, value, distance):
        return self.send(value, [(i, (i + distance) % self.size) for i in range(self.size)])

    def exchange(self, blocks):
        groups = [[o + i * self.stride for i in range(self.size)] for o in self.starts]
        return lax.all_to_all(
            blocks, self.axis, split_axis=0, concat_axis=0, axis_index_groups=groups, tiled=True
        )

    def total(self, value):
        every = [value] + [self.ring(value, d) for d in range(1, self.size)]
        if self.size == 2:
            return every[0] + every[1]
        out = 0.0
        for position in range(self.size):
            out = out + self.pick(every, position)
        return out

    def pick(self, every, position):
        out = every[0]
        for d in range(1, self.size):
            source = lax.rem(self.here() - d + self.size, self.size)
            out = jnp.where(source == position, every[d], out)
        return out


class Plan:
    def __init__(self, mesh):
        seq, shard = mesh.shape["seq"], mesh.shape["shard"]
        self.seq, self.shard = seq, shard
        self.along_x = Line("seq", seq, seq // CHIPS_Z, 1)
        self.along_z = Line("seq", seq, CHIPS_Z, seq // CHIPS_Z)
        self.along_core = Line("shard", shard, CORES, 1)
        self.along_y = Line("shard", shard, shard // CORES, CORES)

    def slot_owner(self):
        x, z = self.along_x, self.along_z
        return jnp.stack(
            [
                k * x.size + lax.rem(x.here() + j, x.size)
                for j in range(x.size)
                for k in range(z.size)
            ]
        ).astype(jnp.int32)

    def owner_slot(self):
        x, z = self.along_x, self.along_z
        return jnp.stack(
            [
                lax.rem(x.size + j - x.here(), x.size) * z.size + k
                for k in range(z.size)
                for j in range(x.size)
            ]
        ).astype(jnp.int32)

    def row_tiles(self):
        core, y = self.along_core, self.along_y
        return jnp.stack(
            [
                lax.rem(core.here() + j, core.size) * y.size + lax.rem(y.here() + k, y.size)
                for j in (*range(1, core.size), 0)
                for k in range(y.size)
            ]
        ).astype(jnp.int32)

    def own_rows(self, whole):
        core, y = self.along_core, self.along_y
        step = whole.shape[0] // self.shard
        return lax.dynamic_slice_in_dim(whole, (core.here() * y.size + y.here()) * step, step, 0)

    def copies(self, own):
        def kernel(_, in_ref, out_ref):
            out_ref[0] = in_ref[...]

        return call(
            kernel,
            jnp.zeros((1,), jnp.int32),
            (self.along_z.size,),
            [own],
            [resident(own)],
            [((self.along_z.size, *own.shape), own.dtype)],
            [pl.BlockSpec((1, *own.shape), lambda i, _: (i, 0, 0))],
        )[0]

    def gather_z(self, own):
        return [own] + [self.along_z.ring(own, -k) for k in range(1, self.along_z.size)]

    def gather_x(self, row):
        return [row] + [self.along_x.ring(row, -j) for j in range(1, self.along_x.size)]

    def scatter_x(self, others):
        return [self.along_x.ring(part, j) for j, part in enumerate(others, 1)]

    def sum_cores(self, others):
        core = self.along_core
        return [core.ring(piece, d) for d in range(1, core.size) for piece in others]

    def sum_y(self, pieces):
        y = self.along_y
        return [y.ring(piece, k) for k, group in enumerate(pieces, 1) for piece in group]

    def share_y(self, pieces):
        y = self.along_y
        return [pieces] + [[y.ring(piece, -k) for piece in pieces] for k in range(1, y.size)]

    def share_cores(self, tiles, kind, columns=None):
        core, y = self.along_core, self.along_y
        others = [[core.ring(piece, 1) for piece in pieces] for pieces in tiles]
        here = jnp.stack([core.here(), y.here()]).astype(jnp.int32)
        if columns is None:
            columns = jnp.zeros((1,), jnp.int32)
        return place_tiles(jnp.concatenate([here, columns]), tiles, others, kind)

    def scan_begin(self, own):
        x = self.along_x
        step = own.shape[2] // x.size

        def part_for(distance):
            index = lax.rem(x.here() + distance, x.size) * step
            return lax.dynamic_slice_in_dim(own, index, step, 2)

        return [part_for(0)] + [
            x.ring(part_for(d).astype(BF16), d).astype(F32) for d in range(1, x.size)
        ]

    def order(self, device, later):
        return self.along_x.size - 1 - device if later else device

    def scan_sums(self, pieces, decay, later):
        x = self.along_x
        decay = decay[None, :, None, None]
        out = []
        for b in range(pieces[0].shape[0]):
            parts = [piece[b : b + 1] for piece in pieces]
            ordered = [x.pick(parts, self.order(i, later)) for i in range(x.size)]
            row_sum = ordered[0]
            for piece in ordered[1:]:
                row_sum = row_sum * decay + piece
            out.append((ordered[:-1], row_sum, row_sum.astype(BF16)))
        return out

    def scan_middle(self, sums, decay, later):
        x, z = self.along_x, self.along_z
        row_decays = decay**x.size
        decay = decay[None, :, None, None]
        row_decay = decay**x.size
        pairs = [[(i, i + d) for i in range(z.size - d)] for d in (1, 2)]
        if later:
            pairs = [[(j, i) for i, j in moves] for moves in pairs]
        near = [z.send(low, pairs[0]) for _, _, low in sums]
        pair = [decayed_sum(row_sum, part, row_decays) for (_, row_sum, _), part in zip(sums, near)]
        far = [z.send(value, pairs[1]).astype(F32) for value in pair]
        near = [part.astype(F32) for part in near]
        out = []
        for (ordered, _, _), near_part, far_part in zip(sums, near, far):
            entering = [near_part + row_decay * far_part]
            for piece in ordered:
                entering.append(entering[-1] * decay + piece)

            def for_device(distance):
                target = self.order(lax.rem(x.here() + distance, x.size), later)
                value = entering[0]
                for i in range(1, x.size):
                    value = jnp.where(target == i, entering[i], value)
                return value

            out.append(
                [for_device(0)] + [for_device(d).astype(BF16) for d in range(1, x.size)]
            )
        return out

    def scan_end(self, shares):
        x = self.along_x
        out = []
        for own, *others in shares:
            back = [own] + [x.ring(part, d).astype(F32) for d, part in enumerate(others, 1)]
            out.append(jnp.concatenate([x.pick(back, i) for i in range(x.size)], axis=2))
        return jnp.concatenate(out, axis=0)

    def gains_x(self, gains):
        x, z = self.along_x, self.along_z
        slots = jnp.zeros((2, z.size, x.size, gains.shape[1]), gains.dtype)
        slots = lax.dynamic_update_slice(slots, gains[:, None, None], (0, z.here(), x.here(), 0))
        return x.total(slots.reshape(2, z.size, -1))

    def gains_z(self, slots):
        x, z = self.along_x, self.along_z
        slots = z.total(slots).reshape(2, z.size, x.size, -1)
        turned = [
            lax.dynamic_slice_in_dim(slots, lax.rem(x.here() + j, x.size), 1, 2)[:, :, 0]
            for j in range(x.size)
        ]
        return jnp.concatenate(turned, axis=1).reshape(2, -1)

    def sum_vectors(self, vectors):
        mine = vectors[:, 0]
        for part in self.scatter_x([vectors[:, j] for j in range(1, self.along_x.size)]):
            mine = mine + part
        return mine.reshape(mine.shape[0], self.along_z.size, -1).transpose(1, 0, 2)


CHEAP = pl.CostEstimate(flops=0, bytes_accessed=0, transcendentals=0)


def resident(array):
    if isinstance(array, Part):
        return pl.BlockSpec(
            array.shape, lambda *_: (0, array.index, 0), pipeline_mode=pl.Buffered(1)
        )
    return pl.BlockSpec(
        array.shape, lambda *_: (0,) * array.ndim, pipeline_mode=pl.Buffered(1)
    )


class Part:
    def __init__(self, array, index, count):
        self.array, self.index = array, index
        planes, rows, columns = array.shape
        self.shape, self.ndim, self.dtype = (planes, rows // count, columns), 3, array.dtype


def call(kernel, table, grid, arrays, specs, outs, out_specs, flops=0):
    return pl.pallas_call(
        kernel,
        grid_spec=pltpu.PrefetchScalarGridSpec(
            num_scalar_prefetch=1, grid=grid, in_specs=specs, out_specs=out_specs
        ),
        out_shape=[jax.ShapeDtypeStruct(*out) for out in outs],
        compiler_params=pltpu.CompilerParams(vmem_limit_bytes=VMEM_LIMIT),
        cost_estimate=pl.CostEstimate(flops=flops, bytes_accessed=0, transcendentals=0),
    )(table, *[array.array if isinstance(array, Part) else array for array in arrays])


def turn_kernel(table, in_ref, out_ref):
    width = in_ref.shape[1] // table.shape[0]
    for i in range(table.shape[0]):
        start = pl.multiple_of(table[i] * width, width)
        out_ref[:, i * width : (i + 1) * width] = in_ref[:, pl.ds(start, width)]


def turn(value, table):
    rows, width = value.shape
    tile = min(rows, 256)
    return pl.pallas_call(
        turn_kernel,
        grid_spec=pltpu.PrefetchScalarGridSpec(
            num_scalar_prefetch=1,
            grid=(rows // tile,),
            in_specs=[pl.BlockSpec((tile, width), lambda i, t: (i, 0))],
            out_specs=pl.BlockSpec((tile, width), lambda i, t: (i, 0)),
        ),
        out_shape=jax.ShapeDtypeStruct(value.shape, value.dtype),
        cost_estimate=CHEAP,
    )(table, value)


def norm_turn_kernel(table, in_ref, gain_ref, out_ref):
    width = in_ref.shape[1] // table.shape[0]
    values = in_ref[...].astype(F32)
    mean = jnp.mean(values, axis=-1, keepdims=True)
    centred = values - mean
    scale = lax.rsqrt(jnp.mean(centred * centred, axis=-1, keepdims=True) + 1e-05)
    for i in range(table.shape[0]):
        start = pl.multiple_of(table[i] * width, width)
        block = in_ref[:, pl.ds(start, width)].astype(F32)
        gain = gain_ref[:, i * width : (i + 1) * width]
        out_ref[:, i * width : (i + 1) * width] = ((block - mean) * scale * gain).astype(BF16)


def norm_turn(value, gain, table):
    rows, width = value.shape
    tile = min(rows, 256)
    return pl.pallas_call(
        norm_turn_kernel,
        grid_spec=pltpu.PrefetchScalarGridSpec(
            num_scalar_prefetch=1,
            grid=(rows // tile,),
            in_specs=[
                pl.BlockSpec((tile, width), lambda i, t: (i, 0)),
                pl.BlockSpec((1, width), lambda i, t: (0, 0)),
            ],
            out_specs=pl.BlockSpec((tile, width), lambda i, t: (i, 0)),
        ),
        out_shape=jax.ShapeDtypeStruct(value.shape, BF16),
        cost_estimate=CHEAP,
    )(table, value, gain.reshape(1, -1))


def silu_parts(values):
    sigmoid = 1.0 / (1.0 + jnp.exp(-values))
    return sigmoid, values * sigmoid


def norm_parts(values):
    centred = values - jnp.mean(values, axis=-1, keepdims=True)
    scale = lax.rsqrt(jnp.mean(centred * centred, axis=-1, keepdims=True) + 1e-05)
    return centred * scale, scale


def halves(values):
    high = values.astype(BF16)
    return high, (values - high.astype(F32)).astype(BF16)


def row_decay(log, rows, first, step):
    position = lax.broadcasted_iota(jnp.int32, (rows, 1), 0)
    return jnp.exp((first + step * position).astype(F32) * log)


def pair_decay(log, rows):
    row = lax.broadcasted_iota(jnp.int32, (rows, rows), 0)
    column = lax.broadcasted_iota(jnp.int32, (rows, rows), 1)
    offset = row - column
    return jnp.where(offset >= 0, jnp.exp(jnp.maximum(offset, 0).astype(F32) * log), 0.0)


def state_kernel(logs, key_ref, value_ref, state_ref):
    rows = key_ref.shape[0]
    scaled = key_ref[...].astype(F32) * row_decay(logs[pl.program_id(1)], rows, rows - 1, -1)
    high, low = halves(scaled)
    value = value_ref[...]
    state_ref[0, 0] = t_matmul(high, value) + t_matmul(low, value)


def mix_kernel(logs, query_ref, key_ref, value_ref, state_ref, swish_ref, gated_ref, mixed_ref):
    rows = key_ref.shape[0]
    log = logs[pl.program_id(1)]
    query = query_ref[...]
    weights = (matmul_t(query, key_ref[...]) * pair_decay(log, rows)).astype(BF16)
    high, low = halves(state_ref[0, 0])
    cross = matmul(query, high) + matmul(query, low)
    mixed = matmul(weights, value_ref[...]) + cross * row_decay(log, rows, 1, 1)
    mixed_ref[...] = mixed
    gated_ref[...] = (silu_parts(swish_ref[...])[1] * norm_parts(mixed)[0]).astype(BF16)


def gate_kernel(logs, *refs):
    (branch_ref, *output_refs), (swish_ref, mixed_ref, query_ref) = refs[:-6], refs[-6:-3]
    swish_low_ref, mixed_low_ref, state_ref = refs[-3:]
    rows = query_ref.shape[0]
    swish_pre = swish_ref[...]
    grad = from_columns(branch_ref[...], output_refs)
    normalized, scale = norm_parts(mixed_ref[...])
    sigmoid, silu = silu_parts(swish_pre)
    slope = sigmoid * (1.0 + swish_pre * (1.0 - sigmoid))
    swish_low_ref[...] = (grad * normalized * slope).astype(BF16)
    e = grad * silu
    mean = jnp.mean(e, axis=-1, keepdims=True)
    along = jnp.mean(e * normalized, axis=-1, keepdims=True)
    mixed_low = (scale * (e - mean - normalized * along)).astype(BF16)
    mixed_low_ref[...] = mixed_low
    scaled = query_ref[...].astype(F32) * row_decay(logs[pl.program_id(1)], rows, 1, 1)
    high, low = halves(scaled)
    state_ref[0, 0] = t_matmul(high, mixed_low) + t_matmul(low, mixed_low)


def mix_back_kernel(
    logs,
    query_ref,
    key_ref,
    value_ref,
    mixed_low_ref,
    state_ref,
    state_grad_ref,
    query_low_ref,
    key_low_ref,
    value_low_ref,
):
    rows = key_ref.shape[0]
    log = logs[pl.program_id(1)]
    query, key, value, mixed_low = (
        query_ref[...],
        key_ref[...],
        value_ref[...],
        mixed_low_ref[...],
    )
    decay = pair_decay(log, rows)
    weights = (matmul_t(query, key) * decay).astype(BF16)
    score = (matmul_t(mixed_low, value) * decay).astype(BF16)
    high, low = halves(state_ref[0, 0])
    cross = matmul_t(mixed_low, high) + matmul_t(mixed_low, low)
    query_low_ref[...] = (matmul(score, key) + cross * row_decay(log, rows, 1, 1)).astype(BF16)
    high, low = halves(state_grad_ref[0, 0])
    to_end = row_decay(log, rows, rows - 1, -1)
    cross = matmul_t(value, high) + matmul_t(value, low)
    key_low_ref[...] = (t_matmul(score, query) + cross * to_end).astype(BF16)
    cross = matmul(key, high) + matmul(key, low)
    value_low_ref[...] = (t_matmul(weights, mixed_low) + cross * to_end).astype(BF16)


def at_once(kernel, arrays, outs, table=None, flops=0):
    if table is None:
        table = jnp.zeros((1,), jnp.int32)
    return call(
        kernel,
        table,
        (1,),
        arrays,
        [resident(array) for array in arrays],
        outs,
        [pl.BlockSpec(shape, lambda i, _, n=len(shape): (0,) * n) for shape, _ in outs],
        flops,
    )


def add_blocks(own, arrived, extra=None, flops=0):
    count, rows, columns = own.shape
    more = () if extra is None else (extra,)
    below = 0 if extra is None else 16
    arrays, specs = [own], [pl.BlockSpec((1, rows, columns), lambda i, _: (i, 0, 0))]
    for parts in arrived:
        start = 0
        for part in parts if isinstance(parts, list) else [parts]:
            size = part.shape[0]
            arrays.append(part)
            specs.append(
                pl.BlockSpec(
                    (1, rows, columns),
                    lambda i, _, start=start, size=size: (jnp.clip(i - start, 0, size - 1), 0, 0),
                )
            )
            start += size
    sizes = [array.shape[0] for array in arrays[1:]]

    def kernel(_, *refs):
        step = pl.program_id(0)
        out = refs[0][...].astype(F32)
        start = 0
        for ref, size in zip(refs[1 : len(arrays)], sizes):
            part = ref[...].astype(F32)
            if size < count:
                part = jnp.where((step >= start) & (step < start + size), part, 0.0)
                start = (start + size) % count
            out = out + part
        refs[-1][:, :rows, :] = out.astype(BF16)
        if more:
            refs[-1][:, rows:, :] = refs[-2][...]

    if more:
        extra = jnp.pad(
            extra.astype(BF16),
            ((0, 0), (0, below - extra.shape[1]), (0, columns - extra.shape[2])),
        )
        more = (extra,)
    return call(
        kernel,
        jnp.zeros((1,), jnp.int32),
        (count,),
        [*arrays, *more],
        specs + [pl.BlockSpec((1, below, columns), lambda i, _: (i, 0, 0)) for _ in more],
        [((count, rows + below, columns), BF16)],
        [pl.BlockSpec((1, rows + below, columns), lambda i, _: (i, 0, 0))],
        flops,
    )[0]


def decayed_sum(own, before, decays):
    _, heads, rows, columns = own.shape

    def kernel(decays, own_ref, before_ref, out_ref):
        decay = decays[pl.program_id(0)]
        out_ref[...] = (own_ref[...] + decay * before_ref[...].astype(F32)).astype(BF16)

    block = pl.BlockSpec((1, 1, rows, columns), lambda h, _: (0, h, 0, 0))
    return call(
        kernel, decays, (heads,), [own, before], [block, block], [(own.shape, BF16)], [block],
        flops=3_000_000_000,
    )[0]


def order_blocks(first, blocks):
    count = len(blocks)
    shape = blocks[0].shape

    def kernel(first, *refs):
        for k in range(count):

            @pl.when(pl.program_id(0) == lax.rem(first[0] + k, count))
            def _(k=k):
                refs[-1][0] = refs[k][...]

    return call(
        kernel,
        first.astype(jnp.int32).reshape(1),
        (count,),
        blocks,
        [resident(block) for block in blocks],
        [((count, *shape), blocks[0].dtype)],
        [pl.BlockSpec((1, *shape), lambda i, _: (i, 0, 0))],
    )[0]


def fold_tiles(own, arrived, tiles, flops=0):
    rows, width = own.shape
    tile = rows // tiles
    piece = tile // 2

    def kernel(_, own_ref, *refs):
        outs = refs[len(arrived) :]
        for i in range(2 * tiles):
            value = own_ref[i * piece : (i + 1) * piece, :]
            for ref in refs[i : len(arrived) : 2 * tiles]:
                value = value + ref[...].astype(F32)
            if i < 2:
                outs[0][i * piece : (i + 1) * piece, :] = value
            else:
                outs[i - 1][...] = value.astype(BF16)

    mine, *pieces = at_once(
        kernel,
        [own, *arrived],
        [((tile, width), F32)] + [((piece, width), BF16)] * (2 * tiles - 2),
        flops=flops,
    )
    return mine, [pieces[2 * k : 2 * k + 2] for k in range(tiles - 1)]


def summed(mine_ref, refs, piece):
    rows = mine_ref.shape[0] // 2
    value = mine_ref[piece * rows : (piece + 1) * rows, :]
    for ref in refs[piece::2]:
        value = value + ref[...].astype(F32)
    return value


def enter_dense(mine, arrived, tokens, gain):
    rows, width = mine.shape
    half = rows // 2

    def kernel(_, mine_ref, tokens_ref, gain_ref, *refs):
        hidden_ref, *outs = refs[len(arrived) :]
        for i in range(2):
            part = slice(i * half, (i + 1) * half)
            hidden = tokens_ref[part, :].astype(F32) + summed(mine_ref, refs[: len(arrived)], i)
            hidden_ref[part, :] = hidden
            outs[i][...] = (norm_parts(hidden)[0] * gain_ref[...]).astype(BF16)

    hidden, *pieces = at_once(
        kernel,
        [mine, tokens, gain.reshape(1, -1), *arrived],
        [((rows, width), F32)] + [((half, width), BF16)] * 2,
    )
    return hidden, pieces


def leave_dense(mine, arrived, hidden):
    rows, width = mine.shape
    half = rows // 2

    def kernel(_, mine_ref, hidden_ref, *refs):
        for i in range(2):
            value = hidden_ref[i * half : (i + 1) * half, :] + summed(
                mine_ref, refs[: len(arrived)], i
            )
            refs[len(arrived) + i][...] = value.astype(BF16)

    return at_once(kernel, [mine, hidden, *arrived], [((half, width), BF16)] * 2)


def norm_backward(mine, arrived, values, gain, residual, keep):
    rows, width = mine.shape
    half = rows // 2

    def kernel(_, mine_ref, values_ref, gain_ref, residual_ref, *refs):
        gain_out, first, second, *whole = refs[len(arrived) :]
        gain_sum = 0.0
        for i in range(2):
            part = slice(i * half, (i + 1) * half)
            grad = summed(mine_ref, refs[: len(arrived)], i)
            normalized, scale = norm_parts(values_ref[part, :].astype(F32))
            gain_sum = gain_sum + jnp.sum(grad * normalized, axis=0, keepdims=True)
            e = grad * gain_ref[...]
            mean = jnp.mean(e, axis=-1, keepdims=True)
            along = jnp.mean(e * normalized, axis=-1, keepdims=True)
            out = residual_ref[part, :].astype(F32) + scale * (e - mean - normalized * along)
            (first, second)[i][...] = out.astype(BF16)
            for ref in whole:
                ref[part, :] = out
        gain_out[...] = gain_sum

    gain_part, first, second, *whole = at_once(
        kernel,
        [mine, values, gain.reshape(1, -1), residual, *arrived],
        [((1, width), F32)]
        + [((half, width), BF16)] * 2
        + [((rows, width), F32)] * (1 if keep else 0),
    )
    return gain_part, [first, second], *whole


def place_tiles(table, near, far, kind):
    tiles = len(near)
    pieces = [piece for tile in near + far for piece in tile]
    piece, width = pieces[0].shape
    columns = table.shape[0] - 2
    block = width // columns

    def kernel(table, *refs):
        out_ref = refs[-1]
        step = pl.program_id(0)
        for i in range(2 * tiles):
            core = lax.rem(table[0] + i // tiles, CORES)
            row = lax.rem(table[1] + i % tiles, tiles)

            @pl.when(step == core * tiles + row)
            def _(i=i):
                for part in range(2):
                    ref = refs[2 * i + part]
                    for j in range(columns):
                        start = pl.multiple_of(table[2 + j] * block, block)
                        out_ref[
                            part * piece : (part + 1) * piece, j * block : (j + 1) * block
                        ] = ref[:, pl.ds(start, block)].astype(kind)

    return call(
        kernel,
        table,
        (CORES * tiles,),
        pieces,
        [resident(ref) for ref in pieces],
        [((2 * CORES * tiles * piece, width), kind)],
        [pl.BlockSpec((2 * piece, width), lambda i, _: (i, 0))],
    )[0]


def by_rows(ref):
    return ref[...].reshape(-1, ref.shape[2])


def from_columns(values, refs):
    out, start = 0.0, 0
    for ref in refs:
        weight = jnp.concatenate([ref[k] for k in range(ref.shape[0])], axis=1)
        stop = start + weight.shape[1]
        out = out + matmul_t(values[:, start:stop], weight)
        start = stop
    return out


def project(values, weight, kind):
    rows, width = values.shape
    tile = min(rows, 256)
    columns = weight[0].shape[2]

    def kernel(_, in_ref, *refs):
        depth = width // len(weight)
        out = matmul(in_ref[:, :depth], by_rows(refs[0]))
        for j in range(1, len(weight)):
            out = out + matmul(in_ref[:, j * depth : (j + 1) * depth], by_rows(refs[j]))
        refs[-1][...] = out.astype(kind)

    return call(
        kernel,
        jnp.zeros((1,), jnp.int32),
        (rows // tile,),
        [values, *weight],
        [pl.BlockSpec((tile, width), lambda i, _: (i, 0))] + [resident(w) for w in weight],
        [((rows, columns), kind)],
        [pl.BlockSpec((tile, columns), lambda i, _: (i, 0))],
    )[0]


def parts_by_rows(compute, table, model_width, arrays, specs, outs, out_specs):
    count = table.shape[0]
    rows = arrays[0].shape[0]
    tile = rows // count
    away = count - count // CORES
    half = tile // 2

    def kernel(table, *refs):
        step = pl.program_id(0)
        pieces, own_ref = refs[-2 * away - 1 : -1], refs[-1]
        value = compute(*refs[: -2 * away - 1])
        for i in range(away):

            @pl.when(step == i)
            def _(i=i):
                pieces[2 * i][...] = value[:half].astype(BF16)
                pieces[2 * i + 1][...] = value[half:].astype(BF16)

        @pl.when(step >= away)
        def _():
            own_ref[...] = value

    *results, own = call(
        kernel,
        table,
        (count,),
        arrays,
        specs,
        outs + [((half, model_width), BF16)] * (2 * away) + [(((count - away) * tile, model_width), F32)],
        out_specs
        + [pl.BlockSpec((half, model_width), lambda i, t: (0, 0))] * (2 * away)
        + [pl.BlockSpec((tile, model_width), lambda i, t: (jnp.maximum(i - away, 0), 0))],
    )
    return *results[: len(outs)], results[len(outs) :], own


def tile_of(array, table):
    return pl.BlockSpec(
        (array.shape[0] // table.shape[0], array.shape[1]), lambda i, t: (t[i], 0)
    )


def to_columns(values, weight, table):
    def compute(in_ref, *refs):
        value = in_ref[...]
        return jnp.concatenate(
            [matmul(value, ref[k]) for ref in refs for k in range(ref.shape[0])], axis=1
        )

    return parts_by_rows(
        compute,
        table,
        sum(w.shape[0] * w.shape[2] for w in weight),
        [values, *weight],
        [tile_of(values, table)] + [resident(w) for w in weight],
        [],
        [],
    )


def dense_forward(dense_in, gate, up):
    rows, width = dense_in.shape
    tile = min(rows, 256)
    units = gate[0].shape[2]

    def kernel(_, in_ref, *refs):
        gate_refs, up_refs = refs[: len(gate)], refs[len(gate) : -3]
        depth = width // len(gate)
        pre = []
        for weights in (gate_refs, up_refs):
            out = 0.0
            for j, ref in enumerate(weights):
                out = out + matmul(in_ref[:, j * depth : (j + 1) * depth], by_rows(ref))
            pre.append(out)
        refs[-3][...], refs[-2][...] = pre
        refs[-1][...] = (gelu_parts(pre[0])[0] * pre[1]).astype(BF16)

    block = pl.BlockSpec((tile, units), lambda i, _: (i, 0))
    return call(
        kernel,
        jnp.zeros((1,), jnp.int32),
        (rows // tile,),
        [dense_in, *gate, *up],
        [pl.BlockSpec((tile, width), lambda i, _: (i, 0))] + [resident(w) for w in (*gate, *up)],
        [((rows, units), F32), ((rows, units), F32), ((rows, units), BF16)],
        [block] * 3,
    )


def dense_backward(grad_out, gate_pre, up_pre, down, gate, up, table):
    units = gate_pre.shape[1]

    def compute(grad_ref, gate_pre_ref, up_pre_ref, *refs):
        count = len(down)
        down_refs, gate_refs, up_refs = (refs[i * count : (i + 1) * count] for i in range(3))
        gate_low_ref, up_low_ref = refs[3 * count :]
        grad = from_columns(grad_ref[...], down_refs).astype(BF16).astype(F32)
        act, slope = gelu_parts(gate_pre_ref[...])
        gate_low = (grad * up_pre_ref[...] * slope).astype(BF16)
        up_low = (grad * act).astype(BF16)
        gate_low_ref[...] = gate_low
        up_low_ref[...] = up_low
        return jnp.concatenate(
            [
                matmul_t(gate_low, by_rows(g)) + matmul_t(up_low, by_rows(u))
                for g, u in zip(gate_refs, up_refs)
            ],
            axis=1,
        )

    weights = [*down, *gate, *up]
    tiles = [grad_out, gate_pre, up_pre]
    return parts_by_rows(
        compute,
        table,
        grad_out.shape[1],
        tiles + weights,
        [tile_of(a, table) for a in tiles]
        + [resident(w) for w in weights],
        [((gate_pre.shape[0], units), BF16)] * 2,
        [tile_of(gate_pre, table)] * 2,
    )


def to_rows(values, weights, table):
    counts = [len(group) for group in values]
    blocks = len(weights[0])

    def compute(*refs):
        refs = list(refs)
        inputs = []
        for count in counts:
            group = [refs.pop(0)[...] for _ in range(count)]
            inputs.append(group[0] if count == 1 else jnp.concatenate(group, axis=1))
        outs = [0.0] * blocks
        for value in inputs:
            for j in range(blocks):
                outs[j] = outs[j] + matmul_t(value, by_rows(refs.pop(0)))
        return jnp.concatenate(outs, axis=1)

    flat = [value for group in values for value in group]
    every = [w for weight in weights for w in weight]
    model_width = sum(w.shape[0] * w.shape[1] for w in weights[0])
    return parts_by_rows(
        compute,
        table,
        model_width,
        flat + every,
        [tile_of(value, table) for value in flat] + [resident(w) for w in every],
        [],
        [],
    )


def grad_by_rows(left, rights, plan, own=True, others=True, pieces=1):
    rows, width = left.shape
    x, z = plan.along_x.size, plan.along_z.size
    block = width // (x * z)
    columns = sum(right.shape[1] for right in rights)
    half = z // 2
    away = 2 * (x - 1) if others else 0
    steps = away + (2 if own else 0)
    first = 0 if own and not others else 2

    def kernel(_, left_ref, *refs):
        step = pl.program_id(0)
        value = []
        for right_ref in refs[: len(rights)]:
            value.append(t_matmul(left_ref[...], right_ref[...]))
        value = value[0] if len(value) == 1 else jnp.concatenate(value, axis=1)
        value = value.astype(BF16).reshape(half, block, columns)
        outs = refs[len(rights) :]
        for i in range(away):

            @pl.when(step == i)
            def _(i=i):
                outs[i * pieces // 2][...] = value

        if own:

            @pl.when(step >= away)
            def _():
                outs[-1][...] = value

    piece = (half, block, columns)
    results = call(
        kernel,
        jnp.zeros((1,), jnp.int32),
        (steps,),
        [left, *rights],
        [pl.BlockSpec((rows, half * block), lambda i, _: (0, lax.rem(i + first, 2 * x)))]
        + [resident(right) for right in rights],
        [((z // pieces, block, columns), BF16)] * (away * pieces // 2)
        + [((z, block, columns), BF16)] * own,
        [
            pl.BlockSpec(piece, lambda i, _, j=j: (jnp.clip(i - 2 * j, 0, 1) if pieces == 1 else 0, 0, 0))
            for j in range(away * pieces // 2)
        ]
        + [pl.BlockSpec(piece, lambda i, _: (jnp.maximum(i - away, 0), 0, 0))] * own,
    )
    if not others:
        return results[0]
    parts = list(results[: away * pieces // 2])
    if pieces == 2:
        parts = [parts[2 * j : 2 * j + 2] for j in range(x - 1)]
    return (results[-1], parts) if own else parts


def grad_by_columns(left, right, plan, pieces=1):
    rows, units = left.shape
    x, z = plan.along_x.size, plan.along_z.size
    block = right.shape[1] // (x * z)
    tile = min(units, 512)
    half = z // pieces

    def kernel(_, left_ref, right_ref, own_ref, *other_refs):
        value = t_matmul(left_ref[...], right_ref[...])
        for i in range(x * z):
            part = value[:, i * block : (i + 1) * block].astype(BF16)
            if i < z:
                own_ref[i] = part
            else:
                other_refs[(i - z) // half][(i - z) % half] = part

    own, *others = call(
        kernel,
        jnp.zeros((1,), jnp.int32),
        (units // tile,),
        [left, right],
        [pl.BlockSpec((rows, tile), lambda i, _: (0, i)), resident(right)],
        [((z, units, block), BF16)] + [((half, units, block), BF16)] * (pieces * (x - 1)),
        [pl.BlockSpec((z, tile, block), lambda i, _: (0, i, 0))]
        + [pl.BlockSpec((half, tile, block), lambda i, _: (0, i, 0))] * (pieces * (x - 1)),
    )
    if pieces == 2:
        others = [others[2 * j : 2 * j + 2] for j in range(x - 1)]
    return own, others


def gelu_parts(values):
    root = 0.7978845608028654
    inner = jnp.tanh(root * (values + 0.044715 * (values * values * values)))
    half = 0.5 * (1.0 + inner)
    slope = half + 0.5 * values * (1.0 - inner * inner) * root * (
        1.0 + 3 * 0.044715 * (values * values)
    )
    return values * half, slope


class Heads:
    def __init__(self, logs, seqs, rows):
        self.logs, self.seqs, self.rows = logs, seqs, rows
        self.heads = logs.shape[0]

    def flat(self, array, width, first):
        return array, pl.BlockSpec((self.rows, width), lambda b, h, _: (b, first + h))

    def whole(self, array):
        return array, pl.BlockSpec((self.rows, array.shape[1]), lambda b, h, _: (b, 0))

    def rows_of(self, weight):
        count, _, width = weight.shape
        return weight, pl.BlockSpec((count, VD, width), lambda b, h, _: (0, h, 0))

    def state(self, array):
        return array, pl.BlockSpec((1, 1, QK, VD), lambda b, h, _: (b, h, 0, 0))

    def call(self, kernel, inputs, outs):
        shapes, specs = [], []
        for width, kind in outs:
            if width is None:
                shapes.append(((self.seqs, self.heads, QK, VD), kind))
                specs.append(self.state(None)[1])
            else:
                shapes.append(((self.seqs * self.rows, self.heads * width), kind))
                specs.append(self.flat(None, width, 0)[1])
        return call(
            kernel,
            self.logs,
            (self.seqs, self.heads),
            [array for array, _ in inputs],
            [spec for _, spec in inputs],
            shapes,
            specs,
        )


def matmul(left, right):
    return jnp.dot(left, right, preferred_element_type=F32)


def matmul_t(left, right):
    return lax.dot_general(left, right, (((1,), (1,)), ((), ())), preferred_element_type=F32)


def t_matmul(left, right):
    return lax.dot_general(left, right, (((0,), (0,)), ((), ())), preferred_element_type=F32)


class Live:
    def fence(self):
        names = list(vars(self))
        values = lax.optimization_barrier([getattr(self, name) for name in names])
        for name, value in zip(names, values):
            setattr(self, name, value)


def added(blocks):
    count, rows, columns = blocks.shape
    parts = 2 if rows % 32 == 0 else 1

    def kernel(_, in_ref, out_ref):
        out = in_ref[0].astype(F32)
        for k in range(1, count):
            out = out + in_ref[k].astype(F32)
        out_ref[...] = out

    return call(
        kernel,
        jnp.zeros((1,), jnp.int32),
        (parts,),
        [blocks],
        [pl.BlockSpec((count, rows // parts, columns), lambda i, _: (0, i, 0))],
        [((rows, columns), F32)],
        [pl.BlockSpec((rows // parts, columns), lambda i, _: (i, 0))],
    )[0]


def added_last(blocks, rows, width):
    count = blocks.shape[0]

    def kernel(_, in_ref, first_ref, second_ref, vectors_ref):
        out = in_ref[0].astype(F32)
        for k in range(1, count):
            out = out + in_ref[k].astype(F32)
        first_ref[...] = out[:rows, :width]
        second_ref[...] = out[:rows, width:]
        vectors_ref[...] = out[rows : rows + 8, :rows]

    return at_once(
        kernel, [blocks], [((rows, width), F32), ((rows, width), F32), ((8, rows), F32)]
    )


def on_device(
    plan,
    tokens,
    pre_gain,
    query_weight,
    key_weight,
    value_weight,
    swish_weight,
    output_weight,
    mid_gain,
    gate_weight,
    up_weight,
    down_weight,
    cotangent,
):
    seq_count, seg_rows, model_width = tokens.shape
    row_count = seq_count * seg_rows
    to_slots, to_owners, table = plan.slot_owner(), plan.owner_slot(), plan.row_tiles()
    e = Live()
    e.tokens = tokens.reshape(row_count, model_width)
    e.cotangent = cotangent.reshape(row_count, model_width)
    key_width = query_weight.shape[1]
    local_heads = key_width // QK
    copies, blocks_x = plan.copies, plan.along_x.size
    along_z, along_core, along_y = plan.along_z, plan.along_core, plan.along_y
    def parts_of(array):
        return [Part(array, j, blocks_x) for j in range(blocks_x)]

    head_index = (lax.axis_index("shard") * local_heads + jnp.arange(local_heads)).astype(F32)
    logs = jnp.log1p(-jnp.exp2(-5.0 - head_index))
    carry_scale = jnp.exp(seg_rows * logs)
    each = Heads(logs, seq_count, seg_rows)

    e.value = plan.gather_z(value_weight)
    e.gains = plan.gains_x(jnp.stack([pre_gain, mid_gain]).astype(BF16))
    e.query_key = copies(jnp.concatenate([query_weight, key_weight], axis=1))
    e.down = plan.gather_x(down_weight)
    e.grad_out = turn(e.cotangent, to_slots)
    del e.cotangent
    e.own_tokens = turn(plan.own_rows(e.tokens), to_slots)
    e.fence()
    e.value = plan.gather_x(order_blocks(along_z.here(), e.value))
    e.query_key = along_z.exchange(e.query_key)
    e.own_grad_out = plan.own_rows(e.grad_out)
    gains = plan.gains_z(e.gains).astype(F32)
    e.full_pre, e.full_mid = gains[0], gains[1]
    del e.gains
    e.swish = swish_weight
    e.fence()
    e.query_key = plan.gather_x(e.query_key)
    e.swish = plan.gather_z(e.swish)
    e.output = copies(output_weight)
    e.mixer_in = norm_turn(e.tokens, e.full_pre, to_slots)
    del e.tokens
    e.values = project(e.mixer_in, e.value, BF16)
    e.fence()
    output_z = along_z.exchange(e.output)
    del e.output
    e.swish = order_blocks(along_z.here(), e.swish)
    e.queries_keys = project(e.mixer_in, e.query_key, BF16)
    (state,) = each.call(
        state_kernel,
        [each.flat(e.queries_keys, QK, local_heads), each.flat(e.values, VD, 0)],
        [(None, F32)],
    )
    e.state = plan.scan_begin(state)
    e.fence()
    swish_x = plan.gather_x(e.swish)
    del e.swish
    e.output = output_z
    e.gate = copies(gate_weight)
    e.state = plan.scan_sums(e.state, carry_scale, False)
    e.fence()
    e.output_first = plan.gather_x(e.output[:1])[1:]
    e.state = plan.scan_middle(e.state, carry_scale, False)
    e.swish = swish_x
    e.fence()
    gate_z = along_z.exchange(e.gate)
    del e.gate
    e.state = plan.scan_end(e.state)
    e.fence()
    output_x = [e.output]
    for parts in zip(e.output_first, plan.gather_x(e.output[1:])[1:]):
        output_x += parts
    del e.output, e.output_first
    e.gate = gate_z
    e.swish_pre = project(e.mixer_in, e.swish, F32)
    e.gated, e.mixed = each.call(
        mix_kernel,
        [
            each.flat(e.queries_keys, QK, 0),
            each.flat(e.queries_keys, QK, local_heads),
            each.flat(e.values, VD, 0),
            each.state(e.state),
            each.flat(e.swish_pre, VD, 0),
        ],
        [(VD, BF16), (VD, F32)],
    )
    e.up = copies(up_weight)
    e.fence()
    e.up = along_z.exchange(e.up)
    e.gate = plan.gather_x(e.gate)
    branch_others, branch_own = to_columns(e.gated, output_x, table)
    e.output = output_x
    mine, pieces = fold_tiles(
        branch_own, plan.sum_cores(branch_others), along_y.size, flops=9_000_000_000
    )
    e.mine, e.arrived = mine, plan.sum_y(pieces)
    e.down = copies(jnp.concatenate(e.down, axis=0))
    e.fence()
    down_z = along_z.exchange(e.down)
    del e.down
    up_x = plan.gather_x(e.up)
    del e.up
    e.hidden_state, dense_own = enter_dense(e.mine, e.arrived, e.own_tokens, e.full_mid)
    del e.mine, e.arrived
    e.dense_tiles = plan.share_y(dense_own)
    e.fence()
    e.dense_in = plan.share_cores(e.dense_tiles, BF16)
    del e.dense_tiles
    e.up = up_x
    e.fence()
    e.gate_pre, e.up_pre, e.inner_act = dense_forward(e.dense_in, e.gate, e.up)
    e.down_own, e.down_others = grad_by_columns(e.inner_act, e.grad_out, plan)
    e.fence()
    down_x = plan.scatter_x(e.down_others)
    del e.down_others
    e.down = down_z
    e.fence()
    e.gate_low, e.up_low, e.part_others, e.part_own = dense_backward(
        e.grad_out, e.gate_pre, e.up_pre, parts_of(e.down), e.gate, e.up, table
    )
    del e.gate_pre, e.up_pre, e.gate, e.up, e.grad_out
    e.fence()
    e.gate_others = grad_by_rows(e.dense_in, [e.gate_low], plan, own=False)
    e.fence()
    gate_x = plan.scatter_x(e.gate_others)
    del e.gate_others
    e.down_sum = add_blocks(e.down_own, down_x)
    del e.down_own
    e.fence()
    down_z = along_z.exchange(e.down_sum)
    del e.down_sum
    e.part_others = plan.sum_cores(e.part_others)
    e.gate_own = grad_by_rows(e.dense_in, [e.gate_low], plan, others=False)
    del e.gate_low
    e.fence()
    mine, pieces = fold_tiles(e.part_own, e.part_others, along_y.size)
    e.mine, e.arrived = mine, plan.sum_y(pieces)
    del e.part_own, e.part_others
    e.up_own, e.up_others = grad_by_rows(e.dense_in, [e.up_low], plan)
    del e.dense_in, e.up_low
    e.fence()
    e.mid_part, branch_own, e.hidden_grad = norm_backward(
        e.mine, e.arrived, e.hidden_state, e.full_mid, e.own_grad_out, True
    )
    del e.mine, e.arrived, e.own_grad_out
    e.branch_own = branch_own
    e.gate_sum = add_blocks(e.gate_own, gate_x, flops=12_000_000_000)
    del e.gate_own
    e.down_sum = down_z
    e.fence()
    gate_z = along_z.exchange(e.gate_sum)
    del e.gate_sum
    up_x = plan.scatter_x(e.up_others)
    del e.up_others
    e.branch_tiles = plan.share_y(e.branch_own)
    del e.branch_own
    e.out_others, e.out_own = to_columns(e.inner_act, parts_of(e.down), table)
    del e.inner_act, e.down
    e.fence()
    e.branch_low = plan.share_cores(e.branch_tiles, BF16)
    del e.branch_tiles
    e.output_own, e.output_others = grad_by_columns(e.gated, e.branch_low, plan, pieces=2)
    del e.gated
    e.up_sum = add_blocks(e.up_own, up_x, flops=12_000_000_000)
    del e.up_own
    e.gate_sum = gate_z
    e.fence()
    up_z = along_z.exchange(e.up_sum)
    del e.up_sum
    e.output_first = plan.scatter_x([part[0] for part in e.output_others])
    e.output_others = [part[1] for part in e.output_others]
    e.swish_low, e.mixed_low, e.state_grad = each.call(
        gate_kernel,
        [
            each.whole(e.branch_low),
            *[each.rows_of(weight) for weight in e.output],
            each.flat(e.swish_pre, VD, 0),
            each.flat(e.mixed, VD, 0),
            each.flat(e.queries_keys, QK, 0),
        ],
        [(VD, BF16), (VD, BF16), (None, F32)],
    )
    del e.swish_pre, e.mixed, e.output, e.branch_low
    e.fence()
    e.swish_own, e.swish_others = grad_by_rows(e.mixer_in, [e.swish_low], plan, pieces=2)
    e.state_grad = plan.scan_begin(e.state_grad)
    e.out_others = plan.sum_cores(e.out_others)
    e.fence()
    output_x = plan.scatter_x(e.output_others)
    del e.output_others
    e.mine, e.pieces = fold_tiles(e.out_own, e.out_others, along_y.size)
    del e.out_own, e.out_others
    e.state_grad = plan.scan_sums(e.state_grad, carry_scale, True)
    e.up_sum = up_z
    e.fence()
    e.swish_first = plan.scatter_x([part[0] for part in e.swish_others])
    e.swish_others = [part[1] for part in e.swish_others]
    e.state_grad = plan.scan_middle(e.state_grad, carry_scale, True)
    output_x = [list(parts) for parts in zip(e.output_first, output_x)]
    e.output_sum = add_blocks(e.output_own, output_x, flops=14_000_000_000)
    del e.output_own, e.output_first
    e.fence()
    output_z = along_z.exchange(e.output_sum)
    del e.output_sum
    e.state_grad = plan.scan_end(e.state_grad)
    e.fence()
    swish_x = plan.scatter_x(e.swish_others)
    del e.swish_others
    e.query_low, e.key_low, e.value_low = each.call(
        mix_back_kernel,
        [
            each.flat(e.queries_keys, QK, 0),
            each.flat(e.queries_keys, QK, local_heads),
            each.flat(e.values, VD, 0),
            each.flat(e.mixed_low, VD, 0),
            each.state(e.state),
            each.state(e.state_grad),
        ],
        [(QK, BF16), (QK, BF16), (VD, BF16)],
    )
    del e.state, e.state_grad, e.mixed_low, e.queries_keys, e.values
    e.value_own, e.value_others = grad_by_rows(e.mixer_in, [e.value_low], plan)
    e.arrived = plan.sum_y(e.pieces)
    del e.pieces
    e.fence()
    swish_x = [list(parts) for parts in zip(e.swish_first, swish_x)]
    e.swish_sum = add_blocks(e.swish_own, swish_x)
    del e.swish_own, e.swish_first
    e.output_sum = output_z
    e.fence()
    swish_z = along_z.exchange(e.swish_sum)
    del e.swish_sum
    value_x = plan.scatter_x(e.value_others)
    del e.value_others
    e.part_others, e.part_own = to_rows(
        [[e.query_low, e.key_low], [e.value_low], [e.swish_low]],
        [e.query_key, e.value, e.swish],
        table,
    )
    del e.value_low, e.swish_low, e.query_key, e.value, e.swish
    e.layer_tiles = plan.share_y(leave_dense(e.mine, e.arrived, e.hidden_state))
    del e.mine, e.arrived, e.hidden_state
    e.fence()
    e.query_key_own, e.query_key_others = grad_by_rows(
        e.mixer_in, [e.query_low, e.key_low], plan
    )
    del e.query_low, e.key_low, e.mixer_in
    query_key_x = plan.scatter_x(e.query_key_others)
    del e.query_key_others
    e.part_others = plan.sum_cores(e.part_others)
    e.value_sum = add_blocks(e.value_own, value_x, flops=12_000_000_000)
    del e.value_own
    e.fence()
    e.swish_sum = swish_z
    e.fence()
    value_z = along_z.exchange(e.value_sum)
    del e.value_sum
    e.mine, pieces = fold_tiles(e.part_own, e.part_others, along_y.size)
    e.arrived = plan.sum_y(pieces)
    del e.part_own, e.part_others
    e.down_sum = added(e.down_sum)
    e.gate_sum = added(e.gate_sum)
    e.up_sum = added(e.up_sum)
    e.fence()
    e.pre_part, e.tokens_own = norm_backward(
        e.mine, e.arrived, e.own_tokens, e.full_pre, e.hidden_grad, False
    )
    del e.mine, e.arrived, e.own_tokens, e.hidden_grad
    vectors = jnp.stack([e.mid_part, e.pre_part]).reshape(2, blocks_x, -1)
    vectors = plan.sum_vectors(along_y.total(along_core.total(vectors)))
    del e.mid_part, e.pre_part
    e.query_key_sum = add_blocks(
        e.query_key_own, query_key_x, vectors, flops=12_000_000_000
    )
    del e.query_key_own
    e.value_sum = value_z
    e.fence()
    e.layer_out = plan.share_cores(e.layer_tiles, BF16, to_owners)
    e.tokens_grad = plan.share_cores(plan.share_y(e.tokens_own), F32, to_owners)
    last = along_z.exchange(e.query_key_sum)
    query_grad, key_grad, vectors = added_last(last, pre_gain.shape[0], key_width)
    return (
        e.layer_out.reshape(tokens.shape),
        e.tokens_grad.reshape(tokens.shape),
        vectors[1],
        query_grad,
        key_grad,
        added(e.value_sum),
        added(e.swish_sum),
        added(e.output_sum),
        vectors[0],
        e.gate_sum,
        e.up_sum,
        e.down_sum,
    )


def solution(mesh):
    rows, weight, turned, vector = (
        P(None, "seq", None),
        P("seq", "shard"),
        P("shard", "seq"),
        P("seq"),
    )
    return jax.shard_map(
        functools.partial(on_device, Plan(mesh)),
        mesh=mesh,
        in_specs=(
            rows,
            vector,
            weight,
            weight,
            weight,
            weight,
            turned,
            vector,
            weight,
            weight,
            turned,
            rows,
        ),
        out_specs=(
            rows,
            rows,
            vector,
            weight,
            weight,
            weight,
            weight,
            turned,
            vector,
            weight,
            weight,
            turned,
        ),
        check_vma=False,
    )
```

```python
import functools

import jax
import jax.numpy as jnp
from jax import lax
from jax.experimental import pallas as pl
from jax.experimental.pallas import tpu as pltpu
from jax.sharding import PartitionSpec as P

QK = 256
VD = 512
CHIPS_Z = 4
CORES = 2
F32 = jnp.float32
BF16 = jnp.bfloat16
VMEM_LIMIT = 52 * 1024 * 1024


class Line:
    def __init__(self, axis, total, size, stride):
        self.axis, self.size, self.stride = axis, size, stride
        self.starts = [i for i in range(total) if (i // stride) % size == 0]

    def here(self):
        return lax.rem(lax.div(lax.axis_index(self.axis), self.stride), self.size)

    def send(self, value, moves):
        pairs = [(o + i * self.stride, o + j * self.stride) for i, j in moves for o in self.starts]
        return lax.ppermute(value, self.axis, pairs)

    def ring(self, value, distance):
        return self.send(value, [(i, (i + distance) % self.size) for i in range(self.size)])

    def exchange(self, blocks):
        groups = [[o + i * self.stride for i in range(self.size)] for o in self.starts]
        return lax.all_to_all(
            blocks, self.axis, split_axis=0, concat_axis=0, axis_index_groups=groups, tiled=True
        )

    def total(self, value):
        every = [value] + [self.ring(value, d) for d in range(1, self.size)]
        if self.size == 2:
            return every[0] + every[1]
        out = 0.0
        for position in range(self.size):
            out = out + self.pick(every, position)
        return out

    def pick(self, every, position):
        out = every[0]
        for d in range(1, self.size):
            source = lax.rem(self.here() - d + self.size, self.size)
            out = jnp.where(source == position, every[d], out)
        return out


class Plan:
    def __init__(self, mesh):
        seq, shard = mesh.shape["seq"], mesh.shape["shard"]
        self.seq, self.shard = seq, shard
        self.along_x = Line("seq", seq, seq // CHIPS_Z, 1)
        self.along_z = Line("seq", seq, CHIPS_Z, seq // CHIPS_Z)
        self.along_core = Line("shard", shard, CORES, 1)
        self.along_y = Line("shard", shard, shard // CORES, CORES)

    def slot_owner(self):
        x, z = self.along_x, self.along_z
        return jnp.stack(
            [
                k * x.size + lax.rem(x.here() + j, x.size)
                for j in range(x.size)
                for k in range(z.size)
            ]
        ).astype(jnp.int32)

    def owner_slot(self):
        x, z = self.along_x, self.along_z
        return jnp.stack(
            [
                lax.rem(x.size + j - x.here(), x.size) * z.size + k
                for k in range(z.size)
                for j in range(x.size)
            ]
        ).astype(jnp.int32)

    def row_tiles(self):
        core, y = self.along_core, self.along_y
        return jnp.stack(
            [
                lax.rem(core.here() + j, core.size) * y.size + lax.rem(y.here() + k, y.size)
                for j in (*range(1, core.size), 0)
                for k in range(y.size)
            ]
        ).astype(jnp.int32)

    def own_rows(self, whole):
        core, y = self.along_core, self.along_y
        step = whole.shape[0] // self.shard
        return lax.dynamic_slice_in_dim(whole, (core.here() * y.size + y.here()) * step, step, 0)

    def copies(self, own):
        def kernel(_, in_ref, out_ref):
            out_ref[0] = in_ref[...]

        return call(
            kernel,
            jnp.zeros((1,), jnp.int32),
            (self.along_z.size,),
            [own],
            [resident(own)],
            [((self.along_z.size, *own.shape), own.dtype)],
            [pl.BlockSpec((1, *own.shape), lambda i, _: (i, 0, 0))],
        )[0]

    def gather_z(self, own):
        return [own] + [self.along_z.ring(own, -k) for k in range(1, self.along_z.size)]

    def gather_x(self, row):
        return [row] + [self.along_x.ring(row, -j) for j in range(1, self.along_x.size)]

    def scatter_x(self, others):
        return [self.along_x.ring(part, j) for j, part in enumerate(others, 1)]

    def sum_cores(self, others):
        core = self.along_core
        return [core.ring(piece, d) for d in range(1, core.size) for piece in others]

    def sum_y(self, pieces):
        y = self.along_y
        return [y.ring(piece, k) for k, group in enumerate(pieces, 1) for piece in group]

    def share_y(self, pieces):
        y = self.along_y
        return [pieces] + [[y.ring(piece, -k) for piece in pieces] for k in range(1, y.size)]

    def share_cores(self, tiles, kind, columns=None):
        core, y = self.along_core, self.along_y
        others = [[core.ring(piece, 1) for piece in pieces] for pieces in tiles]
        here = jnp.stack([core.here(), y.here()]).astype(jnp.int32)
        if columns is None:
            columns = jnp.zeros((1,), jnp.int32)
        return place_tiles(jnp.concatenate([here, columns]), tiles, others, kind)

    def scan_begin(self, own):
        x = self.along_x
        step = own.shape[2] // x.size

        def part_for(distance):
            index = lax.rem(x.here() + distance, x.size) * step
            return lax.dynamic_slice_in_dim(own, index, step, 2)

        return [part_for(0)] + [
            x.ring(part_for(d).astype(BF16), d).astype(F32) for d in range(1, x.size)
        ]

    def order(self, device, later):
        return self.along_x.size - 1 - device if later else device

    def scan_sums(self, pieces, decay, later):
        x = self.along_x
        decay = decay[None, :, None, None]
        out = []
        for b in range(pieces[0].shape[0]):
            parts = [piece[b : b + 1] for piece in pieces]
            ordered = [x.pick(parts, self.order(i, later)) for i in range(x.size)]
            row_sum = ordered[0]
            for piece in ordered[1:]:
                row_sum = row_sum * decay + piece
            out.append((ordered[:-1], row_sum, row_sum.astype(BF16)))
        return out

    def scan_middle(self, sums, decay, later):
        x, z = self.along_x, self.along_z
        row_decays = decay**x.size
        decay = decay[None, :, None, None]
        row_decay = decay**x.size
        pairs = [[(i, i + d) for i in range(z.size - d)] for d in (1, 2)]
        if later:
            pairs = [[(j, i) for i, j in moves] for moves in pairs]
        near = [z.send(low, pairs[0]) for _, _, low in sums]
        pair = [decayed_sum(row_sum, part, row_decays) for (_, row_sum, _), part in zip(sums, near)]
        far = [z.send(value, pairs[1]).astype(F32) for value in pair]
        near = [part.astype(F32) for part in near]
        out = []
        for (ordered, _, _), near_part, far_part in zip(sums, near, far):
            entering = [near_part + row_decay * far_part]
            for piece in ordered:
                entering.append(entering[-1] * decay + piece)

            def for_device(distance):
                target = self.order(lax.rem(x.here() + distance, x.size), later)
                value = entering[0]
                for i in range(1, x.size):
                    value = jnp.where(target == i, entering[i], value)
                return value

            out.append(
                [for_device(0)] + [for_device(d).astype(BF16) for d in range(1, x.size)]
            )
        return out

    def scan_end(self, shares):
        x = self.along_x
        out = []
        for own, *others in shares:
            back = [own] + [x.ring(part, d).astype(F32) for d, part in enumerate(others, 1)]
            out.append(jnp.concatenate([x.pick(back, i) for i in range(x.size)], axis=2))
        return jnp.concatenate(out, axis=0)

    def gains_x(self, gains):
        x, z = self.along_x, self.along_z
        slots = jnp.zeros((2, z.size, x.size, gains.shape[1]), gains.dtype)
        slots = lax.dynamic_update_slice(slots, gains[:, None, None], (0, z.here(), x.here(), 0))
        return x.total(slots.reshape(2, z.size, -1))

    def gains_z(self, slots):
        x, z = self.along_x, self.along_z
        slots = z.total(slots).reshape(2, z.size, x.size, -1)
        turned = [
            lax.dynamic_slice_in_dim(slots, lax.rem(x.here() + j, x.size), 1, 2)[:, :, 0]
            for j in range(x.size)
        ]
        return jnp.concatenate(turned, axis=1).reshape(2, -1)

    def sum_vectors(self, vectors):
        mine = vectors[:, 0]
        for part in self.scatter_x([vectors[:, j] for j in range(1, self.along_x.size)]):
            mine = mine + part
        return mine.reshape(mine.shape[0], self.along_z.size, -1).transpose(1, 0, 2)


CHEAP = pl.CostEstimate(flops=0, bytes_accessed=0, transcendentals=0)


def resident(array):
    if isinstance(array, Part):
        return pl.BlockSpec(
            array.shape, lambda *_: (0, array.index, 0), pipeline_mode=pl.Buffered(1)
        )
    return pl.BlockSpec(
        array.shape, lambda *_: (0,) * array.ndim, pipeline_mode=pl.Buffered(1)
    )


class Part:
    def __init__(self, array, index, count):
        self.array, self.index = array, index
        planes, rows, columns = array.shape
        self.shape, self.ndim, self.dtype = (planes, rows // count, columns), 3, array.dtype


def call(kernel, table, grid, arrays, specs, outs, out_specs, flops=0):
    return pl.pallas_call(
        kernel,
        grid_spec=pltpu.PrefetchScalarGridSpec(
            num_scalar_prefetch=1, grid=grid, in_specs=specs, out_specs=out_specs
        ),
        out_shape=[jax.ShapeDtypeStruct(*out) for out in outs],
        compiler_params=pltpu.CompilerParams(vmem_limit_bytes=VMEM_LIMIT),
        cost_estimate=pl.CostEstimate(flops=flops, bytes_accessed=0, transcendentals=0),
    )(table, *[array.array if isinstance(array, Part) else array for array in arrays])


def turn_kernel(table, in_ref, out_ref):
    width = in_ref.shape[1] // table.shape[0]
    for i in range(table.shape[0]):
        start = pl.multiple_of(table[i] * width, width)
        out_ref[:, i * width : (i + 1) * width] = in_ref[:, pl.ds(start, width)]


def turn(value, table):
    rows, width = value.shape
    tile = min(rows, 256)
    return pl.pallas_call(
        turn_kernel,
        grid_spec=pltpu.PrefetchScalarGridSpec(
            num_scalar_prefetch=1,
            grid=(rows // tile,),
            in_specs=[pl.BlockSpec((tile, width), lambda i, t: (i, 0))],
            out_specs=pl.BlockSpec((tile, width), lambda i, t: (i, 0)),
        ),
        out_shape=jax.ShapeDtypeStruct(value.shape, value.dtype),
        cost_estimate=CHEAP,
    )(table, value)


def norm_turn_kernel(table, in_ref, gain_ref, out_ref):
    width = in_ref.shape[1] // table.shape[0]
    values = in_ref[...].astype(F32)
    mean = jnp.mean(values, axis=-1, keepdims=True)
    centred = values - mean
    scale = lax.rsqrt(jnp.mean(centred * centred, axis=-1, keepdims=True) + 1e-05)
    for i in range(table.shape[0]):
        start = pl.multiple_of(table[i] * width, width)
        block = in_ref[:, pl.ds(start, width)].astype(F32)
        gain = gain_ref[:, i * width : (i + 1) * width]
        out_ref[:, i * width : (i + 1) * width] = ((block - mean) * scale * gain).astype(BF16)


def norm_turn(value, gain, table):
    rows, width = value.shape
    tile = min(rows, 256)
    return pl.pallas_call(
        norm_turn_kernel,
        grid_spec=pltpu.PrefetchScalarGridSpec(
            num_scalar_prefetch=1,
            grid=(rows // tile,),
            in_specs=[
                pl.BlockSpec((tile, width), lambda i, t: (i, 0)),
                pl.BlockSpec((1, width), lambda i, t: (0, 0)),
            ],
            out_specs=pl.BlockSpec((tile, width), lambda i, t: (i, 0)),
        ),
        out_shape=jax.ShapeDtypeStruct(value.shape, BF16),
        cost_estimate=CHEAP,
    )(table, value, gain.reshape(1, -1))


def silu_parts(values):
    sigmoid = 1.0 / (1.0 + jnp.exp(-values))
    return sigmoid, values * sigmoid


def norm_parts(values):
    centred = values - jnp.mean(values, axis=-1, keepdims=True)
    scale = lax.rsqrt(jnp.mean(centred * centred, axis=-1, keepdims=True) + 1e-05)
    return centred * scale, scale


def halves(values):
    high = values.astype(BF16)
    return high, (values - high.astype(F32)).astype(BF16)


def row_decay(log, rows, first, step):
    position = lax.broadcasted_iota(jnp.int32, (rows, 1), 0)
    return jnp.exp((first + step * position).astype(F32) * log)


def pair_decay(log, rows):
    row = lax.broadcasted_iota(jnp.int32, (rows, rows), 0)
    column = lax.broadcasted_iota(jnp.int32, (rows, rows), 1)
    offset = row - column
    return jnp.where(offset >= 0, jnp.exp(jnp.maximum(offset, 0).astype(F32) * log), 0.0)


def state_kernel(logs, key_ref, value_ref, state_ref):
    rows = key_ref.shape[0]
    scaled = key_ref[...].astype(F32) * row_decay(logs[pl.program_id(1)], rows, rows - 1, -1)
    high, low = halves(scaled)
    value = value_ref[...]
    state_ref[0, 0] = t_matmul(high, value) + t_matmul(low, value)


def mix_kernel(logs, query_ref, key_ref, value_ref, state_ref, swish_ref, gated_ref, mixed_ref):
    rows = key_ref.shape[0]
    log = logs[pl.program_id(1)]
    query = query_ref[...]
    weights = (matmul_t(query, key_ref[...]) * pair_decay(log, rows)).astype(BF16)
    high, low = halves(state_ref[0, 0])
    cross = matmul(query, high) + matmul(query, low)
    mixed = matmul(weights, value_ref[...]) + cross * row_decay(log, rows, 1, 1)
    mixed_ref[...] = mixed
    gated_ref[...] = (silu_parts(swish_ref[...])[1] * norm_parts(mixed)[0]).astype(BF16)


def gate_kernel(logs, *refs):
    (branch_ref, *output_refs), (swish_ref, mixed_ref, query_ref) = refs[:-6], refs[-6:-3]
    swish_low_ref, mixed_low_ref, state_ref = refs[-3:]
    rows = query_ref.shape[0]
    swish_pre = swish_ref[...]
    grad = from_columns(branch_ref[...], output_refs)
    normalized, scale = norm_parts(mixed_ref[...])
    sigmoid, silu = silu_parts(swish_pre)
    slope = sigmoid * (1.0 + swish_pre * (1.0 - sigmoid))
    swish_low_ref[...] = (grad * normalized * slope).astype(BF16)
    e = grad * silu
    mean = jnp.mean(e, axis=-1, keepdims=True)
    along = jnp.mean(e * normalized, axis=-1, keepdims=True)
    mixed_low = (scale * (e - mean - normalized * along)).astype(BF16)
    mixed_low_ref[...] = mixed_low
    scaled = query_ref[...].astype(F32) * row_decay(logs[pl.program_id(1)], rows, 1, 1)
    high, low = halves(scaled)
    state_ref[0, 0] = t_matmul(high, mixed_low) + t_matmul(low, mixed_low)


def mix_back_kernel(
    logs,
    query_ref,
    key_ref,
    value_ref,
    mixed_low_ref,
    state_ref,
    state_grad_ref,
    query_low_ref,
    key_low_ref,
    value_low_ref,
):
    rows = key_ref.shape[0]
    log = logs[pl.program_id(1)]
    query, key, value, mixed_low = (
        query_ref[...],
        key_ref[...],
        value_ref[...],
        mixed_low_ref[...],
    )
    decay = pair_decay(log, rows)
    weights = (matmul_t(query, key) * decay).astype(BF16)
    score = (matmul_t(mixed_low, value) * decay).astype(BF16)
    high, low = halves(state_ref[0, 0])
    cross = matmul_t(mixed_low, high) + matmul_t(mixed_low, low)
    query_low_ref[...] = (matmul(score, key) + cross * row_decay(log, rows, 1, 1)).astype(BF16)
    high, low = halves(state_grad_ref[0, 0])
    to_end = row_decay(log, rows, rows - 1, -1)
    cross = matmul_t(value, high) + matmul_t(value, low)
    key_low_ref[...] = (t_matmul(score, query) + cross * to_end).astype(BF16)
    cross = matmul(key, high) + matmul(key, low)
    value_low_ref[...] = (t_matmul(weights, mixed_low) + cross * to_end).astype(BF16)


def at_once(kernel, arrays, outs, table=None, flops=0):
    if table is None:
        table = jnp.zeros((1,), jnp.int32)
    return call(
        kernel,
        table,
        (1,),
        arrays,
        [resident(array) for array in arrays],
        outs,
        [pl.BlockSpec(shape, lambda i, _, n=len(shape): (0,) * n) for shape, _ in outs],
        flops,
    )


def add_blocks(own, arrived, extra=None, flops=0):
    count, rows, columns = own.shape
    more = () if extra is None else (extra,)
    below = 0 if extra is None else 16
    half = count // 2
    arrays, specs = [own], [pl.BlockSpec((half, rows, columns), lambda i, _: (i, 0, 0))]
    for parts in arrived:
        start = 0
        for part in parts if isinstance(parts, list) else [parts]:
            size = part.shape[0]
            arrays.append(part)
            specs.append(
                pl.BlockSpec(
                    (half, rows, columns),
                    lambda i, _, size=size: (i if size == count else 0, 0, 0),
                )
            )
            start += size
    sizes = [array.shape[0] for array in arrays[1:]]

    def kernel(_, *refs):
        step = pl.program_id(0)
        out = refs[0][...].astype(F32)
        start = 0
        for ref, size in zip(refs[1 : len(arrays)], sizes):
            part = ref[...].astype(F32)
            if size < count:
                part = jnp.where(step * half == start, part, 0.0)
                start = (start + size) % count
            out = out + part
        refs[-1][:, :rows, :] = out.astype(BF16)
        if more:
            refs[-1][:, rows:, :] = refs[-2][...]

    if more:
        extra = jnp.pad(
            extra.astype(BF16),
            ((0, 0), (0, below - extra.shape[1]), (0, columns - extra.shape[2])),
        )
        more = (extra,)
    return call(
        kernel,
        jnp.zeros((1,), jnp.int32),
        (2,),
        [*arrays, *more],
        specs + [pl.BlockSpec((half, below, columns), lambda i, _: (i, 0, 0)) for _ in more],
        [((count, rows + below, columns), BF16)],
        [pl.BlockSpec((half, rows + below, columns), lambda i, _: (i, 0, 0))],
        flops,
    )[0]


def decayed_sum(own, before, decays):
    _, heads, rows, columns = own.shape

    def kernel(decays, own_ref, before_ref, out_ref):
        decay = decays[pl.program_id(0)]
        out_ref[...] = (own_ref[...] + decay * before_ref[...].astype(F32)).astype(BF16)

    block = pl.BlockSpec((1, 1, rows, columns), lambda h, _: (0, h, 0, 0))
    return call(
        kernel, decays, (heads,), [own, before], [block, block], [(own.shape, BF16)], [block],
        flops=3_000_000_000,
    )[0]


def order_blocks(first, blocks):
    count = len(blocks)
    shape = blocks[0].shape

    def kernel(first, *refs):
        for k in range(count):

            @pl.when(pl.program_id(0) == lax.rem(first[0] + k, count))
            def _(k=k):
                refs[-1][0] = refs[k][...]

    return call(
        kernel,
        first.astype(jnp.int32).reshape(1),
        (count,),
        blocks,
        [resident(block) for block in blocks],
        [((count, *shape), blocks[0].dtype)],
        [pl.BlockSpec((1, *shape), lambda i, _: (i, 0, 0))],
    )[0]


def fold_tiles(own, arrived, tiles, flops=0):
    rows, width = own.shape
    tile = rows // tiles
    piece = tile // 2

    def kernel(_, own_ref, *refs):
        outs = refs[len(arrived) :]
        for i in range(2 * tiles):
            value = own_ref[i * piece : (i + 1) * piece, :]
            for ref in refs[i : len(arrived) : 2 * tiles]:
                value = value + ref[...].astype(F32)
            if i < 2:
                outs[0][i * piece : (i + 1) * piece, :] = value
            else:
                outs[i - 1][...] = value.astype(BF16)

    mine, *pieces = at_once(
        kernel,
        [own, *arrived],
        [((tile, width), F32)] + [((piece, width), BF16)] * (2 * tiles - 2),
        flops=flops,
    )
    return mine, [pieces[2 * k : 2 * k + 2] for k in range(tiles - 1)]


def summed(mine_ref, refs, piece):
    rows = mine_ref.shape[0] // 2
    value = mine_ref[piece * rows : (piece + 1) * rows, :]
    for ref in refs[piece::2]:
        value = value + ref[...].astype(F32)
    return value


def enter_dense(mine, arrived, tokens, gain):
    rows, width = mine.shape
    half = rows // 2

    def kernel(_, mine_ref, tokens_ref, gain_ref, *refs):
        hidden_ref, *outs = refs[len(arrived) :]
        for i in range(2):
            part = slice(i * half, (i + 1) * half)
            hidden = tokens_ref[part, :].astype(F32) + summed(mine_ref, refs[: len(arrived)], i)
            hidden_ref[part, :] = hidden
            outs[i][...] = (norm_parts(hidden)[0] * gain_ref[...]).astype(BF16)

    hidden, *pieces = at_once(
        kernel,
        [mine, tokens, gain.reshape(1, -1), *arrived],
        [((rows, width), F32)] + [((half, width), BF16)] * 2,
    )
    return hidden, pieces


def leave_dense(mine, arrived, hidden):
    rows, width = mine.shape
    half = rows // 2

    def kernel(_, mine_ref, hidden_ref, *refs):
        for i in range(2):
            value = hidden_ref[i * half : (i + 1) * half, :] + summed(
                mine_ref, refs[: len(arrived)], i
            )
            refs[len(arrived) + i][...] = value.astype(BF16)

    return at_once(kernel, [mine, hidden, *arrived], [((half, width), BF16)] * 2)


def norm_backward(mine, arrived, values, gain, residual, keep):
    rows, width = mine.shape
    half = rows // 2

    def kernel(_, mine_ref, values_ref, gain_ref, residual_ref, *refs):
        gain_out, first, second, *whole = refs[len(arrived) :]
        gain_sum = 0.0
        for i in range(2):
            part = slice(i * half, (i + 1) * half)
            grad = summed(mine_ref, refs[: len(arrived)], i)
            normalized, scale = norm_parts(values_ref[part, :].astype(F32))
            gain_sum = gain_sum + jnp.sum(grad * normalized, axis=0, keepdims=True)
            e = grad * gain_ref[...]
            mean = jnp.mean(e, axis=-1, keepdims=True)
            along = jnp.mean(e * normalized, axis=-1, keepdims=True)
            out = residual_ref[part, :].astype(F32) + scale * (e - mean - normalized * along)
            (first, second)[i][...] = out.astype(BF16)
            for ref in whole:
                ref[part, :] = out
        gain_out[...] = gain_sum

    gain_part, first, second, *whole = at_once(
        kernel,
        [mine, values, gain.reshape(1, -1), residual, *arrived],
        [((1, width), F32)]
        + [((half, width), BF16)] * 2
        + [((rows, width), F32)] * (1 if keep else 0),
    )
    return gain_part, [first, second], *whole


def place_tiles(table, near, far, kind):
    tiles = len(near)
    pieces = [piece for tile in near + far for piece in tile]
    piece, width = pieces[0].shape
    columns = table.shape[0] - 2
    block = width // columns

    def kernel(table, *refs):
        out_ref = refs[-1]
        step = pl.program_id(0)
        for i in range(2 * tiles):
            core = lax.rem(table[0] + i // tiles, CORES)
            row = lax.rem(table[1] + i % tiles, tiles)

            @pl.when(step == core * tiles + row)
            def _(i=i):
                for part in range(2):
                    ref = refs[2 * i + part]
                    for j in range(columns):
                        start = pl.multiple_of(table[2 + j] * block, block)
                        out_ref[
                            part * piece : (part + 1) * piece, j * block : (j + 1) * block
                        ] = ref[:, pl.ds(start, block)].astype(kind)

    return call(
        kernel,
        table,
        (CORES * tiles,),
        pieces,
        [resident(ref) for ref in pieces],
        [((2 * CORES * tiles * piece, width), kind)],
        [pl.BlockSpec((2 * piece, width), lambda i, _: (i, 0))],
    )[0]


def by_rows(ref):
    return ref[...].reshape(-1, ref.shape[2])


def from_columns(values, refs):
    out, start = 0.0, 0
    for ref in refs:
        weight = jnp.concatenate([ref[k] for k in range(ref.shape[0])], axis=1)
        stop = start + weight.shape[1]
        out = out + matmul_t(values[:, start:stop], weight)
        start = stop
    return out


def project(values, weight, kind):
    rows, width = values.shape
    tile = min(rows, 256)
    columns = weight[0].shape[2]

    def kernel(_, in_ref, *refs):
        depth = width // len(weight)
        out = matmul(in_ref[:, :depth], by_rows(refs[0]))
        for j in range(1, len(weight)):
            out = out + matmul(in_ref[:, j * depth : (j + 1) * depth], by_rows(refs[j]))
        refs[-1][...] = out.astype(kind)

    return call(
        kernel,
        jnp.zeros((1,), jnp.int32),
        (rows // tile,),
        [values, *weight],
        [pl.BlockSpec((tile, width), lambda i, _: (i, 0))] + [resident(w) for w in weight],
        [((rows, columns), kind)],
        [pl.BlockSpec((tile, columns), lambda i, _: (i, 0))],
    )[0]


def parts_by_rows(compute, table, model_width, arrays, specs, outs, out_specs):
    count = table.shape[0]
    rows = arrays[0].shape[0]
    tile = rows // count
    away = count - count // CORES
    half = tile // 2

    def kernel(table, *refs):
        step = pl.program_id(0)
        pieces, own_ref = refs[-2 * away - 1 : -1], refs[-1]
        value = compute(*refs[: -2 * away - 1])
        for i in range(away):

            @pl.when(step == i)
            def _(i=i):
                pieces[2 * i][...] = value[:half].astype(BF16)
                pieces[2 * i + 1][...] = value[half:].astype(BF16)

        @pl.when(step >= away)
        def _():
            own_ref[...] = value

    *results, own = call(
        kernel,
        table,
        (count,),
        arrays,
        specs,
        outs + [((half, model_width), BF16)] * (2 * away) + [(((count - away) * tile, model_width), F32)],
        out_specs
        + [pl.BlockSpec((half, model_width), lambda i, t: (0, 0))] * (2 * away)
        + [pl.BlockSpec((tile, model_width), lambda i, t: (jnp.maximum(i - away, 0), 0))],
    )
    return *results[: len(outs)], results[len(outs) :], own


def tile_of(array, table):
    return pl.BlockSpec(
        (array.shape[0] // table.shape[0], array.shape[1]), lambda i, t: (t[i], 0)
    )


def to_columns(values, weight, table):
    def compute(in_ref, *refs):
        value = in_ref[...]
        return jnp.concatenate(
            [matmul(value, ref[k]) for ref in refs for k in range(ref.shape[0])], axis=1
        )

    return parts_by_rows(
        compute,
        table,
        sum(w.shape[0] * w.shape[2] for w in weight),
        [values, *weight],
        [tile_of(values, table)] + [resident(w) for w in weight],
        [],
        [],
    )


def dense_forward(dense_in, gate, up):
    rows, width = dense_in.shape
    tile = min(rows, 256)
    units = gate[0].shape[2]

    def kernel(_, in_ref, *refs):
        gate_refs, up_refs = refs[: len(gate)], refs[len(gate) : -3]
        depth = width // len(gate)
        pre = []
        for weights in (gate_refs, up_refs):
            out = 0.0
            for j, ref in enumerate(weights):
                out = out + matmul(in_ref[:, j * depth : (j + 1) * depth], by_rows(ref))
            pre.append(out)
        refs[-3][...], refs[-2][...] = pre
        refs[-1][...] = (gelu_parts(pre[0])[0] * pre[1]).astype(BF16)

    block = pl.BlockSpec((tile, units), lambda i, _: (i, 0))
    return call(
        kernel,
        jnp.zeros((1,), jnp.int32),
        (rows // tile,),
        [dense_in, *gate, *up],
        [pl.BlockSpec((tile, width), lambda i, _: (i, 0))] + [resident(w) for w in (*gate, *up)],
        [((rows, units), F32), ((rows, units), F32), ((rows, units), BF16)],
        [block] * 3,
    )


def dense_backward(grad_out, gate_pre, up_pre, down, gate, up, table):
    units = gate_pre.shape[1]

    def compute(grad_ref, gate_pre_ref, up_pre_ref, *refs):
        count = len(down)
        down_refs, gate_refs, up_refs = (refs[i * count : (i + 1) * count] for i in range(3))
        gate_low_ref, up_low_ref = refs[3 * count :]
        grad = from_columns(grad_ref[...], down_refs).astype(BF16).astype(F32)
        act, slope = gelu_parts(gate_pre_ref[...])
        gate_low = (grad * up_pre_ref[...] * slope).astype(BF16)
        up_low = (grad * act).astype(BF16)
        gate_low_ref[...] = gate_low
        up_low_ref[...] = up_low
        return jnp.concatenate(
            [
                matmul_t(gate_low, by_rows(g)) + matmul_t(up_low, by_rows(u))
                for g, u in zip(gate_refs, up_refs)
            ],
            axis=1,
        )

    weights = [*down, *gate, *up]
    tiles = [grad_out, gate_pre, up_pre]
    return parts_by_rows(
        compute,
        table,
        grad_out.shape[1],
        tiles + weights,
        [tile_of(a, table) for a in tiles]
        + [resident(w) for w in weights],
        [((gate_pre.shape[0], units), BF16)] * 2,
        [tile_of(gate_pre, table)] * 2,
    )


def to_rows(values, weights, table):
    counts = [len(group) for group in values]
    blocks = len(weights[0])

    def compute(*refs):
        refs = list(refs)
        inputs = []
        for count in counts:
            group = [refs.pop(0)[...] for _ in range(count)]
            inputs.append(group[0] if count == 1 else jnp.concatenate(group, axis=1))
        outs = [0.0] * blocks
        for value in inputs:
            for j in range(blocks):
                outs[j] = outs[j] + matmul_t(value, by_rows(refs.pop(0)))
        return jnp.concatenate(outs, axis=1)

    flat = [value for group in values for value in group]
    every = [w for weight in weights for w in weight]
    model_width = sum(w.shape[0] * w.shape[1] for w in weights[0])
    return parts_by_rows(
        compute,
        table,
        model_width,
        flat + every,
        [tile_of(value, table) for value in flat] + [resident(w) for w in every],
        [],
        [],
    )


def grad_by_rows(left, rights, plan, own=True, others=True, pieces=1):
    rows, width = left.shape
    x, z = plan.along_x.size, plan.along_z.size
    block = width // (x * z)
    columns = sum(right.shape[1] for right in rights)
    half = z // 2
    away = 2 * (x - 1) if others else 0
    steps = away + (2 if own else 0)
    first = 0 if own and not others else 2

    def kernel(_, left_ref, *refs):
        step = pl.program_id(0)
        value = []
        for right_ref in refs[: len(rights)]:
            value.append(t_matmul(left_ref[...], right_ref[...]))
        value = value[0] if len(value) == 1 else jnp.concatenate(value, axis=1)
        value = value.astype(BF16).reshape(half, block, columns)
        outs = refs[len(rights) :]
        for i in range(away):

            @pl.when(step == i)
            def _(i=i):
                outs[i * pieces // 2][...] = value

        if own:

            @pl.when(step >= away)
            def _():
                outs[-1][...] = value

    piece = (half, block, columns)
    results = call(
        kernel,
        jnp.zeros((1,), jnp.int32),
        (steps,),
        [left, *rights],
        [pl.BlockSpec((rows, half * block), lambda i, _: (0, lax.rem(i + first, 2 * x)))]
        + [resident(right) for right in rights],
        [((z // pieces, block, columns), BF16)] * (away * pieces // 2)
        + [((z, block, columns), BF16)] * own,
        [
            pl.BlockSpec(piece, lambda i, _, j=j: (jnp.clip(i - 2 * j, 0, 1) if pieces == 1 else 0, 0, 0))
            for j in range(away * pieces // 2)
        ]
        + [pl.BlockSpec(piece, lambda i, _: (jnp.maximum(i - away, 0), 0, 0))] * own,
    )
    if not others:
        return results[0]
    parts = list(results[: away * pieces // 2])
    if pieces == 2:
        parts = [parts[2 * j : 2 * j + 2] for j in range(x - 1)]
    return (results[-1], parts) if own else parts


def grad_by_columns(left, right, plan, pieces=1):
    rows, units = left.shape
    x, z = plan.along_x.size, plan.along_z.size
    block = right.shape[1] // (x * z)
    tile = min(units, 512)
    half = z // pieces

    def kernel(_, left_ref, right_ref, own_ref, *other_refs):
        value = t_matmul(left_ref[...], right_ref[...])
        for i in range(x * z):
            part = value[:, i * block : (i + 1) * block].astype(BF16)
            if i < z:
                own_ref[i] = part
            else:
                other_refs[(i - z) // half][(i - z) % half] = part

    own, *others = call(
        kernel,
        jnp.zeros((1,), jnp.int32),
        (units // tile,),
        [left, right],
        [pl.BlockSpec((rows, tile), lambda i, _: (0, i)), resident(right)],
        [((z, units, block), BF16)] + [((half, units, block), BF16)] * (pieces * (x - 1)),
        [pl.BlockSpec((z, tile, block), lambda i, _: (0, i, 0))]
        + [pl.BlockSpec((half, tile, block), lambda i, _: (0, i, 0))] * (pieces * (x - 1)),
    )
    if pieces == 2:
        others = [others[2 * j : 2 * j + 2] for j in range(x - 1)]
    return own, others


def gelu_parts(values):
    root = 0.7978845608028654
    inner = jnp.tanh(root * (values + 0.044715 * (values * values * values)))
    half = 0.5 * (1.0 + inner)
    slope = half + 0.5 * values * (1.0 - inner * inner) * root * (
        1.0 + 3 * 0.044715 * (values * values)
    )
    return values * half, slope


class Heads:
    def __init__(self, logs, seqs, rows):
        self.logs, self.seqs, self.rows = logs, seqs, rows
        self.heads = logs.shape[0]

    def flat(self, array, width, first):
        return array, pl.BlockSpec((self.rows, width), lambda b, h, _: (b, first + h))

    def whole(self, array):
        return array, pl.BlockSpec((self.rows, array.shape[1]), lambda b, h, _: (b, 0))

    def rows_of(self, weight):
        count, _, width = weight.shape
        return weight, pl.BlockSpec((count, VD, width), lambda b, h, _: (0, h, 0))

    def state(self, array):
        return array, pl.BlockSpec((1, 1, QK, VD), lambda b, h, _: (b, h, 0, 0))

    def call(self, kernel, inputs, outs):
        shapes, specs = [], []
        for width, kind in outs:
            if width is None:
                shapes.append(((self.seqs, self.heads, QK, VD), kind))
                specs.append(self.state(None)[1])
            else:
                shapes.append(((self.seqs * self.rows, self.heads * width), kind))
                specs.append(self.flat(None, width, 0)[1])
        return call(
            kernel,
            self.logs,
            (self.seqs, self.heads),
            [array for array, _ in inputs],
            [spec for _, spec in inputs],
            shapes,
            specs,
        )


def matmul(left, right):
    return jnp.dot(left, right, preferred_element_type=F32)


def matmul_t(left, right):
    return lax.dot_general(left, right, (((1,), (1,)), ((), ())), preferred_element_type=F32)


def t_matmul(left, right):
    return lax.dot_general(left, right, (((0,), (0,)), ((), ())), preferred_element_type=F32)


class Live:
    def fence(self):
        names = list(vars(self))
        values = lax.optimization_barrier([getattr(self, name) for name in names])
        for name, value in zip(names, values):
            setattr(self, name, value)


def added(blocks):
    count, rows, columns = blocks.shape
    parts = 2 if rows % 32 == 0 else 1

    def kernel(_, in_ref, out_ref):
        out = in_ref[0].astype(F32)
        for k in range(1, count):
            out = out + in_ref[k].astype(F32)
        out_ref[...] = out

    return call(
        kernel,
        jnp.zeros((1,), jnp.int32),
        (parts,),
        [blocks],
        [pl.BlockSpec((count, rows // parts, columns), lambda i, _: (0, i, 0))],
        [((rows, columns), F32)],
        [pl.BlockSpec((rows // parts, columns), lambda i, _: (i, 0))],
    )[0]


def added_last(blocks, rows, width):
    count = blocks.shape[0]

    def kernel(_, in_ref, first_ref, second_ref, vectors_ref):
        out = in_ref[0].astype(F32)
        for k in range(1, count):
            out = out + in_ref[k].astype(F32)
        first_ref[...] = out[:rows, :width]
        second_ref[...] = out[:rows, width:]
        vectors_ref[...] = out[rows : rows + 8, :rows]

    return at_once(
        kernel, [blocks], [((rows, width), F32), ((rows, width), F32), ((8, rows), F32)]
    )


def on_device(
    plan,
    tokens,
    pre_gain,
    query_weight,
    key_weight,
    value_weight,
    swish_weight,
    output_weight,
    mid_gain,
    gate_weight,
    up_weight,
    down_weight,
    cotangent,
):
    seq_count, seg_rows, model_width = tokens.shape
    row_count = seq_count * seg_rows
    to_slots, to_owners, table = plan.slot_owner(), plan.owner_slot(), plan.row_tiles()
    e = Live()
    e.tokens = tokens.reshape(row_count, model_width)
    e.cotangent = cotangent.reshape(row_count, model_width)
    key_width = query_weight.shape[1]
    local_heads = key_width // QK
    copies, blocks_x = plan.copies, plan.along_x.size
    along_z, along_core, along_y = plan.along_z, plan.along_core, plan.along_y
    def parts_of(array):
        return [Part(array, j, blocks_x) for j in range(blocks_x)]

    head_index = (lax.axis_index("shard") * local_heads + jnp.arange(local_heads)).astype(F32)
    logs = jnp.log1p(-jnp.exp2(-5.0 - head_index))
    carry_scale = jnp.exp(seg_rows * logs)
    each = Heads(logs, seq_count, seg_rows)

    e.value = plan.gather_z(value_weight)
    e.gains = plan.gains_x(jnp.stack([pre_gain, mid_gain]).astype(BF16))
    e.query_key = copies(jnp.concatenate([query_weight, key_weight], axis=1))
    e.down = plan.gather_x(down_weight)
    e.grad_out = turn(e.cotangent, to_slots)
    del e.cotangent
    e.own_tokens = turn(plan.own_rows(e.tokens), to_slots)
    e.fence()
    e.value = plan.gather_x(order_blocks(along_z.here(), e.value))
    e.query_key = along_z.exchange(e.query_key)
    e.own_grad_out = plan.own_rows(e.grad_out)
    gains = plan.gains_z(e.gains).astype(F32)
    e.full_pre, e.full_mid = gains[0], gains[1]
    del e.gains
    e.swish = swish_weight
    e.fence()
    e.query_key = plan.gather_x(e.query_key)
    e.swish = plan.gather_z(e.swish)
    e.output = copies(output_weight)
    e.mixer_in = norm_turn(e.tokens, e.full_pre, to_slots)
    del e.tokens
    e.values = project(e.mixer_in, e.value, BF16)
    e.fence()
    output_z = along_z.exchange(e.output)
    del e.output
    e.swish = order_blocks(along_z.here(), e.swish)
    e.queries_keys = project(e.mixer_in, e.query_key, BF16)
    (state,) = each.call(
        state_kernel,
        [each.flat(e.queries_keys, QK, local_heads), each.flat(e.values, VD, 0)],
        [(None, F32)],
    )
    e.state = plan.scan_begin(state)
    e.fence()
    swish_x = plan.gather_x(e.swish)
    del e.swish
    e.output = output_z
    e.gate = copies(gate_weight)
    e.state = plan.scan_sums(e.state, carry_scale, False)
    e.fence()
    e.output_first = plan.gather_x(e.output[:1])[1:]
    e.state = plan.scan_middle(e.state, carry_scale, False)
    e.swish = swish_x
    e.fence()
    gate_z = along_z.exchange(e.gate)
    del e.gate
    e.state = plan.scan_end(e.state)
    e.fence()
    output_x = [e.output]
    for parts in zip(e.output_first, plan.gather_x(e.output[1:])[1:]):
        output_x += parts
    del e.output, e.output_first
    e.gate = gate_z
    e.swish_pre = project(e.mixer_in, e.swish, F32)
    e.gated, e.mixed = each.call(
        mix_kernel,
        [
            each.flat(e.queries_keys, QK, 0),
            each.flat(e.queries_keys, QK, local_heads),
            each.flat(e.values, VD, 0),
            each.state(e.state),
            each.flat(e.swish_pre, VD, 0),
        ],
        [(VD, BF16), (VD, F32)],
    )
    e.up = copies(up_weight)
    e.fence()
    e.up = along_z.exchange(e.up)
    e.gate = plan.gather_x(e.gate)
    branch_others, branch_own = to_columns(e.gated, output_x, table)
    e.output = output_x
    mine, pieces = fold_tiles(
        branch_own, plan.sum_cores(branch_others), along_y.size, flops=9_000_000_000
    )
    e.mine, e.arrived = mine, plan.sum_y(pieces)
    e.down = copies(jnp.concatenate(e.down, axis=0))
    e.fence()
    down_z = along_z.exchange(e.down)
    del e.down
    up_x = plan.gather_x(e.up)
    del e.up
    e.hidden_state, dense_own = enter_dense(e.mine, e.arrived, e.own_tokens, e.full_mid)
    del e.mine, e.arrived
    e.dense_tiles = plan.share_y(dense_own)
    e.fence()
    e.dense_in = plan.share_cores(e.dense_tiles, BF16)
    del e.dense_tiles
    e.up = up_x
    e.fence()
    e.gate_pre, e.up_pre, e.inner_act = dense_forward(e.dense_in, e.gate, e.up)
    e.down_own, e.down_others = grad_by_columns(e.inner_act, e.grad_out, plan)
    e.fence()
    down_x = plan.scatter_x(e.down_others)
    del e.down_others
    e.down = down_z
    e.fence()
    e.gate_low, e.up_low, e.part_others, e.part_own = dense_backward(
        e.grad_out, e.gate_pre, e.up_pre, parts_of(e.down), e.gate, e.up, table
    )
    del e.gate_pre, e.up_pre, e.gate, e.up, e.grad_out
    e.fence()
    e.gate_others = grad_by_rows(e.dense_in, [e.gate_low], plan, own=False)
    e.fence()
    gate_x = plan.scatter_x(e.gate_others)
    del e.gate_others
    e.down_sum = add_blocks(e.down_own, down_x)
    del e.down_own
    e.fence()
    down_z = along_z.exchange(e.down_sum)
    del e.down_sum
    e.part_others = plan.sum_cores(e.part_others)
    e.gate_own = grad_by_rows(e.dense_in, [e.gate_low], plan, others=False)
    del e.gate_low
    e.fence()
    mine, pieces = fold_tiles(e.part_own, e.part_others, along_y.size)
    e.mine, e.arrived = mine, plan.sum_y(pieces)
    del e.part_own, e.part_others
    e.up_own, e.up_others = grad_by_rows(e.dense_in, [e.up_low], plan)
    del e.dense_in, e.up_low
    e.fence()
    e.mid_part, branch_own, e.hidden_grad = norm_backward(
        e.mine, e.arrived, e.hidden_state, e.full_mid, e.own_grad_out, True
    )
    del e.mine, e.arrived, e.own_grad_out
    e.branch_own = branch_own
    e.gate_sum = add_blocks(e.gate_own, gate_x, flops=12_000_000_000)
    del e.gate_own
    e.down_sum = down_z
    e.fence()
    gate_z = along_z.exchange(e.gate_sum)
    del e.gate_sum
    up_x = plan.scatter_x(e.up_others)
    del e.up_others
    e.branch_tiles = plan.share_y(e.branch_own)
    del e.branch_own
    e.out_others, e.out_own = to_columns(e.inner_act, parts_of(e.down), table)
    del e.inner_act, e.down
    e.fence()
    e.branch_low = plan.share_cores(e.branch_tiles, BF16)
    del e.branch_tiles
    e.output_own, e.output_others = grad_by_columns(e.gated, e.branch_low, plan, pieces=2)
    del e.gated
    e.up_sum = add_blocks(e.up_own, up_x, flops=12_000_000_000)
    del e.up_own
    e.gate_sum = gate_z
    e.fence()
    up_z = along_z.exchange(e.up_sum)
    del e.up_sum
    e.output_first = plan.scatter_x([part[0] for part in e.output_others])
    e.output_others = [part[1] for part in e.output_others]
    e.swish_low, e.mixed_low, e.state_grad = each.call(
        gate_kernel,
        [
            each.whole(e.branch_low),
            *[each.rows_of(weight) for weight in e.output],
            each.flat(e.swish_pre, VD, 0),
            each.flat(e.mixed, VD, 0),
            each.flat(e.queries_keys, QK, 0),
        ],
        [(VD, BF16), (VD, BF16), (None, F32)],
    )
    del e.swish_pre, e.mixed, e.output, e.branch_low
    e.fence()
    e.swish_own, e.swish_others = grad_by_rows(e.mixer_in, [e.swish_low], plan, pieces=2)
    e.state_grad = plan.scan_begin(e.state_grad)
    e.out_others = plan.sum_cores(e.out_others)
    e.fence()
    output_x = plan.scatter_x(e.output_others)
    del e.output_others
    e.mine, e.pieces = fold_tiles(e.out_own, e.out_others, along_y.size)
    del e.out_own, e.out_others
    e.state_grad = plan.scan_sums(e.state_grad, carry_scale, True)
    e.up_sum = up_z
    e.fence()
    e.swish_first = plan.scatter_x([part[0] for part in e.swish_others])
    e.swish_others = [part[1] for part in e.swish_others]
    e.state_grad = plan.scan_middle(e.state_grad, carry_scale, True)
    output_x = [list(parts) for parts in zip(e.output_first, output_x)]
    e.output_sum = add_blocks(e.output_own, output_x, flops=14_000_000_000)
    del e.output_own, e.output_first
    e.fence()
    output_z = along_z.exchange(e.output_sum)
    del e.output_sum
    e.state_grad = plan.scan_end(e.state_grad)
    e.fence()
    swish_x = plan.scatter_x(e.swish_others)
    del e.swish_others
    e.query_low, e.key_low, e.value_low = each.call(
        mix_back_kernel,
        [
            each.flat(e.queries_keys, QK, 0),
            each.flat(e.queries_keys, QK, local_heads),
            each.flat(e.values, VD, 0),
            each.flat(e.mixed_low, VD, 0),
            each.state(e.state),
            each.state(e.state_grad),
        ],
        [(QK, BF16), (QK, BF16), (VD, BF16)],
    )
    del e.state, e.state_grad, e.mixed_low, e.queries_keys, e.values
    e.value_own, e.value_others = grad_by_rows(e.mixer_in, [e.value_low], plan)
    e.arrived = plan.sum_y(e.pieces)
    del e.pieces
    e.fence()
    swish_x = [list(parts) for parts in zip(e.swish_first, swish_x)]
    e.swish_sum = add_blocks(e.swish_own, swish_x)
    del e.swish_own, e.swish_first
    e.output_sum = output_z
    e.fence()
    swish_z = along_z.exchange(e.swish_sum)
    del e.swish_sum
    value_x = plan.scatter_x(e.value_others)
    del e.value_others
    e.part_others, e.part_own = to_rows(
        [[e.query_low, e.key_low], [e.value_low], [e.swish_low]],
        [e.query_key, e.value, e.swish],
        table,
    )
    del e.value_low, e.swish_low, e.query_key, e.value, e.swish
    e.layer_tiles = plan.share_y(leave_dense(e.mine, e.arrived, e.hidden_state))
    del e.mine, e.arrived, e.hidden_state
    e.fence()
    e.query_key_own, e.query_key_others = grad_by_rows(
        e.mixer_in, [e.query_low, e.key_low], plan
    )
    del e.query_low, e.key_low, e.mixer_in
    query_key_x = plan.scatter_x(e.query_key_others)
    del e.query_key_others
    e.part_others = plan.sum_cores(e.part_others)
    e.value_sum = add_blocks(e.value_own, value_x, flops=12_000_000_000)
    del e.value_own
    e.fence()
    e.swish_sum = swish_z
    e.fence()
    value_z = along_z.exchange(e.value_sum)
    del e.value_sum
    e.mine, pieces = fold_tiles(e.part_own, e.part_others, along_y.size)
    e.arrived = plan.sum_y(pieces)
    del e.part_own, e.part_others
    e.down_sum = added(e.down_sum)
    e.gate_sum = added(e.gate_sum)
    e.up_sum = added(e.up_sum)
    e.fence()
    e.pre_part, e.tokens_own = norm_backward(
        e.mine, e.arrived, e.own_tokens, e.full_pre, e.hidden_grad, False
    )
    del e.mine, e.arrived, e.own_tokens, e.hidden_grad
    vectors = jnp.stack([e.mid_part, e.pre_part]).reshape(2, blocks_x, -1)
    vectors = plan.sum_vectors(along_y.total(along_core.total(vectors)))
    del e.mid_part, e.pre_part
    e.query_key_sum = add_blocks(
        e.query_key_own, query_key_x, vectors, flops=12_000_000_000
    )
    del e.query_key_own
    e.value_sum = value_z
    e.fence()
    e.layer_out = plan.share_cores(e.layer_tiles, BF16, to_owners)
    e.tokens_grad = plan.share_cores(plan.share_y(e.tokens_own), F32, to_owners)
    last = along_z.exchange(e.query_key_sum)
    query_grad, key_grad, vectors = added_last(last, pre_gain.shape[0], key_width)
    return (
        e.layer_out.reshape(tokens.shape),
        e.tokens_grad.reshape(tokens.shape),
        vectors[1],
        query_grad,
        key_grad,
        added(e.value_sum),
        added(e.swish_sum),
        added(e.output_sum),
        vectors[0],
        e.gate_sum,
        e.up_sum,
        e.down_sum,
    )


def solution(mesh):
    rows, weight, turned, vector = (
        P(None, "seq", None),
        P("seq", "shard"),
        P("shard", "seq"),
        P("seq"),
    )
    return jax.shard_map(
        functools.partial(on_device, Plan(mesh)),
        mesh=mesh,
        in_specs=(
            rows,
            vector,
            weight,
            weight,
            weight,
            weight,
            turned,
            vector,
            weight,
            weight,
            turned,
            rows,
        ),
        out_specs=(
            rows,
            rows,
            vector,
            weight,
            weight,
            weight,
            weight,
            turned,
            vector,
            weight,
            weight,
            turned,
        ),
        check_vma=False,
    )
```
